32 devices in a mesh: dp: 8 (over y, x, core), tensor: 4 (over z).
Axes of the slice: x: 2, y: 2, z: 4, core: 2. Of those that a mesh axis runs over, the one named last changes fastest.
Arguments:
- tokens: bfloat16 [16384, 2048], P(('dp', 'tensor')), may hold values from -8 to 8
- segments: int32 [8, 2048], P('dp'), may hold values from 0 to 7, never falling along the last dimension, each value on 1 to 800 neighbouring positions
- norm_gain: float32 [2048], replicated, may hold values from 0.5 to 1.5
- norm_shift: float32 [2048], replicated, may hold values from -4 to 4
- qkv_weight: bfloat16 [3, 2048, 2048], P(None, 'dp', 'tensor'), may hold values from -1 to 1
- qkv_bias: bfloat16 [3, 2048], P(None, ('tensor', 'dp')), may hold values from -6 to 6
- dense_weight: bfloat16 [2048, 2048], P('tensor', 'dp'), may hold values from -0.5 to 0.5
- up_weight: bfloat16 [2048, 8192], P('dp', 'tensor'), may hold values from -1 to 1
- up_bias: bfloat16 [8192], P(('tensor', 'dp')), may hold values from -6 to 6
- down_weight: bfloat16 [8192, 2048], P('tensor', 'dp'), may hold values from -0.0625 to 0.0625
- out_bias: float32 [2048], replicated, may hold values from -6 to 6
- cotangent: bfloat16 [16384, 2048], P(('dp', 'tensor')), may hold values from -6 to 6
Outputs:
- output: bfloat16 [16384, 2048], P(('dp', 'tensor'))
- grad_tokens: bfloat16 [16384, 2048], P(('dp', 'tensor'))
- grad_norm_gain: float32 [2048], P(('dp', 'tensor'))
- grad_norm_shift: float32 [2048], P(('dp', 'tensor'))
- grad_qkv_weight: float32 [3, 2048, 2048], P(None, 'dp', 'tensor')
- grad_qkv_bias: float32 [3, 2048], P(None, ('tensor', 'dp'))
- grad_dense_weight: float32 [2048, 2048], P('tensor', 'dp')
- grad_up_weight: float32 [2048, 8192], P('dp', 'tensor')
- grad_up_bias: float32 [8192], P(('tensor', 'dp'))
- grad_down_weight: float32 [8192, 2048], P('tensor', 'dp')
- grad_out_bias: float32 [2048], P(('dp', 'tensor'))
- root_squares: float32 [3], replicated
The draws below stay inside these ranges and needn't reach their ends.
Inputs may be any that keep to these rules, and one draw needn't show every extreme that they name: `segments`: within a sequence the numbers never fall; every number from 0 to 7 appears, each on 1 to 800 tokens, and one on exactly 800.
All inputs are finite; a program needn't handle non-finite values.
Results may differ from the reference program's by a relative error of at most 0.012.
The reference program's roundings to bfloat16 on the way count: a program that leaves them out, or rounds other values in their place, can miss the bound.
Values may be sent and summed in bfloat16 or wider, within the bound.
A program may use at most 640 MiB of HBM per device.

```python
import math
import jax
import jax.numpy as jnp
import numpy as np
from jax import lax

D = 2048
HEADS = 32
HEAD_DIM = 64
ROT = 32
FF = 8192
SEQ_LEN = 2048
DOCS = 8
DOC_MOST = 800
SEQS = 8
TOKENS = 16384


def draw_tokens(key, part):
    row_index = jnp.arange(TOKENS, dtype=jnp.float32)[:, None]
    rising = 0.6 * jnp.exp(jnp.log(3.0) * row_index / TOKENS)
    entries = jax.random.truncated_normal(key, -4.0, 4.0, (TOKENS, D), jnp.float32)
    return (entries * rising).astype(jnp.bfloat16)


def column_offset(key, shape):
    offset_shape = shape[:-2] + (1, shape[-1])
    return jax.random.truncated_normal(jax.random.fold_in(key, 7), -3.0, 3.0, offset_shape, jnp.float32)


def draw_qkv_weight(key, part):
    shape = (3, D, D)
    weight_scale = 1.0 / math.sqrt(D // 2)
    entries = jax.random.truncated_normal(key, -4.0, 4.0, shape, jnp.float32)
    return ((entries + 0.5 * column_offset(key, shape)) * weight_scale).astype(jnp.bfloat16)


def draw_up_weight(key, part):
    shape = (D, FF)
    weight_scale = 1.0 / math.sqrt(D)
    entries = jax.random.truncated_normal(key, -4.0, 4.0, shape, jnp.float32)
    return ((entries + 0.5 * column_offset(key, shape)) * weight_scale).astype(jnp.bfloat16)


def strengthened(drawn, rng, source, target, blocks, factor):
    owner, partner = [(jnp.arange(drawn.shape[dim]) // (drawn.shape[dim] // blocks)).reshape([-1 if axis == dim else 1 for axis in range(drawn.ndim)]) for dim in (source, target)]
    chosen = jax.random.permutation(rng, blocks)[partner]
    strong = (owner == chosen) | (owner == (partner + blocks // 2) % blocks)
    return jnp.where(strong, factor * drawn, drawn)


def levels(rng, extent, cuts, smallest, top_value):
    factor_of, own = 1.0, jax.random.fold_in(rng, 6)
    for axis_at, blocks in cuts:
        heights = jnp.exp(jax.random.uniform(jax.random.fold_in(own, axis_at), (blocks,), jnp.float32, smallest / len(cuts), top_value / len(cuts)))
        factor_of = factor_of * jnp.repeat(heights, extent[axis_at] // blocks).reshape([-1 if axis == axis_at else 1 for axis in range(len(extent))])
    return factor_of


def profile(count, total, reach, lean):
    portions = [(1 << 20) // math.isqrt(standing ** lean) + 1 for standing in range(2, count + 1)]
    surplus, counts = total - reach - (count - 1), [1] * (count - 1)
    while surplus > 0:
        free = [i for i in range(count - 1) if counts[i] < reach]
        mass, remaining = sum([portions[i] for i in free]), surplus
        for i in free:
            addition = min(reach - counts[i], max(1, remaining * portions[i] // mass), surplus)
            counts[i] = counts[i] + addition
            surplus = surplus - addition
    return np.array([reach] + counts)


def uneven_parts(own_key, count, total, limit, skew):
    if count == 2:
        one = jax.random.randint(own_key, (), max(1, total - limit), min(limit, total - 1) + 1)
        return jnp.stack([one, total - one])
    sizes = jnp.asarray(profile(count, total, limit, skew), jnp.int32)
    twos = (count - 1) // 2
    donor, sink = sizes[1:1 + 2 * twos:2], sizes[2:2 + 2 * twos:2]
    slack = jnp.minimum(donor - 1, limit - sink)
    passed = jax.random.randint(jax.random.fold_in(own_key, 1), (twos,), 0, 1 << 20) % (slack + 1)
    sizes = sizes.at[1:1 + 2 * twos:2].set(donor - passed).at[2:2 + 2 * twos:2].set(sink + passed)
    return sizes[jax.random.permutation(jax.random.fold_in(own_key, 2), count)]


def scatter_about(stream_key, dims, spread, bound, pieces=(), kind=jnp.bfloat16):
    level = levels(stream_key, dims, pieces, -0.22, 0.18) if pieces else 1.0
    values = jax.random.normal(stream_key, dims, jnp.float32) * spread * level
    return jnp.minimum(jnp.maximum(values, -bound), bound).astype(kind)


def noise_with(own_key, extent, width, reach, cuts, heavy, kind=jnp.bfloat16):
    values = width * jax.random.normal(own_key, extent, jnp.float32)
    if cuts:
        values = values * levels(own_key, extent, cuts, -0.22, 0.18)
    return jnp.clip(strengthened(values, jax.random.fold_in(own_key, 3), *heavy), -reach, reach).astype(kind)


def setup_inputs(seed: int = 0) -> dict:
    key_list = jax.random.split(jax.random.key(seed), 13)
    tokens = draw_tokens(jax.random.fold_in(key_list[12], 71), 0)
    segments = jax.vmap(lambda own: jnp.searchsorted(jnp.cumsum(uneven_parts(own, DOCS, SEQ_LEN, DOC_MOST, 1)), jnp.arange(SEQ_LEN), side="right"))(jax.random.split(key_list[1], SEQS)).reshape((SEQS, SEQ_LEN)).astype(jnp.int32)
    norm_gain = jnp.clip(1.0 + 0.1 * jax.random.normal(key_list[2], (D,), jnp.float32), 0.5, 1.5)
    norm_shift = scatter_about(key_list[3], (D,), 0.3, 4.0, (), jnp.float32)
    qkv_weight = draw_qkv_weight(jax.random.fold_in(key_list[12], 71), 0)
    qkv_bias = scatter_about(key_list[5], (3, D), 0.5, 6.0, ((1, 32),))
    dense_weight = scatter_about(key_list[6], (D, D), (D // 16) ** -0.5, 0.5, ((0, 4), (1, 8)))
    up_weight = draw_up_weight(jax.random.fold_in(key_list[12], 71), 0)
    up_bias = scatter_about(key_list[8], (FF,), 0.5, 6.0, ((0, 32),))
    down_weight = scatter_about(key_list[9], (FF, D), FF ** -0.5, 0.0625, ((0, 4), (1, 8)))
    out_bias = scatter_about(key_list[10], (D,), 0.5, 6.0, (), jnp.float32)
    cotangent = noise_with(key_list[11], (TOKENS, D), 1.0, 6.0, ((0, 32),), (0, 1, 32, 2.75))
    return {"tokens": tokens, "segments": segments, "norm_gain": norm_gain, "norm_shift": norm_shift, "qkv_weight": qkv_weight, "qkv_bias": qkv_bias, "dense_weight": dense_weight, "up_weight": up_weight, "up_bias": up_bias, "down_weight": down_weight, "out_bias": out_bias, "cotangent": cotangent}


@jax.custom_vjp
def low(v):
    return lax.optimization_barrier(v.astype(jnp.bfloat16)).astype(jnp.float32)

@jax.custom_vjp
def low_back(v):
    return v

def low_keep(v):
    return (low(v), None)

def low_pass(kept, grad):
    return (grad,)

def back_keep(v):
    return (v, None)

def back_low(kept, grad):
    return (low(grad),)
low.defvjp(low_keep, low_pass)
low_back.defvjp(back_keep, back_low)
EPS = 1e-05
GELU_C = math.sqrt(2.0 / math.pi)
PRECISE = lax.Precision.HIGHEST

def positions_of(segs):
    count = segs.shape[-1]
    position = jnp.broadcast_to(jnp.arange(count, dtype=jnp.int32), segs.shape)
    first_flag = jnp.ones(segs.shape[:-1] + (1,), dtype=bool)
    change = jnp.concatenate([first_flag, segs[..., 1:] != segs[..., :-1]], axis=-1)
    seg_start = lax.cummax(jnp.where(change, position, jnp.zeros_like(position)), axis=segs.ndim - 1)
    return position - seg_start

def rotary_tables(segs):
    half_rot = ROT // 2
    frequency = jnp.exp(-math.log(10000.0) * (2.0 * jnp.arange(half_rot, dtype=jnp.float32) / ROT))
    angles = positions_of(segs).astype(jnp.float32)[..., None] * frequency
    return (jnp.cos(angles), jnp.sin(angles))

def rotate(values_in, cosines, sines, direction):
    half_rot = ROT // 2
    front_part = values_in[..., :half_rot]
    back_part = values_in[..., half_rot:ROT]
    cos_wide = cosines[..., None, :]
    sin_wide = sines[..., None, :]
    return jnp.concatenate([front_part * cos_wide - direction * back_part * sin_wide, back_part * cos_wide + direction * front_part * sin_wide, values_in[..., ROT:]], axis=-1)

def gelu_value(u):
    tanh_value = jnp.tanh(GELU_C * (u + 0.044715 * u * u * u))
    return 0.5 * u * (1.0 + tanh_value)

def attend(query, keys, values, seg_row):
    block = min(512, SEQ_LEN)
    blocks = SEQ_LEN // block
    score_scale = 1.0 / math.sqrt(HEAD_DIM)
    key_pos = jnp.arange(SEQ_LEN, dtype=jnp.int32)

    def one_block(block_index):
        query_block = lax.dynamic_slice_in_dim(query, block_index * block, block, 0)
        query_seg = lax.dynamic_slice_in_dim(seg_row, block_index * block, block, 0)
        query_pos = block_index * block + jnp.arange(block, dtype=jnp.int32)
        scores = low_back(jnp.einsum('qhd,khd->hqk', query_block, keys, precision=PRECISE) * score_scale)
        allowed = (query_seg[:, None] == seg_row[None, :]) & (key_pos[None, :] <= query_pos[:, None])
        scores = jnp.where(allowed[None], scores, -jnp.inf)
        row_top = lax.optimization_barrier(jnp.max(scores, axis=-1, keepdims=True))
        exponent = jnp.exp(scores - row_top)
        attn_prob = low(exponent / lax.optimization_barrier(jnp.sum(exponent, axis=-1, keepdims=True)))
        return jnp.einsum('hqk,khd->qhd', attn_prob, values, precision=PRECISE)
    block_outs = lax.map(jax.checkpoint(one_block), jnp.arange(blocks, dtype=jnp.int32))
    return block_outs.reshape(SEQ_LEN, HEADS, HEAD_DIM)

def sequence_forward(resid, seg_row, norm_gain, norm_shift, qkv_weight, qkv_bias, dense_weight, up_weight, up_bias, down_weight, out_bias):
    row_mean = lax.optimization_barrier(jnp.mean(resid, axis=-1, keepdims=True))
    centered = resid - row_mean
    row_var = lax.optimization_barrier(jnp.mean(centered * centered, axis=-1, keepdims=True))
    normed = centered * lax.rsqrt(row_var + EPS)
    normed_low = low(normed * norm_gain + norm_shift)
    projected = low_back(jnp.einsum('td,cde->cte', normed_low, qkv_weight, precision=PRECISE) + qkv_bias[:, None, :])
    projected = projected.reshape(3, SEQ_LEN, HEADS, HEAD_DIM)
    cosines, sines = rotary_tables(seg_row)
    query = low(rotate(projected[0], cosines, sines, 1.0))
    keys = low(rotate(projected[1], cosines, sines, 1.0))
    values = low(projected[2])
    valid_rows = (seg_row != 0).astype(jnp.float32)[:, None]
    context = attend(query, keys, values, seg_row).reshape(SEQ_LEN, D)
    context = low(low_back(context * valid_rows))
    attn_out = jnp.dot(context, dense_weight, precision=PRECISE)
    hidden_pre = low_back(jnp.dot(normed_low, up_weight, precision=PRECISE) + up_bias)
    hidden_act = low(gelu_value(hidden_pre))
    mlp_out = jnp.dot(hidden_act, down_weight, precision=PRECISE)
    result = resid + attn_out + mlp_out + out_bias
    partial_sums = jnp.stack([jnp.sum(valid_rows * resid * resid), jnp.sum(valid_rows * attn_out * attn_out), jnp.sum(valid_rows * mlp_out * mlp_out), jnp.sum(valid_rows) * D])
    return (result, partial_sums)

def reference(tokens, segments, norm_gain, norm_shift, qkv_weight, qkv_bias, dense_weight, up_weight, up_bias, down_weight, out_bias, cotangent):

    def forward(resid, gain_in, shift_in, qkv_in, qbias_in, dense_in, up_in, ubias_in, down_in, obias_in):
        resid_seq = resid.reshape(SEQS, SEQ_LEN, D)

        def per_sequence(state, item):
            resid_one, seg_row = item
            result, partial_sums = jax.checkpoint(sequence_forward)(resid_one, seg_row, gain_in, shift_in, qkv_in, qbias_in, dense_in, up_in, ubias_in, down_in, obias_in)
            return (state + partial_sums, result)
        totals, results = lax.scan(per_sequence, jnp.zeros((4,), jnp.float32), (resid_seq, segments))
        return (results.reshape(TOKENS, D), totals)
    output, pullback, totals = jax.vjp(forward, tokens.astype(jnp.float32), norm_gain.astype(jnp.float32), norm_shift.astype(jnp.float32), qkv_weight.astype(jnp.float32), qkv_bias.astype(jnp.float32), dense_weight.astype(jnp.float32), up_weight.astype(jnp.float32), up_bias.astype(jnp.float32), down_weight.astype(jnp.float32), out_bias.astype(jnp.float32), has_aux=True)
    grads = pullback(cotangent.astype(jnp.float32))
    root_squares = jnp.sqrt(totals[:3] / totals[3]).astype(jnp.float32)
    return (output.astype(jnp.bfloat16), grads[0].astype(jnp.bfloat16), grads[1].astype(jnp.float32), grads[2].astype(jnp.float32), grads[3].astype(jnp.float32), grads[4].astype(jnp.float32), grads[5].astype(jnp.float32), grads[6].astype(jnp.float32), grads[7].astype(jnp.float32), grads[8].astype(jnp.float32), grads[9].astype(jnp.float32), root_squares)
```

```python
import functools
import math

import jax
import jax.numpy as jnp
from jax import lax
from jax.experimental import pallas as pl
from jax.experimental.pallas import tpu as pltpu
from jax.sharding import PartitionSpec as P

HEAD_DIM = 64
ROT = 32
PAIR = 2 * HEAD_DIM
BLOCK = 256

EPS = 1e-05
GELU_C = math.sqrt(2.0 / math.pi)


def segment_starts(segs):
    return jnp.sum((segs[:, None, :] < segs[:, :, None]).astype(jnp.int32), axis=-1)


def rotary_wide(starts):
    length = starts.shape[0]
    half_rot = ROT // 2
    frequency = jnp.exp(-math.log(10000.0) * (2.0 * jnp.arange(half_rot, dtype=jnp.float32) / ROT))
    position = jnp.arange(length, dtype=jnp.int32) - starts
    angles = position.astype(jnp.float32)[:, None] * frequency
    cosines, sines = jnp.cos(angles), jnp.sin(angles)
    ones = jnp.ones((length, HEAD_DIM - ROT), jnp.float32)
    cos_head = jnp.concatenate([cosines, cosines, ones], axis=-1)
    sin_head = jnp.concatenate([-sines, sines, 0.0 * ones], axis=-1)
    return (jnp.concatenate([cos_head, cos_head], -1), jnp.concatenate([sin_head, sin_head], -1))


def turn(x, cos_wide, sin_wide):
    lane = lax.broadcasted_iota(jnp.int32, x.shape, 1) % HEAD_DIM
    half_rot = ROT // 2
    partner = jnp.where(
        lane < half_rot, pltpu.roll(x, PAIR - half_rot, 1), pltpu.roll(x, half_rot, 1)
    )
    return x * cos_wide + partner * sin_wide


def first_half(shape):
    return lax.broadcasted_iota(jnp.int32, shape, len(shape) - 1) < HEAD_DIM


def halves(x):
    front = first_half(x.shape)
    zero = jnp.zeros_like(x)
    return (jnp.where(front, x, zero), jnp.where(front, zero, x))


def nt(left, right):
    return lax.dot_general(
        left, right, (((1,), (1,)), ((), ())), preferred_element_type=jnp.float32
    )


def nn(left, right):
    return lax.dot_general(
        left, right, (((1,), (0,)), ((), ())), preferred_element_type=jnp.float32
    )


def tn(left, right):
    return lax.dot_general(
        left, right, (((0,), (0,)), ((), ())), preferred_element_type=jnp.float32
    )


def attend_kernel(
    low_ref, xq_ref, xk_ref, xv_ref, bias_ref, cos_ref, sin_ref, start_ref, valid_ref,
    q_ref, k_ref, v_ref, ctx_ref, lse_ref, km, vm, s_scr,
):
    length = q_ref.shape[0]
    blocks = length // BLOCK
    scale = 1.0 / math.sqrt(HEAD_DIM)

    def project(i, _):
        rows = pl.ds(pl.multiple_of(i * BLOCK, BLOCK), BLOCK)
        cw, sw = cos_ref[rows, :], sin_ref[rows, :]
        q = turn(xq_ref[0, rows, :] + bias_ref[0], cw, sw).astype(jnp.bfloat16)
        q_ref[rows, :] = q * jnp.bfloat16(scale)
        k = turn(xk_ref[0, rows, :] + bias_ref[1], cw, sw).astype(jnp.bfloat16)
        k_ref[rows, :] = k
        v = (xv_ref[0, rows, :] + bias_ref[2]).astype(jnp.bfloat16)
        v_ref[rows, :] = v
        km[0, rows, :], km[1, rows, :] = halves(k)
        vm[0, rows, :], vm[1, rows, :] = halves(v)
        return 0

    lax.fori_loop(0, blocks, project, 0)

    def query_block(i, _):
        rows = pl.ds(pl.multiple_of(i * BLOCK, BLOCK), BLOCK)
        q = q_ref[rows, :]
        start = start_ref[rows, :][:, :1]
        low = low_ref[i]
        qpos = i * BLOCK + lax.broadcasted_iota(jnp.int32, (BLOCK, BLOCK), 0)

        def top(j, tops):
            cols = pl.ds(pl.multiple_of(j * BLOCK, BLOCK), BLOCK)
            kpos = j * BLOCK + lax.broadcasted_iota(jnp.int32, (BLOCK, BLOCK), 1)
            allowed = (kpos >= start) & (kpos <= qpos)
            out = []
            for h in range(2):
                s = jnp.where(allowed, nt(q, km[h, cols, :]), -jnp.inf)
                s_scr[h, j] = s
                out.append(jnp.maximum(tops[h], jnp.max(s, axis=-1, keepdims=True)))
            return tuple(out)

        floor = jnp.full((BLOCK, 1), -jnp.inf, jnp.float32)
        tops = lax.fori_loop(low, i + 1, top, (floor, floor))

        def weigh(j, state):
            sum_0, sum_1, acc = state
            cols = pl.ds(pl.multiple_of(j * BLOCK, BLOCK), BLOCK)
            sums = [sum_0, sum_1]
            for h in range(2):
                e = jnp.exp(s_scr[h, j] - tops[h])
                sums[h] = sums[h] + jnp.sum(e, axis=-1, keepdims=True)
                acc = acc + nn(e.astype(jnp.bfloat16), vm[h, cols, :])
            return (sums[0], sums[1], acc)

        none = jnp.zeros((BLOCK, 1), jnp.float32)
        sum_0, sum_1, acc = lax.fori_loop(
            low, i + 1, weigh, (none, none, jnp.zeros((BLOCK, PAIR), jnp.float32))
        )
        front = first_half((BLOCK, PAIR))
        out = acc / jnp.where(front, sum_0, sum_1)
        ctx_ref[rows, :] = (out * valid_ref[rows, :]).astype(jnp.bfloat16)
        lse = jnp.where(front, tops[0] + jnp.log(sum_0), tops[1] + jnp.log(sum_1))
        lse_t = lse.T
        lse_ref[0, 0:1, rows] = lse_t[0:1, :]
        lse_ref[0, 1:2, rows] = lse_t[HEAD_DIM : HEAD_DIM + 1, :]
        return 0

    lax.fori_loop(0, blocks, query_block, 0)


def attention_forward(projected, bias, cos_wide, sin_wide, starts, valid_wide, lows):
    _, length, width = projected.shape
    pairs = width // PAIR
    blocks = length // BLOCK
    start_wide = jnp.broadcast_to(starts[:, None], (length, PAIR))
    part = lambda c: pl.BlockSpec((1, length, PAIR), lambda p, low, c=c: (c, 0, p))
    table = pl.BlockSpec((length, PAIR), lambda p, low: (0, 0))
    flat = pl.BlockSpec((length, PAIR), lambda p, low: (0, p))
    flat_shape = jax.ShapeDtypeStruct((length, width), jnp.bfloat16)
    return pl.pallas_call(
        attend_kernel,
        grid_spec=pltpu.PrefetchScalarGridSpec(
            num_scalar_prefetch=1,
            grid=(pairs,),
            in_specs=[
                part(0), part(1), part(2),
                pl.BlockSpec((3, 1, PAIR), lambda p, low: (0, 0, p)),
                table, table, table, table,
            ],
            out_specs=[flat, flat, flat, flat,
                       pl.BlockSpec((1, 2, length), lambda p, low: (p, 0, 0))],
            scratch_shapes=[
                pltpu.VMEM((2, length, PAIR), jnp.bfloat16),
                pltpu.VMEM((2, length, PAIR), jnp.bfloat16),
                pltpu.VMEM((2, blocks, BLOCK, BLOCK), jnp.float32),
            ],
        ),
        out_shape=[flat_shape] * 4 + [jax.ShapeDtypeStruct((pairs, 2, length), jnp.float32)],
        compiler_params=pltpu.CompilerParams(vmem_limit_bytes=48 * 2**20),
        name="attend",
    )(lows, projected, projected, projected, bias[:, None, :], cos_wide, sin_wide, start_wide, valid_wide)


def attend_back_kernel(
    low_ref, q_ref, k_ref, v_ref, do_ref, lse_ref, cos_ref, sin_ref, start_ref,
    grad_ref, sums_ref, qm, km, vm, dom, p_scr, dp_scr, dk_acc, dv_acc,
):
    length = q_ref.shape[0]
    blocks = length // BLOCK
    scale = 1.0 / math.sqrt(HEAD_DIM)

    def split(i, _):
        rows = pl.ds(pl.multiple_of(i * BLOCK, BLOCK), BLOCK)
        qm[0, rows, :], qm[1, rows, :] = halves(q_ref[rows, :])
        km[0, rows, :], km[1, rows, :] = halves(k_ref[rows, :])
        vm[0, rows, :], vm[1, rows, :] = halves(v_ref[rows, :])
        dom[0, rows, :], dom[1, rows, :] = halves(do_ref[rows, :])
        dk_acc[rows, :] = jnp.zeros((BLOCK, PAIR), jnp.float32)
        dv_acc[rows, :] = jnp.zeros((BLOCK, PAIR), jnp.float32)
        return 0

    lax.fori_loop(0, blocks, split, 0)

    def query_block(i, total):
        rows = pl.ds(pl.multiple_of(i * BLOCK, BLOCK), BLOCK)
        q = q_ref[rows, :]
        do = do_ref[rows, :]
        start = start_ref[:, rows]
        low = low_ref[i]
        qpos = i * BLOCK + lax.broadcasted_iota(jnp.int32, (BLOCK, BLOCK), 1)
        lse = [lse_ref[0, h : h + 1, rows] for h in range(2)]

        def weigh(j, deltas):
            cols = pl.ds(pl.multiple_of(j * BLOCK, BLOCK), BLOCK)
            kpos = j * BLOCK + lax.broadcasted_iota(jnp.int32, (BLOCK, BLOCK), 0)
            allowed = (kpos >= start) & (kpos <= qpos)
            out = []
            for h in range(2):
                s = nt(km[h, cols, :], q)
                p = jnp.where(allowed, jnp.exp(s - lse[h]), 0.0)
                dp = nt(vm[h, cols, :], do)
                p_scr[h, j] = p
                dp_scr[h, j] = dp
                out.append(deltas[h] + jnp.sum(p * dp, axis=0, keepdims=True))
            return tuple(out)

        none = jnp.zeros((1, BLOCK), jnp.float32)
        deltas = lax.fori_loop(low, i + 1, weigh, (none, none))

        def gather(j, dq):
            cols = pl.ds(pl.multiple_of(j * BLOCK, BLOCK), BLOCK)
            dk = dk_acc[cols, :]
            dv = dv_acc[cols, :]
            for h in range(2):
                p = p_scr[h, j]
                ds = (p * (dp_scr[h, j] - deltas[h])).astype(jnp.bfloat16)
                dv = dv + nn(p.astype(jnp.bfloat16), dom[h, rows, :])
                dk = dk + nn(ds, qm[h, rows, :])
                dq = dq + tn(ds, km[h, cols, :])
            dk_acc[cols, :] = dk
            dv_acc[cols, :] = dv
            return dq

        dq = lax.fori_loop(low, i + 1, gather, jnp.zeros((BLOCK, PAIR), jnp.float32))
        dq = turn(dq * scale, cos_ref[rows, :], -sin_ref[rows, :]).astype(jnp.bfloat16)
        grad_ref[0, rows, :] = dq
        return total + jnp.sum(dq.astype(jnp.float32), axis=0, keepdims=True)

    none = jnp.zeros((1, PAIR), jnp.float32)
    sums_ref[0] = lax.fori_loop(0, blocks, query_block, none)

    def finish(i, totals):
        rows = pl.ds(pl.multiple_of(i * BLOCK, BLOCK), BLOCK)
        dk = turn(dk_acc[rows, :], cos_ref[rows, :], -sin_ref[rows, :]).astype(jnp.bfloat16)
        dv = dv_acc[rows, :].astype(jnp.bfloat16)
        grad_ref[1, rows, :] = dk
        grad_ref[2, rows, :] = dv
        return (
            totals[0] + jnp.sum(dk.astype(jnp.float32), axis=0, keepdims=True),
            totals[1] + jnp.sum(dv.astype(jnp.float32), axis=0, keepdims=True),
        )

    sums_ref[1], sums_ref[2] = lax.fori_loop(0, blocks, finish, (none, none))


def attention_backward(q, k, v, do, lse, cos_wide, sin_wide, starts, lows):
    length, width = q.shape
    pairs = width // PAIR
    blocks = length // BLOCK
    flat = pl.BlockSpec((length, PAIR), lambda p, low: (0, p))
    table = pl.BlockSpec((length, PAIR), lambda p, low: (0, 0))
    grad, sums = pl.pallas_call(
        attend_back_kernel,
        grid_spec=pltpu.PrefetchScalarGridSpec(
            num_scalar_prefetch=1,
            grid=(pairs,),
            in_specs=[
                flat, flat, flat, flat,
                pl.BlockSpec((1, 2, length), lambda p, low: (p, 0, 0)),
                table, table,
                pl.BlockSpec((1, length), lambda p, low: (0, 0)),
            ],
            out_specs=[
                pl.BlockSpec((3, length, PAIR), lambda p, low: (0, 0, p)),
                pl.BlockSpec((3, 1, PAIR), lambda p, low: (0, 0, p)),
            ],
            scratch_shapes=[pltpu.VMEM((2, length, PAIR), jnp.bfloat16)] * 4
            + [pltpu.VMEM((2, blocks, BLOCK, BLOCK), jnp.float32)] * 2
            + [pltpu.VMEM((length, PAIR), jnp.float32)] * 2,
        ),
        out_shape=[
            jax.ShapeDtypeStruct((3, length, width), jnp.bfloat16),
            jax.ShapeDtypeStruct((3, 1, width), jnp.float32),
        ],
        compiler_params=pltpu.CompilerParams(vmem_limit_bytes=48 * 2**20),
        name="attend_back",
    )(lows, q, k, v, do, lse, cos_wide, sin_wide, starts[None, :])
    return (grad, sums[:, 0, :])


def gelu_value(u):
    tanh_value = jnp.tanh(GELU_C * (u + 0.044715 * u * u * u))
    return 0.5 * u * (1.0 + tanh_value)


def gelu_slope(u):
    tanh_value = jnp.tanh(GELU_C * (u + 0.044715 * u * u * u))
    return 0.5 * (1.0 + tanh_value) + 0.5 * u * (1.0 - tanh_value * tanh_value) * GELU_C * (
        1.0 + 3.0 * 0.044715 * u * u
    )


def contract_rows(left, right):
    return lax.dot_general(
        left, right, (((0,), (0,)), ((), ())), preferred_element_type=jnp.float32
    )


def contract_cols(left, right):
    return lax.dot_general(
        left, right, (((1,), (1,)), ((), ())), preferred_element_type=jnp.float32
    )


def scatter_low(part, axis, dim):
    return lax.psum_scatter(
        part.astype(jnp.bfloat16), axis, scatter_dimension=dim, tiled=True
    ).astype(jnp.float32)


def body(
    tokens,
    segments,
    norm_gain,
    norm_shift,
    qkv_weight,
    qkv_bias,
    dense_weight,
    up_weight,
    up_bias,
    down_weight,
    out_bias,
    cotangent,
):
    row_count, model_width = tokens.shape
    seq_count, length = segments.shape
    all_rows = seq_count * length
    my_start = lax.axis_index("tensor") * row_count
    resid = tokens.astype(jnp.float32)
    row_mean = jnp.mean(resid, axis=-1, keepdims=True)
    centered = resid - row_mean
    inverse = lax.rsqrt(jnp.mean(centered * centered, axis=-1, keepdims=True) + EPS)
    normed = centered * inverse
    normed_mine = (normed * norm_gain + norm_shift).astype(jnp.bfloat16)
    normed_low = lax.all_gather(normed_mine, "tensor", axis=0, tiled=True)
    full_qkv, full_dense, full_up, full_down, full_qbias, full_ubias = (
        lax.all_gather(qkv_weight, "dp", axis=1, tiled=True),
        lax.all_gather(dense_weight, "dp", axis=1, tiled=True),
        lax.all_gather(up_weight, "dp", axis=0, tiled=True),
        lax.all_gather(down_weight, "dp", axis=1, tiled=True),
        lax.all_gather(qkv_bias, "dp", axis=1, tiled=True),
        lax.all_gather(up_bias, "dp", axis=0, tiled=True),
    )
    starts = segment_starts(segments)[0]
    cos_wide, sin_wide = rotary_wide(starts)
    valid_rows = (segments != 0).astype(jnp.float32).reshape(all_rows, 1)
    valid_wide = jnp.broadcast_to(valid_rows, (length, PAIR))
    lows = starts[::BLOCK] // BLOCK
    projected = jnp.einsum(
        "td,cde->cte", normed_low, full_qkv, preferred_element_type=jnp.float32
    )
    query, keys, values, context_low, logsum = attention_forward(
        projected, full_qbias.astype(jnp.float32), cos_wide, sin_wide, starts, valid_wide, lows
    )
    attn_part = jnp.dot(context_low, full_dense, preferred_element_type=jnp.float32)
    every_up, every_down = (full_up, full_down)
    hidden_pre = jnp.dot(
        normed_low, full_up, preferred_element_type=jnp.float32
    ) + full_ubias.astype(jnp.float32)
    hidden_act = gelu_value(hidden_pre).astype(jnp.bfloat16)
    mlp_part = jnp.dot(hidden_act, full_down, preferred_element_type=jnp.float32)
    attn_mine, mlp_mine = (
        scatter_low(attn_part, "tensor", 0),
        scatter_low(mlp_part, "tensor", 0),
    )
    output = (resid + attn_mine + mlp_mine + out_bias).astype(jnp.bfloat16)
    valid_mine = lax.dynamic_slice_in_dim(valid_rows, my_start, row_count, 0)
    totals = lax.psum(
        (
            jnp.sum(valid_mine * resid * resid),
            jnp.sum(valid_mine * attn_mine * attn_mine),
            jnp.sum(valid_mine * mlp_mine * mlp_mine),
            jnp.sum(valid_mine) * model_width,
        ),
        ("dp", "tensor"),
    )
    root_squares = jnp.sqrt(jnp.stack([totals[0], totals[1], totals[2]]) / totals[3])
    grad_full = lax.all_gather(cotangent, "tensor", axis=0, tiled=True)
    grad_dense = contract_rows(context_low, grad_full)
    grad_context = contract_cols(grad_full, full_dense)
    grad_context_low = grad_context.astype(jnp.bfloat16) * valid_rows.astype(jnp.bfloat16)
    grad_down = contract_rows(hidden_act, grad_full)
    grad_act = contract_cols(grad_full, every_down)
    grad_pre = (grad_act * gelu_slope(hidden_pre)).astype(jnp.bfloat16)
    grad_up = contract_rows(normed_low, grad_pre)
    grad_ubias = jnp.sum(grad_pre, axis=0, dtype=jnp.float32)
    mlp_normed = contract_cols(grad_pre, every_up)
    grad_proj, grad_qbias = attention_backward(
        query, keys, values, grad_context_low, logsum, cos_wide, sin_wide, starts, lows
    )
    grad_qkv = jnp.einsum("td,cte->cde", normed_low, grad_proj, preferred_element_type=jnp.float32)
    grad_normed = jnp.einsum("cte,cde->td", grad_proj, full_qkv, preferred_element_type=jnp.float32)
    part_qkv, part_dense, part_up, part_down, part_qbias, part_ubias = (
        scatter_low(grad_qkv, "dp", 1),
        scatter_low(grad_dense, "dp", 1),
        scatter_low(grad_up, "dp", 0),
        scatter_low(grad_down, "dp", 1),
        lax.psum_scatter(grad_qbias, "dp", scatter_dimension=1, tiled=True),
        lax.psum_scatter(grad_ubias, "dp", scatter_dimension=0, tiled=True),
    )
    normed_term = grad_normed + mlp_normed
    grad_mine = scatter_low(normed_term, "tensor", 0)
    scaled = grad_mine * norm_gain
    grad_tokens = (
        cotangent.astype(jnp.float32)
        + inverse
        * (
            scaled
            - jnp.mean(scaled, axis=-1, keepdims=True)
            - normed * jnp.mean(scaled * normed, axis=-1, keepdims=True)
        )
    ).astype(jnp.bfloat16)
    part_gain, part_shift, part_obias = (
        lax.psum_scatter(
            jnp.sum(grad_mine * normed, axis=0), ("dp", "tensor"), scatter_dimension=0, tiled=True
        ),
        lax.psum_scatter(
            jnp.sum(grad_mine, axis=0), ("dp", "tensor"), scatter_dimension=0, tiled=True
        ),
        lax.psum_scatter(
            jnp.sum(cotangent, axis=0, dtype=jnp.float32),
            ("dp", "tensor"),
            scatter_dimension=0,
            tiled=True,
        ),
    )
    return (
        output,
        grad_tokens,
        part_gain,
        part_shift,
        part_qkv,
        part_qbias,
        part_dense,
        part_up,
        part_ubias,
        part_down,
        part_obias,
        root_squares,
    )


def solution(mesh):
    placed = (
        P(("dp", "tensor"), None),
        P("dp", None),
        P(),
        P(),
        P(None, "dp", "tensor"),
        P(None, ("tensor", "dp")),
        P("tensor", "dp"),
        P("dp", "tensor"),
        P(("tensor", "dp")),
        P("tensor", "dp"),
        P(),
        P(("dp", "tensor"), None),
    )
    return jax.shard_map(
        body,
        mesh=mesh,
        in_specs=placed,
        out_specs=(
            P(("dp", "tensor"), None),
            P(("dp", "tensor"), None),
            P(("dp", "tensor")),
            P(("dp", "tensor")),
            P(None, "dp", "tensor"),
            P(None, ("tensor", "dp")),
            P("tensor", "dp"),
            P("dp", "tensor"),
            P(("tensor", "dp")),
            P("tensor", "dp"),
            P(("dp", "tensor")),
            P(),
        ),
        check_vma=False,
    )
```

```python
import functools
import math

import jax
import jax.numpy as jnp
from jax import lax
from jax.experimental import pallas as pl
from jax.experimental.pallas import tpu as pltpu
from jax.sharding import PartitionSpec as P

HEAD_DIM = 64
ROT = 32
PAIR = 2 * HEAD_DIM
BLOCK = 256
MOST = 5

EPS = 1e-05
GELU_C = math.sqrt(2.0 / math.pi)


def segment_starts(segs):
    return jnp.sum((segs[:, None, :] < segs[:, :, None]).astype(jnp.int32), axis=-1)


def rotary_wide(starts):
    length = starts.shape[0]
    half_rot = ROT // 2
    frequency = jnp.exp(-math.log(10000.0) * (2.0 * jnp.arange(half_rot, dtype=jnp.float32) / ROT))
    position = jnp.arange(length, dtype=jnp.int32) - starts
    angles = position.astype(jnp.float32)[:, None] * frequency
    cosines, sines = jnp.cos(angles), jnp.sin(angles)
    ones = jnp.ones((length, HEAD_DIM - ROT), jnp.float32)
    cos_head = jnp.concatenate([cosines, cosines, ones], axis=-1)
    sin_head = jnp.concatenate([-sines, sines, 0.0 * ones], axis=-1)
    return (jnp.concatenate([cos_head, cos_head], -1), jnp.concatenate([sin_head, sin_head], -1))


def turn(x, cos_wide, sin_wide):
    lane = lax.broadcasted_iota(jnp.int32, x.shape, 1) % HEAD_DIM
    half_rot = ROT // 2
    partner = jnp.where(
        lane < half_rot, pltpu.roll(x, PAIR - half_rot, 1), pltpu.roll(x, half_rot, 1)
    )
    return x * cos_wide + partner * sin_wide


def first_half(shape):
    return lax.broadcasted_iota(jnp.int32, shape, len(shape) - 1) < HEAD_DIM


def halves(x):
    front = first_half(x.shape)
    zero = jnp.zeros_like(x)
    return (jnp.where(front, x, zero), jnp.where(front, zero, x))


def nt(left, right):
    return lax.dot_general(
        left, right, (((1,), (1,)), ((), ())), preferred_element_type=jnp.float32
    )


def nn(left, right):
    return lax.dot_general(
        left, right, (((1,), (0,)), ((), ())), preferred_element_type=jnp.float32
    )


def tn(left, right):
    return lax.dot_general(
        left, right, (((0,), (0,)), ((), ())), preferred_element_type=jnp.float32
    )


def attend_kernel(
    low_ref, place_ref, parts, bias_ref, cos_ref, sin_ref, start_ref, valid_ref,
    q_ref, k_ref, v_ref, ctx_ref, lse_ref, km, vm,
):
    length = q_ref.shape[0]
    blocks = length // BLOCK
    scale = 1.0 / math.sqrt(HEAD_DIM)

    per = length // len(parts) // BLOCK

    def project(i, slot):
        rows = pl.ds(pl.multiple_of(place_ref[slot * per + i] * BLOCK, BLOCK), BLOCK)
        here = pl.ds(i * BLOCK, BLOCK)
        part = parts[slot]
        cw, sw = cos_ref[rows, :], sin_ref[rows, :]
        q = turn(part[0, here, :] + bias_ref[0], cw, sw).astype(jnp.bfloat16)
        q_ref[rows, :] = q * jnp.bfloat16(scale)
        k = turn(part[1, here, :] + bias_ref[1], cw, sw).astype(jnp.bfloat16)
        k_ref[rows, :] = k
        v = (part[2, here, :] + bias_ref[2]).astype(jnp.bfloat16)
        v_ref[rows, :] = v
        km[0, rows, :], km[1, rows, :] = halves(k)
        vm[0, rows, :], vm[1, rows, :] = halves(v)

    for slot in range(len(parts)):
        for i in range(per):
            project(i, slot)

    def query_block(i, count):
        rows = pl.ds(pl.multiple_of(i * BLOCK, BLOCK), BLOCK)
        base = pl.multiple_of((i + 1 - count) * BLOCK, BLOCK)
        cols = pl.ds(base, count * BLOCK)
        shape = (BLOCK, count * BLOCK)
        q = q_ref[rows, :]
        start = start_ref[rows, :][:, :1] - base
        kpos = lax.broadcasted_iota(jnp.int32, shape, 1)
        qpos = lax.broadcasted_iota(jnp.int32, shape, 0) + (count - 1) * BLOCK
        allowed = (kpos >= start) & (kpos <= qpos)
        there = pl.ds(pl.multiple_of(place_ref[i] * BLOCK, BLOCK), BLOCK)
        acc = jnp.zeros((BLOCK, PAIR), jnp.float32)
        tops, sums = [], []
        for h in range(2):
            s = jnp.where(allowed, nt(q, km[h, cols, :]), -jnp.inf)
            top = jnp.max(s, axis=-1, keepdims=True)
            e = jnp.exp(s - top)
            tops.append(top)
            sums.append(jnp.sum(e, axis=-1, keepdims=True))
            acc = acc + nn(e.astype(jnp.bfloat16), vm[h, cols, :])
        front = first_half((BLOCK, PAIR))
        out = acc / jnp.where(front, sums[0], sums[1])
        ctx_ref[there, :] = (out * valid_ref[rows, :]).astype(jnp.bfloat16)
        lse = jnp.where(front, tops[0] + jnp.log(sums[0]), tops[1] + jnp.log(sums[1]))
        lse_t = lse.T
        lse_ref[0, 0:1, rows] = lse_t[0:1, :]
        lse_ref[0, 1:2, rows] = lse_t[HEAD_DIM : HEAD_DIM + 1, :]

    def step(i, _):
        for count in range(1, MOST + 1):
            pl.when(i + 1 - low_ref[i] == count)(functools.partial(query_block, i, count))
        return 0

    lax.fori_loop(0, blocks, step, 0)


def attention_forward(projected, bias, tables, first, count, held=None):
    cos_wide, sin_wide, starts, valid_wide, lows, places = tables
    width = projected[0].shape[2]
    length = starts.shape[0]
    blocks = length // BLOCK
    ways = len(projected)
    start_wide = jnp.broadcast_to(starts[:, None], (length, PAIR))
    part = pl.BlockSpec((3, length // ways, PAIR), lambda p, low, place: (0, 0, p + first))
    table = pl.BlockSpec((length, PAIR), lambda p, low, place: (0, 0))
    flat = pl.BlockSpec((length, PAIR), lambda p, low, place: (0, p + first))
    flat_shape = jax.ShapeDtypeStruct((length, width), jnp.bfloat16)
    held = tuple(held or ())

    def kernel(*refs):
        rest = refs[2 + ways :]
        attend_kernel(*refs[:2], refs[2 : 2 + ways], *rest[:5], *rest[5 + len(held) :])

    return pl.pallas_call(
        kernel,
        grid_spec=pltpu.PrefetchScalarGridSpec(
            num_scalar_prefetch=2,
            grid=(count,),
            in_specs=[
                *[part] * ways,
                pl.BlockSpec((3, 1, PAIR), lambda p, low, place: (0, 0, p + first)),
                table, table, table, table,
            ] + [pl.BlockSpec(memory_space=pl.ANY)] * len(held),
            out_specs=[flat, flat, flat, flat,
                       pl.BlockSpec((1, 2, length), lambda p, low, place: (p + first, 0, 0))],
            scratch_shapes=[
                pltpu.VMEM((2, length, PAIR), jnp.bfloat16),
                pltpu.VMEM((2, length, PAIR), jnp.bfloat16),
            ],
        ),
        out_shape=[flat_shape] * 4
        + [jax.ShapeDtypeStruct((width // PAIR, 2, length), jnp.float32)],
        input_output_aliases={7 + ways + i: i for i in range(len(held))},
        compiler_params=pltpu.CompilerParams(vmem_limit_bytes=48 * 2**20),
        name="attend",
    )(lows, places, *projected, bias[:, None, :], cos_wide, sin_wide,
      start_wide, valid_wide, *held)


def attend_back_kernel(
    low_ref, place_ref, dos, q_ref, k_ref, v_ref, lse_ref, cos_ref, sin_ref, start_ref, valid_ref,
    grad_ref, sums_ref, qm, km, vm, dom, do_scr, dk_acc, dv_acc,
):
    length = q_ref.shape[0]
    blocks = length // BLOCK
    scale = 1.0 / math.sqrt(HEAD_DIM)

    def split(i, _):
        rows = pl.ds(pl.multiple_of(i * BLOCK, BLOCK), BLOCK)
        qm[0, rows, :], qm[1, rows, :] = halves(q_ref[rows, :])
        km[0, rows, :], km[1, rows, :] = halves(k_ref[rows, :])
        vm[0, rows, :], vm[1, rows, :] = halves(v_ref[rows, :])
        dk_acc[rows, :] = jnp.zeros((BLOCK, PAIR), jnp.float32)
        dv_acc[rows, :] = jnp.zeros((BLOCK, PAIR), jnp.float32)
        return 0

    lax.fori_loop(0, blocks, split, 0)

    per = length // len(dos) // BLOCK
    for slot in range(len(dos)):
        for i in range(per):
            rows = pl.ds(pl.multiple_of(place_ref[slot * per + i] * BLOCK, BLOCK), BLOCK)
            do = dos[slot][i * BLOCK : (i + 1) * BLOCK, :].astype(jnp.float32)
            do = (do * valid_ref[rows, :]).astype(jnp.bfloat16)
            do_scr[rows, :] = do
            dom[0, rows, :], dom[1, rows, :] = halves(do)

    def query_block(i, count):
        rows = pl.ds(pl.multiple_of(i * BLOCK, BLOCK), BLOCK)
        base = pl.multiple_of((i + 1 - count) * BLOCK, BLOCK)
        cols = pl.ds(base, count * BLOCK)
        shape = (count * BLOCK, BLOCK)
        q = q_ref[rows, :]
        do = do_scr[rows, :]
        start = start_ref[:, rows] - base
        kpos = lax.broadcasted_iota(jnp.int32, shape, 0)
        qpos = lax.broadcasted_iota(jnp.int32, shape, 1) + (count - 1) * BLOCK
        allowed = (kpos >= start) & (kpos <= qpos)
        dk = dk_acc[cols, :]
        dv = dv_acc[cols, :]
        dq = jnp.zeros((BLOCK, PAIR), jnp.float32)
        for h in range(2):
            s = nt(km[h, cols, :], q)
            p = jnp.where(allowed, jnp.exp(s - lse_ref[0, h : h + 1, rows]), 0.0)
            dp = nt(vm[h, cols, :], do)
            delta = jnp.sum(p * dp, axis=0, keepdims=True)
            dv = dv + nn(p.astype(jnp.bfloat16), dom[h, rows, :])
            ds = (p * (dp - delta)).astype(jnp.bfloat16)
            dk = dk + nn(ds, qm[h, rows, :])
            dq = dq + tn(ds, km[h, cols, :])
        dk_acc[cols, :] = dk
        dv_acc[cols, :] = dv
        dq = turn(dq * scale, cos_ref[rows, :], -sin_ref[rows, :]).astype(jnp.bfloat16)
        there = pl.ds(pl.multiple_of(place_ref[i] * BLOCK, BLOCK), BLOCK)
        grad_ref[0, there, :] = dq
        sums_ref[0] += jnp.sum(dq.astype(jnp.float32), axis=0, keepdims=True)

    none = jnp.zeros((1, PAIR), jnp.float32)
    sums_ref[0] = none

    def step(i, _):
        for count in range(1, MOST + 1):
            pl.when(i + 1 - low_ref[i] == count)(functools.partial(query_block, i, count))
        return 0

    lax.fori_loop(0, blocks, step, 0)

    def finish(i, totals):
        rows = pl.ds(pl.multiple_of(i * BLOCK, BLOCK), BLOCK)
        dk = turn(dk_acc[rows, :], cos_ref[rows, :], -sin_ref[rows, :]).astype(jnp.bfloat16)
        dv = dv_acc[rows, :].astype(jnp.bfloat16)
        there = pl.ds(pl.multiple_of(place_ref[i] * BLOCK, BLOCK), BLOCK)
        grad_ref[1, there, :] = dk
        grad_ref[2, there, :] = dv
        return (
            totals[0] + jnp.sum(dk.astype(jnp.float32), axis=0, keepdims=True),
            totals[1] + jnp.sum(dv.astype(jnp.float32), axis=0, keepdims=True),
        )

    sums_ref[1], sums_ref[2] = lax.fori_loop(0, blocks, finish, (none, none))


def attention_backward(q, k, v, do, lse, tables, first, count, held=None):
    cos_wide, sin_wide, starts, valid_wide, lows, places = tables
    length, width = q.shape
    blocks = length // BLOCK
    flat = pl.BlockSpec((length, PAIR), lambda p, low, place: (0, p + first))
    table = pl.BlockSpec((length, PAIR), lambda p, low, place: (0, 0))
    held = tuple(held or ())
    ways = len(do)

    def kernel(*refs):
        rest = refs[2 + ways :]
        attend_back_kernel(*refs[:2], refs[2 : 2 + ways], *rest[:8], *rest[8 + len(held) :])

    return pl.pallas_call(
        kernel,
        grid_spec=pltpu.PrefetchScalarGridSpec(
            num_scalar_prefetch=2,
            grid=(count,),
            in_specs=[
                *[pl.BlockSpec((length // ways, PAIR), lambda p, low, place: (0, p + first))] * ways,
                flat, flat, flat,
                pl.BlockSpec((1, 2, length), lambda p, low, place: (p + first, 0, 0)),
                table, table,
                pl.BlockSpec((1, length), lambda p, low, place: (0, 0)),
                table,
            ] + [pl.BlockSpec(memory_space=pl.ANY)] * len(held),
            out_specs=[
                pl.BlockSpec((3, length, PAIR), lambda p, low, place: (0, 0, p + first)),
                pl.BlockSpec((3, 1, PAIR), lambda p, low, place: (0, 0, p + first)),
            ],
            scratch_shapes=[pltpu.VMEM((2, length, PAIR), jnp.bfloat16)] * 4
            + [pltpu.VMEM((length, PAIR), jnp.bfloat16)]
            + [pltpu.VMEM((length, PAIR), jnp.float32)] * 2,
        ),
        out_shape=[
            jax.ShapeDtypeStruct((3, length, width), jnp.bfloat16),
            jax.ShapeDtypeStruct((3, 1, width), jnp.float32),
        ],
        input_output_aliases={10 + ways + i: i for i in range(len(held))},
        compiler_params=pltpu.CompilerParams(vmem_limit_bytes=48 * 2**20),
        name="attend_back",
    )(lows, places, *do, q, k, v, lse, cos_wide, sin_wide, starts[None, :], valid_wide, *held)


def gelu_and_slope(u):
    tanh_value = jnp.tanh(GELU_C * (u + 0.044715 * u * u * u))
    value = 0.5 * u * (1.0 + tanh_value)
    slope = 0.5 * (1.0 + tanh_value) + 0.5 * u * (1.0 - tanh_value * tanh_value) * GELU_C * (
        1.0 + 3.0 * 0.044715 * u * u
    )
    return (value, slope)


def contract_rows(left, right):
    return lax.dot_general(
        left, right, (((0,), (0,)), ((), ())), preferred_element_type=jnp.float32
    )


def contract_cols(left, right):
    return lax.dot_general(
        left, right, (((1,), (1,)), ((), ())), preferred_element_type=jnp.float32
    )


def shift(x, pairs):
    return lax.ppermute(x, "tensor", pairs)


class LineGather:
    def __init__(self, x):
        self.up, self.down = [x], [x]

    def step(self):
        n, k = lax.axis_size("tensor"), len(self.up)
        self.up.append(shift(self.up[-1], [(i, i + 1) for i in range(k - 1, n - 1)]))
        self.down.append(shift(self.down[-1], [(i, i - 1) for i in range(1, n - k + 1)]))

    def block(self, k):
        n, me = lax.axis_size("tensor"), lax.axis_index("tensor")
        return jnp.where(me >= k, self.up[k], self.down[n - k]) if k else self.up[0]


class RingScatter:
    def __init__(self, parts, rows):
        self.parts, self.rows, self.k, self.up, self.down = list(parts), rows, 0, None, None

    def next(self):
        place = self.k * self.rows
        for part in self.parts:
            if place < part.shape[0]:
                return part[place : place + self.rows]
            place -= part.shape[0]

    def step(self):
        n, mine = lax.axis_size("tensor"), self.next()
        if self.k:
            mine = (mine.astype(jnp.float32) + self.up.astype(jnp.float32)).astype(jnp.bfloat16)
        self.up = shift(mine, [(i, (i + 1) % n) for i in range(n)])
        self.k += 1

    def total(self):
        return self.next().astype(jnp.float32) + self.up.astype(jnp.float32)


class LineScatter:
    def __init__(self, parts):
        self.parts, self.k, self.up, self.down = parts, 1, None, None

    def step(self):
        n, k = lax.axis_size("tensor"), self.k
        mine_up, mine_down = self.parts[k], self.parts[n - k]
        if k > 1:
            mine_up = mine_up.astype(jnp.float32) + self.up.astype(jnp.float32)
            mine_down = mine_down.astype(jnp.float32) + self.down.astype(jnp.float32)
        self.up = shift(mine_up.astype(jnp.bfloat16), [(i, i + 1) for i in range(k)])
        self.down = shift(mine_down.astype(jnp.bfloat16), [(i, i - 1) for i in range(n - k, n)])
        self.k = k + 1

    def total(self):
        return sum(x.astype(jnp.float32) for x in (self.parts[0], self.up, self.down))


def together(*moves, after=()):
    state = [
        (m.up[-1], m.down[-1]) if isinstance(m, LineGather) else (m.parts, m.up, m.down)
        for m in moves
    ]
    state, after = lax.optimization_barrier((state, after))
    for m, kept in zip(moves, state):
        if isinstance(m, LineGather):
            m.up[-1], m.down[-1] = kept
        else:
            m.parts, m.up, m.down = kept
    return after


def blocks_of(whole, n):
    rows = whole.shape[0] // n
    return [whole[k * rows : (k + 1) * rows] for k in range(n)]


def scatter_low(part, axis, dim):
    return lax.psum_scatter(
        part.astype(jnp.bfloat16), axis, scatter_dimension=dim, tiled=True
    ).astype(jnp.float32)


def body(
    tokens,
    segments,
    norm_gain,
    norm_shift,
    qkv_weight,
    qkv_bias,
    dense_weight,
    up_weight,
    up_bias,
    down_weight,
    out_bias,
    cotangent,
):
    row_count, model_width = tokens.shape
    length = segments.shape[1]
    ways, copies = lax.axis_size("tensor"), lax.axis_size("dp")
    me = lax.axis_index("tensor")
    low = jnp.bfloat16
    resid = tokens.astype(jnp.float32)
    row_mean = jnp.mean(resid, axis=-1, keepdims=True)
    centered = resid - row_mean
    inverse = lax.rsqrt(jnp.mean(centered * centered, axis=-1, keepdims=True) + EPS)
    normed = centered * inverse
    normed_mine = (normed * norm_gain + norm_shift).astype(low)
    full_qkv = lax.all_gather(qkv_weight, "dp", axis=1, tiled=True)
    normed_mine, up_weight, down_weight, dense_weight = lax.optimization_barrier(
        (normed_mine, up_weight, down_weight, dense_weight)
    )
    full_up = lax.all_gather(up_weight, "dp", axis=0, tiled=True)
    full_down = lax.all_gather(down_weight, "dp", axis=1, tiled=True)
    full_dense = lax.all_gather(dense_weight, "dp", axis=1, tiled=True)
    around = [(i, (i + 1) % ways) for i in range(ways)]
    ring = [normed_mine, shift(normed_mine, around)]

    biases = jnp.concatenate([qkv_bias.reshape(-1), up_bias])
    biases = lax.all_gather(biases, "dp", axis=0).astype(jnp.float32)
    third = qkv_bias.shape[1]
    full_qbias = biases[:, : 3 * third].reshape(copies, 3, third)
    full_qbias = full_qbias.transpose(1, 0, 2).reshape(3, copies * third)
    full_ubias = biases[:, 3 * third :].reshape(-1)

    starts = segment_starts(segments)[0]
    cos_wide, sin_wide = rotary_wide(starts)
    valid_rows = (segments != 0).astype(jnp.float32).reshape(length, 1)
    valid_wide = jnp.broadcast_to(valid_rows, (length, PAIR))
    lows = starts[::BLOCK] // BLOCK
    chunk = jnp.arange(length // BLOCK, dtype=jnp.int32)
    per = row_count // BLOCK
    places = (me - 1 - chunk // per) % ways * per + chunk % per

    tables = (cos_wide, sin_wide, starts, valid_wide, lows, places)
    valid_mine = lax.dynamic_slice_in_dim(valid_rows, me * row_count, row_count, 0)
    cot_columns = jnp.sum(cotangent, axis=0, dtype=jnp.float32)
    resid_square = jnp.sum(valid_mine * resid * resid)
    fixed = lax.optimization_barrier
    ring[1], cot_mine, tables, full_qbias, full_ubias, cot_columns, resid_square = fixed(
        (ring[1], cotangent, tables, full_qbias, full_ubias, cot_columns, resid_square)
    )
    pairs = full_qkv.shape[2] // PAIR
    half = max(1, pairs // 2)
    projected, slopes, hidden_act, mlp_parts = ([None] * ways for _ in range(4))
    grad_context, grad_pre, pre_sums = ([None] * ways for _ in range(3))

    def turned(blocks):
        return [*blocks[1:], blocks[0]]

    def project(k):
        projected[k] = jnp.einsum(
            "td,cde->cte", ring[k], full_qkv, preferred_element_type=jnp.float32
        )

    def widen(k):
        pre = jnp.dot(ring[k], full_up, preferred_element_type=jnp.float32) + full_ubias
        value, slopes[k] = gelu_and_slope(pre)
        hidden_act[k] = value.astype(low)

    def narrow(k):
        mlp_parts[k] = jnp.dot(
            hidden_act[k], full_down, preferred_element_type=jnp.float32
        ).astype(low)

    def back(k):
        block = cot.block(k)
        grad_context[k] = contract_cols(block, full_dense).astype(low)
        grad_act = contract_cols(block, full_down)
        grad_pre[k] = (grad_act * slopes[k]).astype(low)
        pre_sums[k] = jnp.sum(grad_pre[k], axis=0, dtype=jnp.float32)

    for k in range(2, ways):
        coming = shift(ring[k - 1], around)
        if k == 2:
            project(0)
            project(1)
        if k == ways - 1:
            for j in range(ways - 1):
                if projected[j] is None:
                    project(j)
                widen(j)
        coming, ring, projected, slopes, hidden_act, cot_mine = fixed(
            (coming, ring, projected, slopes, hidden_act, cot_mine)
        )
        ring.append(coming)

    cot = LineGather(cot_mine)
    cot.step()
    project(ways - 1)
    widen(ways - 1)
    for k in range(ways):
        narrow(k)
    ring, projected, slopes, hidden_act, mlp_parts = together(
        cot, after=(ring, projected, slopes, hidden_act, mlp_parts)
    )

    mlp = LineScatter(mlp_parts)
    while len(cot.up) < ways - 1:
        cot.step()
        mlp.step()
    attended = attention_forward(turned(projected), full_qbias, tables, 0, pairs)
    query, keys, values, context_low, logsum = attended
    mix = lambda rows: jnp.dot(rows, full_dense, preferred_element_type=jnp.float32).astype(low)
    attn_parts = [mix(context_low[:row_count]), mix(context_low[row_count:])]
    ring, attended, attn_parts, slopes, hidden_act = together(
        cot, mlp, after=(ring, attended, attn_parts, slopes, hidden_act)
    )
    query, keys, values, context_low, logsum = attended

    cot.step()
    mlp.step()
    for k in [0, *range(2, ways - 1)]:
        back(k)
    acts = jnp.concatenate(turned(hidden_act), axis=0)
    grad_context, grad_pre, acts, slopes, pre_sums = together(
        cot, mlp, after=(grad_context, grad_pre, acts, slopes, pre_sums)
    )

    while mlp.k < ways:
        mlp.step()
    for k in sorted({1, ways - 1}):
        back(k)
    grad_full = jnp.concatenate(turned([cot.block(k) for k in range(ways)]), axis=0)
    grad_context, grad_pre, pre_sums, attn_parts, grad_full, acts = together(
        mlp, after=(grad_context, grad_pre, pre_sums, attn_parts, grad_full, acts)
    )

    attn = RingScatter(attn_parts, row_count)
    attn.step()
    grads = attention_backward(query, keys, values, turned(grad_context), logsum, tables, 0, half)
    grad_down = contract_rows(acts, grad_full).astype(low)
    normed_low = jnp.concatenate(turned(ring), axis=0)
    pre_full = jnp.concatenate(turned(grad_pre), axis=0)
    grads, grad_context, grad_down, grad_full, context_low, normed_low, pre_full, pre_sums = together(
        attn,
        mlp,
        after=(grads, grad_context, grad_down, grad_full, context_low, normed_low, pre_full, pre_sums),
    )
    part_down = scatter_low(grad_down, "dp", 1)

    while attn.k < ways - 2:
        attn.step()
    if pairs > half:
        grads = attention_backward(
            query, keys, values, turned(grad_context), logsum, tables, half, pairs - half, held=grads
        )
    grad_up = contract_rows(normed_low, pre_full).astype(low)
    grads, grad_up, pre_full, pre_sums, normed_low, grad_full, context_low = together(
        attn, mlp, after=(grads, grad_up, pre_full, pre_sums, normed_low, grad_full, context_low)
    )
    part_up = scatter_low(grad_up, "dp", 0)
    grad_proj, grad_qbias = grads[0], grads[1][:, 0, :]

    def return_normed(low_block, high_block):
        rows = slice(low_block * row_count, high_block * row_count)
        part = contract_cols(pre_full[rows], full_up) + jnp.einsum(
            "cte,cde->td", grad_proj[:, rows], full_qkv, preferred_element_type=jnp.float32
        )
        return part.astype(low)

    attn.step()
    grad_qkv = jnp.einsum(
        "td,cte->cde", normed_low, grad_proj, preferred_element_type=jnp.float32
    ).astype(low)
    grad_parts = [return_normed(0, ways // 2)]
    grad_parts, grad_qkv, pre_full, pre_sums, grad_proj, grad_full, context_low, part_down = together(
        attn,
        mlp,
        after=(grad_parts, grad_qkv, pre_full, pre_sums, grad_proj, grad_full, context_low, part_down),
    )
    part_qkv = scatter_low(grad_qkv, "dp", 1)

    last = RingScatter(grad_parts, row_count)
    last.step()
    grad_dense = contract_rows(context_low, grad_full).astype(low)
    last.parts.append(return_normed(ways // 2, ways))
    grad_dense, pre_sums, part_up = together(last, attn, mlp, after=(grad_dense, pre_sums, part_up))
    part_dense = scatter_low(grad_dense, "dp", 1)
    while last.k < ways - 2:
        last.step()
    attn_mine, mlp_mine = attn.total(), mlp.total()
    grad_ubias = sum(pre_sums)
    attn_mine, mlp_mine, grad_ubias, part_qkv = together(
        last, after=(attn_mine, mlp_mine, grad_ubias, part_qkv)
    )
    last.step()
    output = (resid + attn_mine + mlp_mine + out_bias).astype(low)
    attn_square = jnp.sum(valid_mine * attn_mine * attn_mine)
    mlp_square = jnp.sum(valid_mine * mlp_mine * mlp_mine)
    output, attn_square, mlp_square, part_dense = together(
        last, after=(output, attn_square, mlp_square, part_dense)
    )
    grad_mine = last.total()
    scaled = grad_mine * norm_gain
    grad_tokens = (
        cotangent.astype(jnp.float32)
        + inverse
        * (
            scaled
            - jnp.mean(scaled, axis=-1, keepdims=True)
            - normed * jnp.mean(scaled * normed, axis=-1, keepdims=True)
        )
    ).astype(low)

    totals = jnp.stack(
        [resid_square, attn_square, mlp_square, jnp.sum(valid_mine) * model_width]
    )
    columns = jnp.stack(
        [
            jnp.sum(grad_mine * normed, axis=0),
            jnp.sum(grad_mine, axis=0),
            cot_columns,
        ]
    )
    peers = copies * ways
    share = model_width // peers
    columns = columns.reshape(3, peers, share).transpose(1, 0, 2).reshape(peers, 3 * share)
    own_bias = jnp.concatenate(
        [
            grad_qbias.reshape(3, copies, third).transpose(1, 0, 2).reshape(copies, 3 * third),
            grad_ubias.reshape(copies, -1),
        ],
        axis=1,
    )
    same = (jnp.arange(ways) == me).astype(jnp.float32)[None, :, None]
    own_bias = (own_bias[:, None, :] * same).reshape(peers, -1)
    small = jnp.concatenate(
        [columns, own_bias, jnp.broadcast_to(totals, (peers, 4))], axis=1
    )
    small = jnp.sum(lax.all_to_all(small, ("dp", "tensor"), 0, 0, tiled=True), axis=0)
    part_gain, part_shift, part_obias = small[: 3 * share].reshape(3, share)
    part_qbias = small[3 * share : 3 * share + 3 * third].reshape(3, third)
    part_ubias = small[3 * share + 3 * third : -4]
    root_squares = jnp.sqrt(small[-4:-1] / small[-1])
    return (
        output,
        grad_tokens,
        part_gain,
        part_shift,
        part_qkv,
        part_qbias,
        part_dense,
        part_up,
        part_ubias,
        part_down,
        part_obias,
        root_squares,
    )


def solution(mesh):
    placed = (
        P(("dp", "tensor"), None),
        P("dp", None),
        P(),
        P(),
        P(None, "dp", "tensor"),
        P(None, ("tensor", "dp")),
        P("tensor", "dp"),
        P("dp", "tensor"),
        P(("tensor", "dp")),
        P("tensor", "dp"),
        P(),
        P(("dp", "tensor"), None),
    )
    return jax.shard_map(
        body,
        mesh=mesh,
        in_specs=placed,
        out_specs=(
            P(("dp", "tensor"), None),
            P(("dp", "tensor"), None),
            P(("dp", "tensor")),
            P(("dp", "tensor")),
            P(None, "dp", "tensor"),
            P(None, ("tensor", "dp")),
            P("tensor", "dp"),
            P("dp", "tensor"),
            P(("tensor", "dp")),
            P("tensor", "dp"),
            P(("dp", "tensor")),
            P(),
        ),
        check_vma=False,
    )
```

```python
import functools
import math

import jax
import jax.numpy as jnp
from jax import lax
from jax.experimental import pallas as pl
from jax.experimental.pallas import tpu as pltpu
from jax.sharding import PartitionSpec as P

HEAD_DIM = 64
ROT = 32
PAIR = 2 * HEAD_DIM
BLOCK = 256
MOST = 5

EPS = 1e-05
GELU_C = math.sqrt(2.0 / math.pi)


def segment_starts(segs):
    return jnp.sum((segs[:, None, :] < segs[:, :, None]).astype(jnp.int32), axis=-1)


def rotary_wide(starts):
    length = starts.shape[0]
    half_rot = ROT // 2
    frequency = jnp.exp(-math.log(10000.0) * (2.0 * jnp.arange(half_rot, dtype=jnp.float32) / ROT))
    position = jnp.arange(length, dtype=jnp.int32) - starts
    angles = position.astype(jnp.float32)[:, None] * frequency
    cosines, sines = jnp.cos(angles), jnp.sin(angles)
    ones = jnp.ones((length, HEAD_DIM - ROT), jnp.float32)
    cos_head = jnp.concatenate([cosines, cosines, ones], axis=-1)
    sin_head = jnp.concatenate([-sines, sines, 0.0 * ones], axis=-1)
    return (jnp.concatenate([cos_head, cos_head], -1), jnp.concatenate([sin_head, sin_head], -1))


def turn(x, cos_wide, sin_wide):
    lane = lax.broadcasted_iota(jnp.int32, x.shape, 1) % HEAD_DIM
    half_rot = ROT // 2
    partner = jnp.where(
        lane < half_rot, pltpu.roll(x, PAIR - half_rot, 1), pltpu.roll(x, half_rot, 1)
    )
    return x * cos_wide + partner * sin_wide


def first_half(shape):
    return lax.broadcasted_iota(jnp.int32, shape, len(shape) - 1) < HEAD_DIM


def halves(x):
    front = first_half(x.shape)
    zero = jnp.zeros_like(x)
    return (jnp.where(front, x, zero), jnp.where(front, zero, x))


def nt(left, right):
    return lax.dot_general(
        left, right, (((1,), (1,)), ((), ())), preferred_element_type=jnp.float32
    )


def nn(left, right):
    return lax.dot_general(
        left, right, (((1,), (0,)), ((), ())), preferred_element_type=jnp.float32
    )


def tn(left, right):
    return lax.dot_general(
        left, right, (((0,), (0,)), ((), ())), preferred_element_type=jnp.float32
    )


def attend_kernel(
    low_ref, place_ref, parts, bias_ref, cos_ref, sin_ref, start_ref, valid_ref,
    q_ref, k_ref, v_ref, ctx_ref, lse_ref, km, vm,
):
    length = q_ref.shape[0]
    blocks = length // BLOCK
    scale = 1.0 / math.sqrt(HEAD_DIM)

    per = length // len(parts) // BLOCK

    def project(i, slot):
        rows = pl.ds(pl.multiple_of(place_ref[slot * per + i] * BLOCK, BLOCK), BLOCK)
        here = pl.ds(i * BLOCK, BLOCK)
        part = parts[slot]
        cw, sw = cos_ref[rows, :], sin_ref[rows, :]
        x = part[here, :] + bias_ref[...]
        q = turn(x[:, :PAIR], cw, sw).astype(jnp.bfloat16)
        q_ref[rows, :] = q * jnp.bfloat16(scale)
        k = turn(x[:, PAIR : 2 * PAIR], cw, sw).astype(jnp.bfloat16)
        k_ref[rows, :] = k
        v = x[:, 2 * PAIR :].astype(jnp.bfloat16)
        v_ref[rows, :] = v
        km[0, rows, :], km[1, rows, :] = halves(k)
        vm[0, rows, :], vm[1, rows, :] = halves(v)

    for slot in range(len(parts)):
        for i in range(per):
            project(i, slot)

    def query_block(i, count):
        rows = pl.ds(pl.multiple_of(i * BLOCK, BLOCK), BLOCK)
        base = pl.multiple_of((i + 1 - count) * BLOCK, BLOCK)
        cols = pl.ds(base, count * BLOCK)
        shape = (BLOCK, count * BLOCK)
        q = q_ref[rows, :]
        start = start_ref[rows, :][:, :1] - base
        kpos = lax.broadcasted_iota(jnp.int32, shape, 1)
        qpos = lax.broadcasted_iota(jnp.int32, shape, 0) + (count - 1) * BLOCK
        allowed = (kpos >= start) & (kpos <= qpos)
        there = pl.ds(pl.multiple_of(place_ref[i] * BLOCK, BLOCK), BLOCK)
        acc = jnp.zeros((BLOCK, PAIR), jnp.float32)
        tops, sums = [], []
        for h in range(2):
            s = jnp.where(allowed, nt(q, km[h, cols, :]), -jnp.inf)
            top = jnp.max(s, axis=-1, keepdims=True)
            e = jnp.exp(s - top)
            tops.append(top)
            sums.append(jnp.sum(e, axis=-1, keepdims=True))
            acc = acc + nn(e.astype(jnp.bfloat16), vm[h, cols, :])
        front = first_half((BLOCK, PAIR))
        out = acc / jnp.where(front, sums[0], sums[1])
        ctx_ref[there, :] = (out * valid_ref[rows, :]).astype(jnp.bfloat16)
        lse = jnp.where(front, tops[0] + jnp.log(sums[0]), tops[1] + jnp.log(sums[1]))
        lse_t = lse.T
        lse_ref[0, 0:1, rows] = lse_t[0:1, :]
        lse_ref[0, 1:2, rows] = lse_t[HEAD_DIM : HEAD_DIM + 1, :]

    def step(i, _):
        for count in range(1, MOST + 1):
            pl.when(i + 1 - low_ref[i] == count)(functools.partial(query_block, i, count))
        return 0

    lax.fori_loop(0, blocks, step, 0)


def attention_forward(projected, bias, tables, first, count, held=None):
    cos_wide, sin_wide, starts, valid_wide, lows, places = tables
    width = projected[0].shape[1] // 3
    length = starts.shape[0]
    blocks = length // BLOCK
    ways = len(projected)
    start_wide = jnp.broadcast_to(starts[:, None], (length, PAIR))
    part = pl.BlockSpec((length // ways, 3 * PAIR), lambda p, low, place: (0, p + first))
    table = pl.BlockSpec((length, PAIR), lambda p, low, place: (0, 0))
    flat = pl.BlockSpec((length, PAIR), lambda p, low, place: (0, p + first))
    flat_shape = jax.ShapeDtypeStruct((length, width), jnp.bfloat16)
    held = tuple(held or ())

    def kernel(*refs):
        rest = refs[2 + ways :]
        attend_kernel(*refs[:2], refs[2 : 2 + ways], *rest[:5], *rest[5 + len(held) :])

    return pl.pallas_call(
        kernel,
        grid_spec=pltpu.PrefetchScalarGridSpec(
            num_scalar_prefetch=2,
            grid=(count,),
            in_specs=[
                *[part] * ways,
                pl.BlockSpec((1, 3 * PAIR), lambda p, low, place: (0, p + first)),
                table, table, table, table,
            ] + [pl.BlockSpec(memory_space=pl.ANY)] * len(held),
            out_specs=[flat, flat, flat, flat,
                       pl.BlockSpec((1, 2, length), lambda p, low, place: (p + first, 0, 0))],
            scratch_shapes=[
                pltpu.VMEM((2, length, PAIR), jnp.bfloat16),
                pltpu.VMEM((2, length, PAIR), jnp.bfloat16),
            ],
        ),
        out_shape=[flat_shape] * 4
        + [jax.ShapeDtypeStruct((width // PAIR, 2, length), jnp.float32)],
        input_output_aliases={7 + ways + i: i for i in range(len(held))},
        compiler_params=pltpu.CompilerParams(vmem_limit_bytes=48 * 2**20),
        name="attend",
    )(lows, places, *projected, bias[None, :], cos_wide, sin_wide,
      start_wide, valid_wide, *held)


def attend_back_kernel(
    low_ref, place_ref, dos, q_ref, k_ref, v_ref, lse_ref, cos_ref, sin_ref, start_ref, valid_ref,
    grad_ref, sums_ref, qm, km, vm, dom, do_scr, dk_acc, dv_acc,
):
    length = q_ref.shape[0]
    blocks = length // BLOCK
    scale = 1.0 / math.sqrt(HEAD_DIM)

    def split(i, _):
        rows = pl.ds(pl.multiple_of(i * BLOCK, BLOCK), BLOCK)
        qm[0, rows, :], qm[1, rows, :] = halves(q_ref[rows, :])
        km[0, rows, :], km[1, rows, :] = halves(k_ref[rows, :])
        vm[0, rows, :], vm[1, rows, :] = halves(v_ref[rows, :])
        dk_acc[rows, :] = jnp.zeros((BLOCK, PAIR), jnp.float32)
        dv_acc[rows, :] = jnp.zeros((BLOCK, PAIR), jnp.float32)
        return 0

    lax.fori_loop(0, blocks, split, 0)

    per = length // len(dos) // BLOCK
    for slot in range(len(dos)):
        for i in range(per):
            rows = pl.ds(pl.multiple_of(place_ref[slot * per + i] * BLOCK, BLOCK), BLOCK)
            do = dos[slot][i * BLOCK : (i + 1) * BLOCK, :].astype(jnp.float32)
            do = (do * valid_ref[rows, :]).astype(jnp.bfloat16)
            do_scr[rows, :] = do
            dom[0, rows, :], dom[1, rows, :] = halves(do)

    def query_block(i, count):
        rows = pl.ds(pl.multiple_of(i * BLOCK, BLOCK), BLOCK)
        base = pl.multiple_of((i + 1 - count) * BLOCK, BLOCK)
        cols = pl.ds(base, count * BLOCK)
        shape = (count * BLOCK, BLOCK)
        q = q_ref[rows, :]
        do = do_scr[rows, :]
        start = start_ref[:, rows] - base
        kpos = lax.broadcasted_iota(jnp.int32, shape, 0)
        qpos = lax.broadcasted_iota(jnp.int32, shape, 1) + (count - 1) * BLOCK
        allowed = (kpos >= start) & (kpos <= qpos)
        dk = dk_acc[cols, :]
        dv = dv_acc[cols, :]
        dq = jnp.zeros((BLOCK, PAIR), jnp.float32)
        for h in range(2):
            s = nt(km[h, cols, :], q)
            p = jnp.where(allowed, jnp.exp(s - lse_ref[0, h : h + 1, rows]), 0.0)
            dp = nt(vm[h, cols, :], do)
            delta = jnp.sum(p * dp, axis=0, keepdims=True)
            dv = dv + nn(p.astype(jnp.bfloat16), dom[h, rows, :])
            ds = (p * (dp - delta)).astype(jnp.bfloat16)
            dk = dk + nn(ds, qm[h, rows, :])
            dq = dq + tn(ds, km[h, cols, :])
        dk_acc[cols, :] = dk
        dv_acc[cols, :] = dv
        dq = turn(dq * scale, cos_ref[rows, :], -sin_ref[rows, :]).astype(jnp.bfloat16)
        there = pl.ds(pl.multiple_of(place_ref[i] * BLOCK, BLOCK), BLOCK)
        grad_ref[there, :PAIR] = dq
        sums_ref[0] += jnp.sum(dq.astype(jnp.float32), axis=0, keepdims=True)

    none = jnp.zeros((1, PAIR), jnp.float32)
    sums_ref[0] = none

    def step(i, _):
        for count in range(1, MOST + 1):
            pl.when(i + 1 - low_ref[i] == count)(functools.partial(query_block, i, count))
        return 0

    lax.fori_loop(0, blocks, step, 0)

    def finish(i, totals):
        rows = pl.ds(pl.multiple_of(i * BLOCK, BLOCK), BLOCK)
        dk = turn(dk_acc[rows, :], cos_ref[rows, :], -sin_ref[rows, :]).astype(jnp.bfloat16)
        dv = dv_acc[rows, :].astype(jnp.bfloat16)
        there = pl.ds(pl.multiple_of(place_ref[i] * BLOCK, BLOCK), BLOCK)
        grad_ref[there, PAIR : 2 * PAIR] = dk
        grad_ref[there, 2 * PAIR :] = dv
        return (
            totals[0] + jnp.sum(dk.astype(jnp.float32), axis=0, keepdims=True),
            totals[1] + jnp.sum(dv.astype(jnp.float32), axis=0, keepdims=True),
        )

    sums_ref[1], sums_ref[2] = lax.fori_loop(0, blocks, finish, (none, none))


def attention_backward(q, k, v, do, lse, tables, first, count, held=None):
    cos_wide, sin_wide, starts, valid_wide, lows, places = tables
    length, width = q.shape
    blocks = length // BLOCK
    flat = pl.BlockSpec((length, PAIR), lambda p, low, place: (0, p + first))
    table = pl.BlockSpec((length, PAIR), lambda p, low, place: (0, 0))
    held = tuple(held or ())
    ways = len(do)

    def kernel(*refs):
        rest = refs[2 + ways :]
        attend_back_kernel(*refs[:2], refs[2 : 2 + ways], *rest[:8], *rest[8 + len(held) :])

    return pl.pallas_call(
        kernel,
        grid_spec=pltpu.PrefetchScalarGridSpec(
            num_scalar_prefetch=2,
            grid=(count,),
            in_specs=[
                *[pl.BlockSpec((length // ways, PAIR), lambda p, low, place: (0, p + first))] * ways,
                flat, flat, flat,
                pl.BlockSpec((1, 2, length), lambda p, low, place: (p + first, 0, 0)),
                table, table,
                pl.BlockSpec((1, length), lambda p, low, place: (0, 0)),
                table,
            ] + [pl.BlockSpec(memory_space=pl.ANY)] * len(held),
            out_specs=[
                pl.BlockSpec((length, 3 * PAIR), lambda p, low, place: (0, p + first)),
                pl.BlockSpec((3, 1, PAIR), lambda p, low, place: (0, 0, p + first)),
            ],
            scratch_shapes=[pltpu.VMEM((2, length, PAIR), jnp.bfloat16)] * 4
            + [pltpu.VMEM((length, PAIR), jnp.bfloat16)]
            + [pltpu.VMEM((length, PAIR), jnp.float32)] * 2,
        ),
        out_shape=[
            jax.ShapeDtypeStruct((length, 3 * width), jnp.bfloat16),
            jax.ShapeDtypeStruct((3, 1, width), jnp.float32),
        ],
        input_output_aliases={10 + ways + i: i for i in range(len(held))},
        compiler_params=pltpu.CompilerParams(vmem_limit_bytes=48 * 2**20),
        name="attend_back",
    )(lows, places, *do, q, k, v, lse, cos_wide, sin_wide, starts[None, :], valid_wide, *held)


def hidden_back_kernel(block_ref, weight_ref, slope_ref, *refs):
    grad = nt(block_ref[...], weight_ref[...])
    refs[-1][...] = (grad * slope_ref[...]).astype(jnp.bfloat16)


def hidden_back(block, weight, slope, place, ways, held=None):
    rows, model_width = block.shape
    hidden = weight.shape[0]
    tile = min(512, hidden)
    held = () if held is None else (held,)
    return pl.pallas_call(
        hidden_back_kernel,
        grid=(hidden // tile,),
        in_specs=[
            pl.BlockSpec((rows, model_width), lambda j: (0, 0)),
            pl.BlockSpec((tile, model_width), lambda j: (j, 0)),
            pl.BlockSpec((rows, tile), lambda j: (0, j)),
        ]
        + [pl.BlockSpec(memory_space=pl.ANY)] * len(held),
        out_specs=pl.BlockSpec((rows, tile), lambda j: (place, j)),
        out_shape=jax.ShapeDtypeStruct((ways * rows, hidden), jnp.bfloat16),
        input_output_aliases={3: 0} if held else {},
        compiler_params=pltpu.CompilerParams(vmem_limit_bytes=40 * 2**20),
        cost_estimate=pl.CostEstimate(
            flops=2 * rows * model_width * hidden,
            bytes_accessed=2 * hidden * model_width,
            transcendentals=0,
        ),
        name="hidden_back",
    )(block, weight, slope, *held)


def gelu_and_slope(u):
    tanh_value = jnp.tanh(GELU_C * (u + 0.044715 * u * u * u))
    value = 0.5 * u * (1.0 + tanh_value)
    slope = 0.5 * (1.0 + tanh_value) + 0.5 * u * (1.0 - tanh_value * tanh_value) * GELU_C * (
        1.0 + 3.0 * 0.044715 * u * u
    )
    return (value, slope)


def contract_rows(left, right):
    return lax.dot_general(
        left, right, (((0,), (0,)), ((), ())), preferred_element_type=jnp.float32
    )


def contract_cols(left, right):
    return lax.dot_general(
        left, right, (((1,), (1,)), ((), ())), preferred_element_type=jnp.float32
    )


def shift(x, pairs):
    return lax.ppermute(x, "tensor", pairs)


class LineGather:
    def __init__(self, x):
        self.up, self.down = [x], [x]

    def step(self):
        n, k = lax.axis_size("tensor"), len(self.up)
        self.up.append(shift(self.up[-1], [(i, i + 1) for i in range(k - 1, n - 1)]))
        self.down.append(shift(self.down[-1], [(i, i - 1) for i in range(1, n - k + 1)]))

    def block(self, k):
        n, me = lax.axis_size("tensor"), lax.axis_index("tensor")
        return jnp.where(me >= k, self.up[k], self.down[n - k]) if k else self.up[0]


class RingScatter:
    def __init__(self, parts, rows):
        self.parts, self.rows, self.k, self.up, self.down = list(parts), rows, 0, None, None

    def next(self):
        place = self.k * self.rows
        for part in self.parts:
            if place < part.shape[0]:
                return part[place : place + self.rows]
            place -= part.shape[0]

    def step(self):
        n, mine = lax.axis_size("tensor"), self.next()
        if self.k:
            mine = (mine.astype(jnp.float32) + self.up.astype(jnp.float32)).astype(jnp.bfloat16)
        self.up = shift(mine, [(i, (i + 1) % n) for i in range(n)])
        self.k += 1

    def total(self):
        return self.next().astype(jnp.float32) + self.up.astype(jnp.float32)


class LineScatter:
    def __init__(self, parts):
        self.parts, self.k, self.up, self.down = parts, 1, None, None

    def step(self):
        n, k = lax.axis_size("tensor"), self.k
        mine_up, mine_down = self.parts[k], self.parts[n - k]
        if k > 1:
            mine_up = mine_up.astype(jnp.float32) + self.up.astype(jnp.float32)
            mine_down = mine_down.astype(jnp.float32) + self.down.astype(jnp.float32)
        self.up = shift(mine_up.astype(jnp.bfloat16), [(i, i + 1) for i in range(k)])
        self.down = shift(mine_down.astype(jnp.bfloat16), [(i, i - 1) for i in range(n - k, n)])
        self.k = k + 1

    def total(self):
        return sum(x.astype(jnp.float32) for x in (self.parts[0], self.up, self.down))


def together(*moves, after=()):
    state = [
        (m.up[-1], m.down[-1]) if isinstance(m, LineGather) else (m.parts, m.up, m.down)
        for m in moves
    ]
    state, after = lax.optimization_barrier((state, after))
    for m, kept in zip(moves, state):
        if isinstance(m, LineGather):
            m.up[-1], m.down[-1] = kept
        else:
            m.parts, m.up, m.down = kept
    return after


def blocks_of(whole, n):
    rows = whole.shape[0] // n
    return [whole[k * rows : (k + 1) * rows] for k in range(n)]


def scatter_low(part, axis, dim):
    return lax.psum_scatter(
        part.astype(jnp.bfloat16), axis, scatter_dimension=dim, tiled=True
    ).astype(jnp.float32)


def body(
    tokens,
    segments,
    norm_gain,
    norm_shift,
    qkv_weight,
    qkv_bias,
    dense_weight,
    up_weight,
    up_bias,
    down_weight,
    out_bias,
    cotangent,
):
    row_count, model_width = tokens.shape
    length = segments.shape[1]
    ways, copies = lax.axis_size("tensor"), lax.axis_size("dp")
    me = lax.axis_index("tensor")
    low = jnp.bfloat16
    resid = tokens.astype(jnp.float32)
    row_mean = jnp.mean(resid, axis=-1, keepdims=True)
    centered = resid - row_mean
    inverse = lax.rsqrt(jnp.mean(centered * centered, axis=-1, keepdims=True) + EPS)
    normed = centered * inverse
    normed_mine = (normed * norm_gain + norm_shift).astype(low)
    full_qkv = lax.all_gather(qkv_weight, "dp", axis=1, tiled=True)
    normed_mine, up_weight, down_weight, dense_weight = lax.optimization_barrier(
        (normed_mine, up_weight, down_weight, dense_weight)
    )
    full_up = lax.all_gather(up_weight, "dp", axis=0, tiled=True)
    full_down = lax.all_gather(down_weight, "dp", axis=1, tiled=True)
    full_dense = lax.all_gather(dense_weight, "dp", axis=1, tiled=True)
    around = [(i, (i + 1) % ways) for i in range(ways)]
    ring = [normed_mine, shift(normed_mine, around)]

    biases = jnp.concatenate([qkv_bias.reshape(-1), up_bias])
    biases = lax.all_gather(biases, "dp", axis=0).astype(jnp.float32)
    third = qkv_bias.shape[1]
    full_qbias = biases[:, : 3 * third].reshape(copies, 3, third)
    full_qbias = full_qbias.transpose(1, 0, 2).reshape(3, -1, PAIR).transpose(1, 0, 2).reshape(-1)
    full_ubias = biases[:, 3 * third :].reshape(-1)

    starts = segment_starts(segments)[0]
    cos_wide, sin_wide = rotary_wide(starts)
    valid_rows = (segments != 0).astype(jnp.float32).reshape(length, 1)
    valid_wide = jnp.broadcast_to(valid_rows, (length, PAIR))
    lows = starts[::BLOCK] // BLOCK
    chunk = jnp.arange(length // BLOCK, dtype=jnp.int32)
    per = row_count // BLOCK
    places = (me - 1 - chunk // per) % ways * per + chunk % per

    tables = (cos_wide, sin_wide, starts, valid_wide, lows, places)
    valid_mine = lax.dynamic_slice_in_dim(valid_rows, me * row_count, row_count, 0)
    cot_columns = jnp.sum(cotangent, axis=0, dtype=jnp.float32)
    resid_square = jnp.sum(valid_mine * resid * resid)
    fixed = lax.optimization_barrier
    ring[1], cot_mine, tables, full_qbias, full_ubias, cot_columns, resid_square = fixed(
        (ring[1], cotangent, tables, full_qbias, full_ubias, cot_columns, resid_square)
    )
    pairs = qkv_weight.shape[2] // PAIR
    sorted_qkv = full_qkv.reshape(3, model_width, pairs, PAIR).transpose(1, 2, 0, 3)
    sorted_qkv = sorted_qkv.reshape(model_width, 3 * pairs * PAIR)
    half = max(1, pairs // 2)
    projected, slopes, hidden_act, mlp_parts = ([None] * ways for _ in range(4))
    grad_context, grad_pre = [None] * ways, [None]

    def turned(blocks):
        return [*blocks[1:], blocks[0]]

    def project(k):
        projected[k] = jnp.dot(ring[k], sorted_qkv, preferred_element_type=jnp.float32)

    def widen(k):
        pre = jnp.dot(ring[k], full_up, preferred_element_type=jnp.float32) + full_ubias
        value, slopes[k] = gelu_and_slope(pre)
        hidden_act[k] = value.astype(low)

    def narrow(k):
        mlp_parts[k] = jnp.dot(
            hidden_act[k], full_down, preferred_element_type=jnp.float32
        ).astype(low)

    def back(k):
        block = cot.block(k)
        grad_context[k] = contract_cols(block, full_dense).astype(low)
        grad_pre[0] = hidden_back(
            block, full_down, slopes[k], (k - 1) % ways, ways, held=grad_pre[0]
        )

    for k in range(2, ways):
        coming = shift(ring[k - 1], around)
        if k == 2:
            project(0)
            project(1)
        if k == ways - 1:
            for j in range(ways - 1):
                if projected[j] is None:
                    project(j)
                widen(j)
        coming, ring, projected, slopes, hidden_act, cot_mine = fixed(
            (coming, ring, projected, slopes, hidden_act, cot_mine)
        )
        ring.append(coming)

    cot = LineGather(cot_mine)
    cot.step()
    project(ways - 1)
    widen(ways - 1)
    for k in range(ways):
        narrow(k)
    ring, projected, slopes, hidden_act, mlp_parts = together(
        cot, after=(ring, projected, slopes, hidden_act, mlp_parts)
    )

    mlp = LineScatter(mlp_parts)
    while len(cot.up) < ways - 1:
        cot.step()
        mlp.step()
    attended = attention_forward(turned(projected), full_qbias, tables, 0, pairs)
    ring, attended, slopes, hidden_act, sorted_qkv = together(
        cot, mlp, after=(ring, attended, slopes, hidden_act, sorted_qkv)
    )
    query, keys, values, context_low, logsum = attended

    cot.step()
    mlp.step()
    for k in [0, *range(2, ways - 1)]:
        back(k)
    acts = jnp.concatenate(turned(hidden_act), axis=0)
    attn_part = jnp.dot(context_low, full_dense, preferred_element_type=jnp.float32).astype(low)
    grad_context, grad_pre, acts, slopes, attn_part = together(
        cot, mlp, after=(grad_context, grad_pre, acts, slopes, attn_part)
    )

    while mlp.k < ways:
        mlp.step()
    for k in sorted({1, ways - 1}):
        back(k)
    grad_full = jnp.concatenate(turned([cot.block(k) for k in range(ways)]), axis=0)
    grad_context, grad_pre, attn_part, grad_full, acts = together(
        mlp, after=(grad_context, grad_pre, attn_part, grad_full, acts)
    )
    [pre_full] = grad_pre

    attn = RingScatter([attn_part], row_count)
    attn.step()
    grads = attention_backward(query, keys, values, turned(grad_context), logsum, tables, 0, half)
    grad_down = contract_rows(acts, grad_full).astype(low)
    normed_low = jnp.concatenate(turned(ring), axis=0)
    grads, grad_context, grad_full, context_low, grad_down, pre_full, normed_low = together(
        attn,
        mlp,
        after=(grads, grad_context, grad_full, context_low, grad_down, pre_full, normed_low),
    )
    part_down = scatter_low(grad_down, "dp", 1)

    while attn.k < ways - 2:
        attn.step()
    if pairs > half:
        grads = attention_backward(
            query, keys, values, turned(grad_context), logsum, tables, half, pairs - half, held=grads
        )
    grad_up = contract_rows(normed_low, pre_full).astype(low)
    grads, grad_up, pre_full, normed_low, grad_full, context_low = together(
        attn, mlp, after=(grads, grad_up, pre_full, normed_low, grad_full, context_low)
    )
    part_up = scatter_low(grad_up, "dp", 0)
    grad_proj, grad_qbias = grads[0], grads[1][:, 0, :]

    def return_normed(low_block, high_block):
        rows = slice(low_block * row_count, high_block * row_count)
        part = contract_cols(pre_full[rows], full_up) + contract_cols(grad_proj[rows], sorted_qkv)
        return part.astype(low)

    attn.step()
    grad_qkv = contract_rows(normed_low, grad_proj).astype(low)
    grad_parts = [return_normed(0, ways // 2)]
    grad_parts, grad_qkv, pre_full, grad_proj, grad_full, context_low, part_down = together(
        attn,
        mlp,
        after=(grad_parts, grad_qkv, pre_full, grad_proj, grad_full, context_low, part_down),
    )
    part_qkv = scatter_low(grad_qkv, "dp", 0).reshape(-1, pairs, 3, PAIR)
    part_qkv = part_qkv.transpose(2, 0, 1, 3).reshape(3, -1, pairs * PAIR)

    last = RingScatter(grad_parts, row_count)
    last.step()
    last.parts.append(return_normed(ways // 2, ways))
    grad_dense = contract_rows(context_low, grad_full).astype(low)
    grad_dense, pre_full, part_up = together(last, attn, mlp, after=(grad_dense, pre_full, part_up))
    part_dense = scatter_low(grad_dense, "dp", 1)
    while last.k < ways - 2:
        last.step()
    grad_ubias = jnp.sum(pre_full, axis=0, dtype=jnp.float32)
    attn_mine, mlp_mine = attn.total(), mlp.total()
    attn_mine, mlp_mine, grad_ubias, part_qkv = together(
        last, after=(attn_mine, mlp_mine, grad_ubias, part_qkv)
    )
    last.step()
    output = (resid + attn_mine + mlp_mine + out_bias).astype(low)
    attn_square = jnp.sum(valid_mine * attn_mine * attn_mine)
    mlp_square = jnp.sum(valid_mine * mlp_mine * mlp_mine)
    output, attn_square, mlp_square, part_dense = together(
        last, after=(output, attn_square, mlp_square, part_dense)
    )
    grad_mine = last.total()
    scaled = grad_mine * norm_gain
    grad_tokens = (
        cotangent.astype(jnp.float32)
        + inverse
        * (
            scaled
            - jnp.mean(scaled, axis=-1, keepdims=True)
            - normed * jnp.mean(scaled * normed, axis=-1, keepdims=True)
        )
    ).astype(low)

    totals = jnp.stack(
        [resid_square, attn_square, mlp_square, jnp.sum(valid_mine) * model_width]
    )
    columns = jnp.stack(
        [
            jnp.sum(grad_mine * normed, axis=0),
            jnp.sum(grad_mine, axis=0),
            cot_columns,
        ]
    )
    peers = copies * ways
    share = model_width // peers
    columns = columns.reshape(3, peers, share).transpose(1, 0, 2).reshape(peers, 3 * share)
    own_bias = jnp.concatenate(
        [
            grad_qbias.reshape(3, copies, third).transpose(1, 0, 2).reshape(copies, 3 * third),
            grad_ubias.reshape(copies, -1),
        ],
        axis=1,
    )
    same = (jnp.arange(ways) == me).astype(jnp.float32)[None, :, None]
    own_bias = (own_bias[:, None, :] * same).reshape(peers, -1)
    small = jnp.concatenate(
        [columns, own_bias, jnp.broadcast_to(totals, (peers, 4))], axis=1
    )
    small = jnp.sum(lax.all_to_all(small, ("dp", "tensor"), 0, 0, tiled=True), axis=0)
    part_gain, part_shift, part_obias = small[: 3 * share].reshape(3, share)
    part_qbias = small[3 * share : 3 * share + 3 * third].reshape(3, third)
    part_ubias = small[3 * share + 3 * third : -4]
    root_squares = jnp.sqrt(small[-4:-1] / small[-1])
    return (
        output,
        grad_tokens,
        part_gain,
        part_shift,
        part_qkv,
        part_qbias,
        part_dense,
        part_up,
        part_ubias,
        part_down,
        part_obias,
        root_squares,
    )


def solution(mesh):
    placed = (
        P(("dp", "tensor"), None),
        P("dp", None),
        P(),
        P(),
        P(None, "dp", "tensor"),
        P(None, ("tensor", "dp")),
        P("tensor", "dp"),
        P("dp", "tensor"),
        P(("tensor", "dp")),
        P("tensor", "dp"),
        P(),
        P(("dp", "tensor"), None),
    )
    return jax.shard_map(
        body,
        mesh=mesh,
        in_specs=placed,
        out_specs=(
            P(("dp", "tensor"), None),
            P(("dp", "tensor"), None),
            P(("dp", "tensor")),
            P(("dp", "tensor")),
            P(None, "dp", "tensor"),
            P(None, ("tensor", "dp")),
            P("tensor", "dp"),
            P("dp", "tensor"),
            P(("tensor", "dp")),
            P("tensor", "dp"),
            P(("dp", "tensor")),
            P(),
        ),
        check_vma=False,
    )
```

```python
import functools
import math

import jax
import jax.numpy as jnp
from jax import lax
from jax.experimental import pallas as pl
from jax.experimental.pallas import tpu as pltpu
from jax.sharding import PartitionSpec as P

HEAD_DIM = 64
ROT = 32
PAIR = 2 * HEAD_DIM
BLOCK = 256
MOST = 5

EPS = 1e-05
GELU_C = math.sqrt(2.0 / math.pi)


def segment_starts(segs):
    return jnp.sum((segs[:, None, :] < segs[:, :, None]).astype(jnp.int32), axis=-1)


def rotary_wide(starts):
    length = starts.shape[0]
    half_rot = ROT // 2
    frequency = jnp.exp(-math.log(10000.0) * (2.0 * jnp.arange(half_rot, dtype=jnp.float32) / ROT))
    position = jnp.arange(length, dtype=jnp.int32) - starts
    angles = position.astype(jnp.float32)[:, None] * frequency
    cosines, sines = jnp.cos(angles), jnp.sin(angles)
    ones = jnp.ones((length, HEAD_DIM - ROT), jnp.float32)
    cos_head = jnp.concatenate([cosines, cosines, ones], axis=-1)
    sin_head = jnp.concatenate([-sines, sines, 0.0 * ones], axis=-1)
    return (jnp.concatenate([cos_head, cos_head], -1), jnp.concatenate([sin_head, sin_head], -1))


def turn(x, cos_wide, sin_wide):
    lane = lax.broadcasted_iota(jnp.int32, x.shape, 1) % HEAD_DIM
    half_rot = ROT // 2
    partner = jnp.where(
        lane < half_rot, pltpu.roll(x, PAIR - half_rot, 1), pltpu.roll(x, half_rot, 1)
    )
    return x * cos_wide + partner * sin_wide


def first_half(shape):
    return lax.broadcasted_iota(jnp.int32, shape, len(shape) - 1) < HEAD_DIM


def halves(x):
    front = first_half(x.shape)
    zero = jnp.zeros_like(x)
    return (jnp.where(front, x, zero), jnp.where(front, zero, x))


def nt(left, right):
    return lax.dot_general(
        left, right, (((1,), (1,)), ((), ())), preferred_element_type=jnp.float32
    )


def nn(left, right):
    return lax.dot_general(
        left, right, (((1,), (0,)), ((), ())), preferred_element_type=jnp.float32
    )


def tn(left, right):
    return lax.dot_general(
        left, right, (((0,), (0,)), ((), ())), preferred_element_type=jnp.float32
    )


def attend_kernel(
    low_ref, place_ref, parts, bias_ref, cos_ref, sin_ref, start_ref, valid_ref,
    q_ref, k_ref, v_ref, ctx_ref, lse_ref, km, vm,
):
    length = q_ref.shape[0]
    blocks = length // BLOCK
    scale = 1.0 / math.sqrt(HEAD_DIM)

    per = length // len(parts) // BLOCK

    def project(i, slot):
        rows = pl.ds(pl.multiple_of(place_ref[slot * per + i] * BLOCK, BLOCK), BLOCK)
        here = pl.ds(i * BLOCK, BLOCK)
        part = parts[slot]
        cw, sw = cos_ref[rows, :], sin_ref[rows, :]
        x = part[here, :] + bias_ref[...]
        q = turn(x[:, :PAIR], cw, sw).astype(jnp.bfloat16)
        q_ref[rows, :] = q * jnp.bfloat16(scale)
        k = turn(x[:, PAIR : 2 * PAIR], cw, sw).astype(jnp.bfloat16)
        k_ref[rows, :] = k
        v = x[:, 2 * PAIR :].astype(jnp.bfloat16)
        v_ref[rows, :] = v
        km[0, rows, :], km[1, rows, :] = halves(k)
        vm[0, rows, :], vm[1, rows, :] = halves(v)

    for slot in range(len(parts)):
        for i in range(per):
            project(i, slot)

    def query_block(i, count):
        rows = pl.ds(pl.multiple_of(i * BLOCK, BLOCK), BLOCK)
        base = pl.multiple_of((i + 1 - count) * BLOCK, BLOCK)
        cols = pl.ds(base, count * BLOCK)
        shape = (BLOCK, count * BLOCK)
        q = q_ref[rows, :]
        start = start_ref[rows, :][:, :1] - base
        kpos = lax.broadcasted_iota(jnp.int32, shape, 1)
        qpos = lax.broadcasted_iota(jnp.int32, shape, 0) + (count - 1) * BLOCK
        allowed = (kpos >= start) & (kpos <= qpos)
        there = pl.ds(pl.multiple_of(place_ref[i] * BLOCK, BLOCK), BLOCK)
        acc = jnp.zeros((BLOCK, PAIR), jnp.float32)
        tops, sums = [], []
        for h in range(2):
            s = jnp.where(allowed, nt(q, km[h, cols, :]), -jnp.inf)
            top = jnp.max(s, axis=-1, keepdims=True)
            e = jnp.exp(s - top)
            tops.append(top)
            sums.append(jnp.sum(e, axis=-1, keepdims=True))
            acc = acc + nn(e.astype(jnp.bfloat16), vm[h, cols, :])
        front = first_half((BLOCK, PAIR))
        out = acc / jnp.where(front, sums[0], sums[1])
        ctx_ref[there, :] = (out * valid_ref[rows, :]).astype(jnp.bfloat16)
        lse = jnp.where(front, tops[0] + jnp.log(sums[0]), tops[1] + jnp.log(sums[1]))
        lse_t = lse.T
        lse_ref[0, 0:1, rows] = lse_t[0:1, :]
        lse_ref[0, 1:2, rows] = lse_t[HEAD_DIM : HEAD_DIM + 1, :]

    def step(i, _):
        for count in range(1, MOST + 1):
            pl.when(i + 1 - low_ref[i] == count)(functools.partial(query_block, i, count))
        return 0

    lax.fori_loop(0, blocks, step, 0)


def attention_forward(projected, bias, tables, first, count, held=None):
    cos_wide, sin_wide, starts, valid_wide, lows, places = tables
    width = projected[0].shape[1] // 3
    length = starts.shape[0]
    blocks = length // BLOCK
    ways = len(projected)
    start_wide = jnp.broadcast_to(starts[:, None], (length, PAIR))
    part = pl.BlockSpec((length // ways, 3 * PAIR), lambda p, low, place: (0, p + first))
    table = pl.BlockSpec((length, PAIR), lambda p, low, place: (0, 0))
    flat = pl.BlockSpec((length, PAIR), lambda p, low, place: (0, p + first))
    flat_shape = jax.ShapeDtypeStruct((length, width), jnp.bfloat16)
    held = tuple(held or ())

    def kernel(*refs):
        rest = refs[2 + ways :]
        attend_kernel(*refs[:2], refs[2 : 2 + ways], *rest[:5], *rest[5 + len(held) :])

    return pl.pallas_call(
        kernel,
        grid_spec=pltpu.PrefetchScalarGridSpec(
            num_scalar_prefetch=2,
            grid=(count,),
            in_specs=[
                *[part] * ways,
                pl.BlockSpec((1, 3 * PAIR), lambda p, low, place: (0, p + first)),
                table, table, table, table,
            ] + [pl.BlockSpec(memory_space=pl.ANY)] * len(held),
            out_specs=[flat, flat, flat, flat,
                       pl.BlockSpec((1, 2, length), lambda p, low, place: (p + first, 0, 0))],
            scratch_shapes=[
                pltpu.VMEM((2, length, PAIR), jnp.bfloat16),
                pltpu.VMEM((2, length, PAIR), jnp.bfloat16),
            ],
        ),
        out_shape=[flat_shape] * 4
        + [jax.ShapeDtypeStruct((width // PAIR, 2, length), jnp.float32)],
        input_output_aliases={7 + ways + i: i for i in range(len(held))},
        compiler_params=pltpu.CompilerParams(vmem_limit_bytes=48 * 2**20),
        name="attend",
    )(lows, places, *projected, bias[None, :], cos_wide, sin_wide,
      start_wide, valid_wide, *held)


def attend_back_kernel(
    low_ref, place_ref, dos, q_ref, k_ref, v_ref, lse_ref, cos_ref, sin_ref, start_ref, valid_ref,
    grad_ref, sums_ref, qm, km, vm, dom, do_scr, dk_acc, dv_acc,
):
    length = q_ref.shape[0]
    blocks = length // BLOCK
    scale = 1.0 / math.sqrt(HEAD_DIM)

    def split(i, _):
        rows = pl.ds(pl.multiple_of(i * BLOCK, BLOCK), BLOCK)
        qm[0, rows, :], qm[1, rows, :] = halves(q_ref[rows, :])
        km[0, rows, :], km[1, rows, :] = halves(k_ref[rows, :])
        vm[0, rows, :], vm[1, rows, :] = halves(v_ref[rows, :])
        dk_acc[rows, :] = jnp.zeros((BLOCK, PAIR), jnp.float32)
        dv_acc[rows, :] = jnp.zeros((BLOCK, PAIR), jnp.float32)
        return 0

    lax.fori_loop(0, blocks, split, 0)

    per = length // len(dos) // BLOCK
    for slot in range(len(dos)):
        for i in range(per):
            rows = pl.ds(pl.multiple_of(place_ref[slot * per + i] * BLOCK, BLOCK), BLOCK)
            do = dos[slot][i * BLOCK : (i + 1) * BLOCK, :].astype(jnp.float32)
            do = (do * valid_ref[rows, :]).astype(jnp.bfloat16)
            do_scr[rows, :] = do
            dom[0, rows, :], dom[1, rows, :] = halves(do)

    def query_block(i, count):
        rows = pl.ds(pl.multiple_of(i * BLOCK, BLOCK), BLOCK)
        base = pl.multiple_of((i + 1 - count) * BLOCK, BLOCK)
        cols = pl.ds(base, count * BLOCK)
        shape = (count * BLOCK, BLOCK)
        q = q_ref[rows, :]
        do = do_scr[rows, :]
        start = start_ref[:, rows] - base
        kpos = lax.broadcasted_iota(jnp.int32, shape, 0)
        qpos = lax.broadcasted_iota(jnp.int32, shape, 1) + (count - 1) * BLOCK
        allowed = (kpos >= start) & (kpos <= qpos)
        dk = dk_acc[cols, :]
        dv = dv_acc[cols, :]
        dq = jnp.zeros((BLOCK, PAIR), jnp.float32)
        for h in range(2):
            s = nt(km[h, cols, :], q)
            p = jnp.where(allowed, jnp.exp(s - lse_ref[0, h : h + 1, rows]), 0.0)
            dp = nt(vm[h, cols, :], do)
            delta = jnp.sum(p * dp, axis=0, keepdims=True)
            dv = dv + nn(p.astype(jnp.bfloat16), dom[h, rows, :])
            ds = (p * (dp - delta)).astype(jnp.bfloat16)
            dk = dk + nn(ds, qm[h, rows, :])
            dq = dq + tn(ds, km[h, cols, :])
        dk_acc[cols, :] = dk
        dv_acc[cols, :] = dv
        dq = turn(dq * scale, cos_ref[rows, :], -sin_ref[rows, :]).astype(jnp.bfloat16)
        there = pl.ds(pl.multiple_of(place_ref[i] * BLOCK, BLOCK), BLOCK)
        grad_ref[there, :PAIR] = dq
        sums_ref[0] += jnp.sum(dq.astype(jnp.float32), axis=0, keepdims=True)

    none = jnp.zeros((1, PAIR), jnp.float32)
    sums_ref[0] = none

    def step(i, _):
        for count in range(1, MOST + 1):
            pl.when(i + 1 - low_ref[i] == count)(functools.partial(query_block, i, count))
        return 0

    lax.fori_loop(0, blocks, step, 0)

    def finish(i, totals):
        rows = pl.ds(pl.multiple_of(i * BLOCK, BLOCK), BLOCK)
        dk = turn(dk_acc[rows, :], cos_ref[rows, :], -sin_ref[rows, :]).astype(jnp.bfloat16)
        dv = dv_acc[rows, :].astype(jnp.bfloat16)
        there = pl.ds(pl.multiple_of(place_ref[i] * BLOCK, BLOCK), BLOCK)
        grad_ref[there, PAIR : 2 * PAIR] = dk
        grad_ref[there, 2 * PAIR :] = dv
        return (
            totals[0] + jnp.sum(dk.astype(jnp.float32), axis=0, keepdims=True),
            totals[1] + jnp.sum(dv.astype(jnp.float32), axis=0, keepdims=True),
        )

    sums_ref[1], sums_ref[2] = lax.fori_loop(0, blocks, finish, (none, none))


def attention_backward(q, k, v, do, lse, tables, first, count, held=None):
    cos_wide, sin_wide, starts, valid_wide, lows, places = tables
    length, width = q.shape
    blocks = length // BLOCK
    flat = pl.BlockSpec((length, PAIR), lambda p, low, place: (0, p + first))
    table = pl.BlockSpec((length, PAIR), lambda p, low, place: (0, 0))
    held = tuple(held or ())
    ways = len(do)

    def kernel(*refs):
        rest = refs[2 + ways :]
        attend_back_kernel(*refs[:2], refs[2 : 2 + ways], *rest[:8], *rest[8 + len(held) :])

    return pl.pallas_call(
        kernel,
        grid_spec=pltpu.PrefetchScalarGridSpec(
            num_scalar_prefetch=2,
            grid=(count,),
            in_specs=[
                *[pl.BlockSpec((length // ways, PAIR), lambda p, low, place: (0, p + first))] * ways,
                flat, flat, flat,
                pl.BlockSpec((1, 2, length), lambda p, low, place: (p + first, 0, 0)),
                table, table,
                pl.BlockSpec((1, length), lambda p, low, place: (0, 0)),
                table,
            ] + [pl.BlockSpec(memory_space=pl.ANY)] * len(held),
            out_specs=[
                pl.BlockSpec((length, 3 * PAIR), lambda p, low, place: (0, p + first)),
                pl.BlockSpec((3, 1, PAIR), lambda p, low, place: (0, 0, p + first)),
            ],
            scratch_shapes=[pltpu.VMEM((2, length, PAIR), jnp.bfloat16)] * 4
            + [pltpu.VMEM((length, PAIR), jnp.bfloat16)]
            + [pltpu.VMEM((length, PAIR), jnp.float32)] * 2,
        ),
        out_shape=[
            jax.ShapeDtypeStruct((length, 3 * width), jnp.bfloat16),
            jax.ShapeDtypeStruct((3, 1, width), jnp.float32),
        ],
        input_output_aliases={10 + ways + i: i for i in range(len(held))},
        compiler_params=pltpu.CompilerParams(vmem_limit_bytes=48 * 2**20),
        name="attend_back",
    )(lows, places, *do, q, k, v, lse, cos_wide, sin_wide, starts[None, :], valid_wide, *held)


def hidden_back_kernel(block_ref, weight_ref, slope_ref, *refs):
    grad = nt(block_ref[...], weight_ref[...])
    refs[-1][...] = (grad * slope_ref[...]).astype(jnp.bfloat16)


def hidden_back(block, weight, slope, place, ways, held=None):
    rows, model_width = block.shape
    hidden = weight.shape[0]
    tile = min(512, hidden)
    held = () if held is None else (held,)
    return pl.pallas_call(
        hidden_back_kernel,
        grid=(hidden // tile,),
        in_specs=[
            pl.BlockSpec((rows, model_width), lambda j: (0, 0)),
            pl.BlockSpec((tile, model_width), lambda j: (j, 0)),
            pl.BlockSpec((rows, tile), lambda j: (0, j)),
        ]
        + [pl.BlockSpec(memory_space=pl.ANY)] * len(held),
        out_specs=pl.BlockSpec((rows, tile), lambda j: (place, j)),
        out_shape=jax.ShapeDtypeStruct((ways * rows, hidden), jnp.bfloat16),
        input_output_aliases={3: 0} if held else {},
        compiler_params=pltpu.CompilerParams(vmem_limit_bytes=40 * 2**20),
        cost_estimate=pl.CostEstimate(
            flops=2 * rows * model_width * hidden,
            bytes_accessed=2 * hidden * model_width,
            transcendentals=0,
        ),
        name="hidden_back",
    )(block, weight, slope, *held)


def gelu_and_slope(u):
    tanh_value = jnp.tanh(GELU_C * (u + 0.044715 * u * u * u))
    value = 0.5 * u * (1.0 + tanh_value)
    slope = 0.5 * (1.0 + tanh_value) + 0.5 * u * (1.0 - tanh_value * tanh_value) * GELU_C * (
        1.0 + 3.0 * 0.044715 * u * u
    )
    return (value, slope)


def contract_rows(left, right):
    return lax.dot_general(
        left, right, (((0,), (0,)), ((), ())), preferred_element_type=jnp.float32
    )


def contract_cols(left, right):
    return lax.dot_general(
        left, right, (((1,), (1,)), ((), ())), preferred_element_type=jnp.float32
    )


def shift(x, pairs):
    return lax.ppermute(x, "tensor", pairs)


class LineGather:
    def __init__(self, x):
        self.up, self.down = [x], [x]

    def step(self):
        n, k = lax.axis_size("tensor"), len(self.up)
        self.up.append(shift(self.up[-1], [(i, i + 1) for i in range(k - 1, n - 1)]))
        self.down.append(shift(self.down[-1], [(i, i - 1) for i in range(1, n - k + 1)]))

    def block(self, k):
        n, me = lax.axis_size("tensor"), lax.axis_index("tensor")
        return jnp.where(me >= k, self.up[k], self.down[n - k]) if k else self.up[0]


class RingScatter:
    def __init__(self, parts, rows):
        self.parts, self.rows, self.k, self.up, self.down = list(parts), rows, 0, None, None

    def next(self):
        place = self.k * self.rows
        for part in self.parts:
            if place < part.shape[0]:
                return part[place : place + self.rows]
            place -= part.shape[0]

    def step(self):
        n, mine = lax.axis_size("tensor"), self.next()
        if self.k:
            mine = (mine.astype(jnp.float32) + self.up.astype(jnp.float32)).astype(jnp.bfloat16)
        self.up = shift(mine, [(i, (i + 1) % n) for i in range(n)])
        self.k += 1

    def total(self):
        return self.next().astype(jnp.float32) + self.up.astype(jnp.float32)


class LineScatter:
    def __init__(self, parts):
        self.parts, self.k, self.up, self.down = parts, 1, None, None

    def step(self):
        n, k = lax.axis_size("tensor"), self.k
        mine_up, mine_down = self.parts[k], self.parts[n - k]
        if k > 1:
            mine_up = mine_up.astype(jnp.float32) + self.up.astype(jnp.float32)
            mine_down = mine_down.astype(jnp.float32) + self.down.astype(jnp.float32)
        self.up = shift(mine_up.astype(jnp.bfloat16), [(i, i + 1) for i in range(k)])
        self.down = shift(mine_down.astype(jnp.bfloat16), [(i, i - 1) for i in range(n - k, n)])
        self.k = k + 1

    def total(self):
        return sum(x.astype(jnp.float32) for x in (self.parts[0], self.up, self.down))


def together(*moves, after=()):
    state = [
        (m.up[-1], m.down[-1]) if isinstance(m, LineGather) else (m.parts, m.up, m.down)
        for m in moves
    ]
    state, after = lax.optimization_barrier((state, after))
    for m, kept in zip(moves, state):
        if isinstance(m, LineGather):
            m.up[-1], m.down[-1] = kept
        else:
            m.parts, m.up, m.down = kept
    return after


def blocks_of(whole, n):
    rows = whole.shape[0] // n
    return [whole[k * rows : (k + 1) * rows] for k in range(n)]


def scatter_low(part, axis, dim):
    return lax.psum_scatter(
        part.astype(jnp.bfloat16), axis, scatter_dimension=dim, tiled=True
    ).astype(jnp.float32)


def body(
    tokens,
    segments,
    norm_gain,
    norm_shift,
    qkv_weight,
    qkv_bias,
    dense_weight,
    up_weight,
    up_bias,
    down_weight,
    out_bias,
    cotangent,
):
    row_count, model_width = tokens.shape
    length = segments.shape[1]
    ways, copies = lax.axis_size("tensor"), lax.axis_size("dp")
    me = lax.axis_index("tensor")
    low = jnp.bfloat16
    resid = tokens.astype(jnp.float32)
    row_mean = jnp.mean(resid, axis=-1, keepdims=True)
    centered = resid - row_mean
    inverse = lax.rsqrt(jnp.mean(centered * centered, axis=-1, keepdims=True) + EPS)
    normed = centered * inverse
    normed_mine = (normed * norm_gain + norm_shift).astype(low)
    full_qkv = lax.all_gather(qkv_weight, "dp", axis=1, tiled=True)
    normed_mine, up_weight, down_weight, dense_weight = lax.optimization_barrier(
        (normed_mine, up_weight, down_weight, dense_weight)
    )
    full_up = lax.all_gather(up_weight, "dp", axis=0, tiled=True)
    full_down = lax.all_gather(down_weight, "dp", axis=1, tiled=True)
    full_dense = lax.all_gather(dense_weight, "dp", axis=1, tiled=True)
    around = [(i, (i + 1) % ways) for i in range(ways)]
    ring = [normed_mine, shift(normed_mine, around)]

    biases = jnp.concatenate([qkv_bias.reshape(-1), up_bias])
    biases = lax.all_gather(biases, "dp", axis=0).astype(jnp.float32)
    third = qkv_bias.shape[1]
    full_qbias = biases[:, : 3 * third].reshape(copies, 3, third)
    full_qbias = full_qbias.transpose(1, 0, 2).reshape(3, -1, PAIR).transpose(1, 0, 2).reshape(-1)
    full_ubias = biases[:, 3 * third :].reshape(-1)

    starts = segment_starts(segments)[0]
    cos_wide, sin_wide = rotary_wide(starts)
    valid_rows = (segments != 0).astype(jnp.float32).reshape(length, 1)
    valid_wide = jnp.broadcast_to(valid_rows, (length, PAIR))
    lows = starts[::BLOCK] // BLOCK
    chunk = jnp.arange(length // BLOCK, dtype=jnp.int32)
    per = row_count // BLOCK
    places = (me - 1 - chunk // per) % ways * per + chunk % per

    tables = (cos_wide, sin_wide, starts, valid_wide, lows, places)
    valid_mine = lax.dynamic_slice_in_dim(valid_rows, me * row_count, row_count, 0)
    cot_columns = jnp.sum(cotangent, axis=0, dtype=jnp.float32)
    resid_square = jnp.sum(valid_mine * resid * resid)
    fixed = lax.optimization_barrier
    ring[1], cot_mine, tables, full_qbias, full_ubias, cot_columns, resid_square = fixed(
        (ring[1], cotangent, tables, full_qbias, full_ubias, cot_columns, resid_square)
    )
    pairs = qkv_weight.shape[2] // PAIR
    sorted_qkv = full_qkv.reshape(3, model_width, pairs, PAIR).transpose(1, 2, 0, 3)
    sorted_qkv = sorted_qkv.reshape(model_width, 3 * pairs * PAIR)
    half = max(1, pairs // 2)
    projected, slopes, hidden_act, mlp_parts = ([None] * ways for _ in range(4))
    grad_context, grad_pre = [None] * ways, [None]

    def turned(blocks):
        return [*blocks[1:], blocks[0]]

    def project(k):
        projected[k] = jnp.dot(ring[k], sorted_qkv, preferred_element_type=jnp.float32)

    def widen(k):
        pre = jnp.dot(ring[k], full_up, preferred_element_type=jnp.float32) + full_ubias
        value, slopes[k] = gelu_and_slope(pre)
        hidden_act[k] = value.astype(low)

    def narrow(k):
        mlp_parts[k] = jnp.dot(
            hidden_act[k], full_down, preferred_element_type=jnp.float32
        ).astype(low)

    def context_back(k, block):
        grad_context[k] = contract_cols(block, full_dense).astype(low)

    def inner_back(k, block):
        grad_pre[0] = hidden_back(
            block, full_down, slopes[k], (k - 1) % ways, ways, held=grad_pre[0]
        )

    for k in range(2, ways):
        coming = shift(ring[k - 1], around)
        if k == 2:
            project(0)
            project(1)
        if k == ways - 1:
            for j in range(ways - 1):
                if projected[j] is None:
                    project(j)
                widen(j)
        coming, ring, projected, slopes, hidden_act, cot_mine = fixed(
            (coming, ring, projected, slopes, hidden_act, cot_mine)
        )
        ring.append(coming)

    cot = LineGather(cot_mine)
    cot.step()
    project(ways - 1)
    widen(ways - 1)
    for k in range(ways):
        narrow(k)
    ring, projected, slopes, hidden_act, mlp_parts = together(
        cot, after=(ring, projected, slopes, hidden_act, mlp_parts)
    )

    mlp = LineScatter(mlp_parts)
    while len(cot.up) < ways - 1:
        cot.step()
        mlp.step()
    attended = attention_forward(turned(projected), full_qbias, tables, 0, pairs)
    ring, attended, slopes, hidden_act, sorted_qkv = together(
        cot, mlp, after=(ring, attended, slopes, hidden_act, sorted_qkv)
    )
    query, keys, values, context_low, logsum = attended

    cot.step()
    mlp.step()
    for k in [0, *range(2, ways - 1)]:
        context_back(k, cot.block(k))
        inner_back(k, cot.block(k))
    acts = jnp.concatenate(turned(hidden_act), axis=0)
    attn_part = jnp.dot(context_low, full_dense, preferred_element_type=jnp.float32).astype(low)
    grad_context, grad_pre, acts, slopes, attn_part = together(
        cot, mlp, after=(grad_context, grad_pre, acts, slopes, attn_part)
    )

    while mlp.k < ways:
        mlp.step()
    blocks = [cot.block(k) for k in range(ways)]
    late = sorted({1, ways - 1})
    for k in late:
        context_back(k, blocks[k])
    grad_full = jnp.concatenate(turned(blocks), axis=0)
    grad_down = contract_rows(acts, grad_full).astype(low)
    grad_context, attn_part, grad_full, grad_down, blocks, grad_pre, slopes = together(
        mlp, after=(grad_context, attn_part, grad_full, grad_down, blocks, grad_pre, slopes)
    )
    part_down = scatter_low(grad_down, "dp", 1)

    attn = RingScatter([attn_part], row_count)
    attn.step()
    grads = attention_backward(query, keys, values, turned(grad_context), logsum, tables, 0, half)
    for k in late:
        inner_back(k, blocks[k])
    normed_low = jnp.concatenate(turned(ring), axis=0)
    [pre_full] = grad_pre
    grads, grad_context, grad_full, context_low, pre_full, normed_low = together(
        attn, mlp, after=(grads, grad_context, grad_full, context_low, pre_full, normed_low)
    )

    while attn.k < ways - 2:
        attn.step()
    if pairs > half:
        grads = attention_backward(
            query, keys, values, turned(grad_context), logsum, tables, half, pairs - half, held=grads
        )
    grad_up = contract_rows(normed_low, pre_full).astype(low)
    grads, grad_up, pre_full, normed_low, grad_full, context_low, part_down = together(
        attn, mlp, after=(grads, grad_up, pre_full, normed_low, grad_full, context_low, part_down)
    )
    part_up = scatter_low(grad_up, "dp", 0)
    grad_proj, grad_qbias = grads[0], grads[1][:, 0, :]

    def return_normed(low_block, high_block):
        rows = slice(low_block * row_count, high_block * row_count)
        part = contract_cols(pre_full[rows], full_up) + contract_cols(grad_proj[rows], sorted_qkv)
        return part.astype(low)

    attn.step()
    grad_qkv = contract_rows(normed_low, grad_proj).astype(low)
    grad_parts = [return_normed(0, ways // 2)]
    grad_parts, grad_qkv, pre_full, grad_proj, grad_full, context_low = together(
        attn, mlp, after=(grad_parts, grad_qkv, pre_full, grad_proj, grad_full, context_low)
    )
    part_qkv = scatter_low(grad_qkv, "dp", 0).reshape(-1, pairs, 3, PAIR)
    part_qkv = part_qkv.transpose(2, 0, 1, 3).reshape(3, -1, pairs * PAIR)

    last = RingScatter(grad_parts, row_count)
    last.step()
    last.parts.append(return_normed(ways // 2, ways))
    grad_dense = contract_rows(context_low, grad_full).astype(low)
    grad_dense, pre_full, part_up = together(last, attn, mlp, after=(grad_dense, pre_full, part_up))
    part_dense = scatter_low(grad_dense, "dp", 1)
    while last.k < ways - 2:
        last.step()
    grad_ubias = jnp.sum(pre_full, axis=0, dtype=jnp.float32)
    attn_mine, mlp_mine = attn.total(), mlp.total()
    attn_mine, mlp_mine, grad_ubias, part_qkv = together(
        last, after=(attn_mine, mlp_mine, grad_ubias, part_qkv)
    )
    last.step()
    output = (resid + attn_mine + mlp_mine + out_bias).astype(low)
    attn_square = jnp.sum(valid_mine * attn_mine * attn_mine)
    mlp_square = jnp.sum(valid_mine * mlp_mine * mlp_mine)
    totals = jnp.stack(
        [resid_square, attn_square, mlp_square, jnp.sum(valid_mine) * model_width]
    )
    peers = copies * ways
    share = model_width // peers
    own_bias = jnp.concatenate(
        [
            grad_qbias.reshape(3, copies, third).transpose(1, 0, 2).reshape(copies, 3 * third),
            grad_ubias.reshape(copies, -1),
        ],
        axis=1,
    )
    same = (jnp.arange(ways) == me).astype(jnp.float32)[None, :, None]
    own_bias = (own_bias[:, None, :] * same).reshape(peers, -1)

    def summed(parts):
        return jnp.sum(lax.all_to_all(parts, ("dp", "tensor"), 0, 0, tiled=True), axis=0)

    small = summed(
        jnp.concatenate(
            [cot_columns.reshape(peers, share), own_bias, jnp.broadcast_to(totals, (peers, 4))],
            axis=1,
        )
    )
    output, small, part_dense = together(last, after=(output, small, part_dense))
    part_obias = small[:share]
    part_qbias = small[share : share + 3 * third].reshape(3, third)
    part_ubias = small[share + 3 * third : -4]
    root_squares = jnp.sqrt(small[-4:-1] / small[-1])
    grad_mine = last.total()
    scaled = grad_mine * norm_gain
    grad_tokens = (
        cotangent.astype(jnp.float32)
        + inverse
        * (
            scaled
            - jnp.mean(scaled, axis=-1, keepdims=True)
            - normed * jnp.mean(scaled * normed, axis=-1, keepdims=True)
        )
    ).astype(low)

    columns = jnp.stack([jnp.sum(grad_mine * normed, axis=0), jnp.sum(grad_mine, axis=0)])
    columns = columns.reshape(2, peers, share).transpose(1, 0, 2).reshape(peers, 2 * share)
    columns = summed(columns)
    part_gain, part_shift = columns[:share], columns[share:]
    return (
        output,
        grad_tokens,
        part_gain,
        part_shift,
        part_qkv,
        part_qbias,
        part_dense,
        part_up,
        part_ubias,
        part_down,
        part_obias,
        root_squares,
    )


def solution(mesh):
    placed = (
        P(("dp", "tensor"), None),
        P("dp", None),
        P(),
        P(),
        P(None, "dp", "tensor"),
        P(None, ("tensor", "dp")),
        P("tensor", "dp"),
        P("dp", "tensor"),
        P(("tensor", "dp")),
        P("tensor", "dp"),
        P(),
        P(("dp", "tensor"), None),
    )
    return jax.shard_map(
        body,
        mesh=mesh,
        in_specs=placed,
        out_specs=(
            P(("dp", "tensor"), None),
            P(("dp", "tensor"), None),
            P(("dp", "tensor")),
            P(("dp", "tensor")),
            P(None, "dp", "tensor"),
            P(None, ("tensor", "dp")),
            P("tensor", "dp"),
            P("dp", "tensor"),
            P(("tensor", "dp")),
            P("tensor", "dp"),
            P(("dp", "tensor")),
            P(),
        ),
        check_vma=False,
    )
```

```python
import functools
import math

import jax
import jax.numpy as jnp
from jax import lax
from jax.experimental import pallas as pl
from jax.experimental.pallas import tpu as pltpu
from jax.sharding import PartitionSpec as P

HEAD_DIM = 64
ROT = 32
PAIR = 2 * HEAD_DIM
BLOCK = 256
MOST = 5

EPS = 1e-05
GELU_C = math.sqrt(2.0 / math.pi)


def segment_starts(segs):
    return jnp.sum((segs[:, None, :] < segs[:, :, None]).astype(jnp.int32), axis=-1)


def rotary_wide(starts):
    length = starts.shape[0]
    half_rot = ROT // 2
    frequency = jnp.exp(-math.log(10000.0) * (2.0 * jnp.arange(half_rot, dtype=jnp.float32) / ROT))
    position = jnp.arange(length, dtype=jnp.int32) - starts
    angles = position.astype(jnp.float32)[:, None] * frequency
    cosines, sines = jnp.cos(angles), jnp.sin(angles)
    ones = jnp.ones((length, HEAD_DIM - ROT), jnp.float32)
    cos_head = jnp.concatenate([cosines, cosines, ones], axis=-1)
    sin_head = jnp.concatenate([-sines, sines, 0.0 * ones], axis=-1)
    return (jnp.concatenate([cos_head, cos_head], -1), jnp.concatenate([sin_head, sin_head], -1))


def turn(x, cos_wide, sin_wide):
    lane = lax.broadcasted_iota(jnp.int32, x.shape, 1) % HEAD_DIM
    half_rot = ROT // 2
    partner = jnp.where(
        lane < half_rot, pltpu.roll(x, PAIR - half_rot, 1), pltpu.roll(x, half_rot, 1)
    )
    return x * cos_wide + partner * sin_wide


def first_half(shape):
    return lax.broadcasted_iota(jnp.int32, shape, len(shape) - 1) < HEAD_DIM


def halves(x):
    front = first_half(x.shape)
    zero = jnp.zeros_like(x)
    return (jnp.where(front, x, zero), jnp.where(front, zero, x))


def nt(left, right):
    return lax.dot_general(
        left, right, (((1,), (1,)), ((), ())), preferred_element_type=jnp.float32
    )


def nn(left, right):
    return lax.dot_general(
        left, right, (((1,), (0,)), ((), ())), preferred_element_type=jnp.float32
    )


def tn(left, right):
    return lax.dot_general(
        left, right, (((0,), (0,)), ((), ())), preferred_element_type=jnp.float32
    )


def attend_kernel(
    low_ref, place_ref, parts, bias_ref, cos_ref, sin_ref, start_ref, valid_ref,
    q_ref, k_ref, v_ref, ctx_ref, lse_ref, km, vm,
):
    length = q_ref.shape[0]
    blocks = length // BLOCK
    scale = 1.0 / math.sqrt(HEAD_DIM)

    per = length // len(parts) // BLOCK

    def project(i, slot):
        rows = pl.ds(pl.multiple_of(place_ref[slot * per + i] * BLOCK, BLOCK), BLOCK)
        here = pl.ds(i * BLOCK, BLOCK)
        part = parts[slot]
        cw, sw = cos_ref[rows, :], sin_ref[rows, :]
        x = part[here, :] + bias_ref[...]
        q = turn(x[:, :PAIR], cw, sw).astype(jnp.bfloat16)
        q_ref[rows, :] = q * jnp.bfloat16(scale)
        k = turn(x[:, PAIR : 2 * PAIR], cw, sw).astype(jnp.bfloat16)
        k_ref[rows, :] = k
        v = x[:, 2 * PAIR :].astype(jnp.bfloat16)
        v_ref[rows, :] = v
        km[0, rows, :], km[1, rows, :] = halves(k)
        vm[0, rows, :], vm[1, rows, :] = halves(v)

    for slot in range(len(parts)):
        for i in range(per):
            project(i, slot)

    def query_block(i, count):
        rows = pl.ds(pl.multiple_of(i * BLOCK, BLOCK), BLOCK)
        base = pl.multiple_of((i + 1 - count) * BLOCK, BLOCK)
        cols = pl.ds(base, count * BLOCK)
        shape = (BLOCK, count * BLOCK)
        q = q_ref[rows, :]
        start = start_ref[rows, :][:, :1] - base
        kpos = lax.broadcasted_iota(jnp.int32, shape, 1)
        qpos = lax.broadcasted_iota(jnp.int32, shape, 0) + (count - 1) * BLOCK
        allowed = (kpos >= start) & (kpos <= qpos)
        there = pl.ds(pl.multiple_of(place_ref[i] * BLOCK, BLOCK), BLOCK)
        acc = jnp.zeros((BLOCK, PAIR), jnp.float32)
        tops, sums = [], []
        for h in range(2):
            s = jnp.where(allowed, nt(q, km[h, cols, :]), -jnp.inf)
            top = jnp.max(s, axis=-1, keepdims=True)
            e = jnp.exp(s - top)
            tops.append(top)
            sums.append(jnp.sum(e, axis=-1, keepdims=True))
            acc = acc + nn(e.astype(jnp.bfloat16), vm[h, cols, :])
        front = first_half((BLOCK, PAIR))
        out = acc / jnp.where(front, sums[0], sums[1])
        ctx_ref[there, :] = (out * valid_ref[rows, :]).astype(jnp.bfloat16)
        lse = jnp.where(front, tops[0] + jnp.log(sums[0]), tops[1] + jnp.log(sums[1]))
        lse_t = lse.T
        lse_ref[0, 0:1, rows] = lse_t[0:1, :]
        lse_ref[0, 1:2, rows] = lse_t[HEAD_DIM : HEAD_DIM + 1, :]

    def step(i, _):
        for count in range(1, MOST + 1):
            pl.when(i + 1 - low_ref[i] == count)(functools.partial(query_block, i, count))
        return 0

    lax.fori_loop(0, blocks, step, 0)


def attention_forward(projected, bias, tables, first, count, held=None):
    cos_wide, sin_wide, starts, valid_wide, lows, places = tables
    width = projected[0].shape[1] // 3
    length = starts.shape[0]
    blocks = length // BLOCK
    ways = len(projected)
    start_wide = jnp.broadcast_to(starts[:, None], (length, PAIR))
    part = pl.BlockSpec((length // ways, 3 * PAIR), lambda p, low, place: (0, p + first))
    table = pl.BlockSpec((length, PAIR), lambda p, low, place: (0, 0))
    flat = pl.BlockSpec((length, PAIR), lambda p, low, place: (0, p + first))
    flat_shape = jax.ShapeDtypeStruct((length, width), jnp.bfloat16)
    held = tuple(held or ())

    def kernel(*refs):
        rest = refs[2 + ways :]
        attend_kernel(*refs[:2], refs[2 : 2 + ways], *rest[:5], *rest[5 + len(held) :])

    return pl.pallas_call(
        kernel,
        grid_spec=pltpu.PrefetchScalarGridSpec(
            num_scalar_prefetch=2,
            grid=(count,),
            in_specs=[
                *[part] * ways,
                pl.BlockSpec((1, 3 * PAIR), lambda p, low, place: (0, p + first)),
                table, table, table, table,
            ] + [pl.BlockSpec(memory_space=pl.ANY)] * len(held),
            out_specs=[flat, flat, flat, flat,
                       pl.BlockSpec((1, 2, length), lambda p, low, place: (p + first, 0, 0))],
            scratch_shapes=[
                pltpu.VMEM((2, length, PAIR), jnp.bfloat16),
                pltpu.VMEM((2, length, PAIR), jnp.bfloat16),
            ],
        ),
        out_shape=[flat_shape] * 4
        + [jax.ShapeDtypeStruct((width // PAIR, 2, length), jnp.float32)],
        input_output_aliases={7 + ways + i: i for i in range(len(held))},
        compiler_params=pltpu.CompilerParams(vmem_limit_bytes=48 * 2**20),
        name="attend",
    )(lows, places, *projected, bias[None, :], cos_wide, sin_wide,
      start_wide, valid_wide, *held)


def attend_back_kernel(
    low_ref, place_ref, dos, q_ref, k_ref, v_ref, lse_ref, cos_ref, sin_ref, start_ref, valid_ref,
    grad_ref, sums_ref, qm, km, vm, dom, do_scr, dk_acc, dv_acc,
):
    length = q_ref.shape[0]
    blocks = length // BLOCK
    scale = 1.0 / math.sqrt(HEAD_DIM)

    def split(i, _):
        rows = pl.ds(pl.multiple_of(i * BLOCK, BLOCK), BLOCK)
        qm[0, rows, :], qm[1, rows, :] = halves(q_ref[rows, :])
        km[0, rows, :], km[1, rows, :] = halves(k_ref[rows, :])
        vm[0, rows, :], vm[1, rows, :] = halves(v_ref[rows, :])
        dk_acc[rows, :] = jnp.zeros((BLOCK, PAIR), jnp.float32)
        dv_acc[rows, :] = jnp.zeros((BLOCK, PAIR), jnp.float32)
        return 0

    lax.fori_loop(0, blocks, split, 0)

    per = length // len(dos) // BLOCK
    for slot in range(len(dos)):
        for i in range(per):
            rows = pl.ds(pl.multiple_of(place_ref[slot * per + i] * BLOCK, BLOCK), BLOCK)
            do = dos[slot][i * BLOCK : (i + 1) * BLOCK, :].astype(jnp.float32)
            do = (do * valid_ref[rows, :]).astype(jnp.bfloat16)
            do_scr[rows, :] = do
            dom[0, rows, :], dom[1, rows, :] = halves(do)

    def query_block(i, count):
        rows = pl.ds(pl.multiple_of(i * BLOCK, BLOCK), BLOCK)
        base = pl.multiple_of((i + 1 - count) * BLOCK, BLOCK)
        cols = pl.ds(base, count * BLOCK)
        shape = (count * BLOCK, BLOCK)
        q = q_ref[rows, :]
        do = do_scr[rows, :]
        start = start_ref[:, rows] - base
        kpos = lax.broadcasted_iota(jnp.int32, shape, 0)
        qpos = lax.broadcasted_iota(jnp.int32, shape, 1) + (count - 1) * BLOCK
        allowed = (kpos >= start) & (kpos <= qpos)
        dk = dk_acc[cols, :]
        dv = dv_acc[cols, :]
        dq = jnp.zeros((BLOCK, PAIR), jnp.float32)
        for h in range(2):
            s = nt(km[h, cols, :], q)
            p = jnp.where(allowed, jnp.exp(s - lse_ref[0, h : h + 1, rows]), 0.0)
            dp = nt(vm[h, cols, :], do)
            delta = jnp.sum(p * dp, axis=0, keepdims=True)
            dv = dv + nn(p.astype(jnp.bfloat16), dom[h, rows, :])
            ds = (p * (dp - delta)).astype(jnp.bfloat16)
            dk = dk + nn(ds, qm[h, rows, :])
            dq = dq + tn(ds, km[h, cols, :])
        dk_acc[cols, :] = dk
        dv_acc[cols, :] = dv
        dq = turn(dq * scale, cos_ref[rows, :], -sin_ref[rows, :]).astype(jnp.bfloat16)
        there = pl.ds(pl.multiple_of(place_ref[i] * BLOCK, BLOCK), BLOCK)
        grad_ref[there, :PAIR] = dq
        sums_ref[0] += jnp.sum(dq.astype(jnp.float32), axis=0, keepdims=True)

    none = jnp.zeros((1, PAIR), jnp.float32)
    sums_ref[0] = none

    def step(i, _):
        for count in range(1, MOST + 1):
            pl.when(i + 1 - low_ref[i] == count)(functools.partial(query_block, i, count))
        return 0

    lax.fori_loop(0, blocks, step, 0)

    def finish(i, totals):
        rows = pl.ds(pl.multiple_of(i * BLOCK, BLOCK), BLOCK)
        dk = turn(dk_acc[rows, :], cos_ref[rows, :], -sin_ref[rows, :]).astype(jnp.bfloat16)
        dv = dv_acc[rows, :].astype(jnp.bfloat16)
        there = pl.ds(pl.multiple_of(place_ref[i] * BLOCK, BLOCK), BLOCK)
        grad_ref[there, PAIR : 2 * PAIR] = dk
        grad_ref[there, 2 * PAIR :] = dv
        return (
            totals[0] + jnp.sum(dk.astype(jnp.float32), axis=0, keepdims=True),
            totals[1] + jnp.sum(dv.astype(jnp.float32), axis=0, keepdims=True),
        )

    sums_ref[1], sums_ref[2] = lax.fori_loop(0, blocks, finish, (none, none))


def attention_backward(q, k, v, do, lse, tables, first, count, held=None):
    cos_wide, sin_wide, starts, valid_wide, lows, places = tables
    length, width = q.shape
    blocks = length // BLOCK
    flat = pl.BlockSpec((length, PAIR), lambda p, low, place: (0, p + first))
    table = pl.BlockSpec((length, PAIR), lambda p, low, place: (0, 0))
    held = tuple(held or ())
    ways = len(do)

    def kernel(*refs):
        rest = refs[2 + ways :]
        attend_back_kernel(*refs[:2], refs[2 : 2 + ways], *rest[:8], *rest[8 + len(held) :])

    return pl.pallas_call(
        kernel,
        grid_spec=pltpu.PrefetchScalarGridSpec(
            num_scalar_prefetch=2,
            grid=(count,),
            in_specs=[
                *[pl.BlockSpec((length // ways, PAIR), lambda p, low, place: (0, p + first))] * ways,
                flat, flat, flat,
                pl.BlockSpec((1, 2, length), lambda p, low, place: (p + first, 0, 0)),
                table, table,
                pl.BlockSpec((1, length), lambda p, low, place: (0, 0)),
                table,
            ] + [pl.BlockSpec(memory_space=pl.ANY)] * len(held),
            out_specs=[
                pl.BlockSpec((length, 3 * PAIR), lambda p, low, place: (0, p + first)),
                pl.BlockSpec((3, 1, PAIR), lambda p, low, place: (0, 0, p + first)),
            ],
            scratch_shapes=[pltpu.VMEM((2, length, PAIR), jnp.bfloat16)] * 4
            + [pltpu.VMEM((length, PAIR), jnp.bfloat16)]
            + [pltpu.VMEM((length, PAIR), jnp.float32)] * 2,
        ),
        out_shape=[
            jax.ShapeDtypeStruct((length, 3 * width), jnp.bfloat16),
            jax.ShapeDtypeStruct((3, 1, width), jnp.float32),
        ],
        input_output_aliases={10 + ways + i: i for i in range(len(held))},
        compiler_params=pltpu.CompilerParams(vmem_limit_bytes=48 * 2**20),
        name="attend_back",
    )(lows, places, *do, q, k, v, lse, cos_wide, sin_wide, starts[None, :], valid_wide, *held)


def hidden_back_kernel(block_ref, weight_ref, slope_ref, *refs):
    grad = nt(block_ref[...], weight_ref[...])
    refs[-1][...] = (grad * slope_ref[...]).astype(jnp.bfloat16)


def hidden_back(block, weight, slope, place, ways, held=None):
    rows, model_width = block.shape
    hidden = weight.shape[0]
    tile = min(512, hidden)
    held = () if held is None else (held,)
    return pl.pallas_call(
        hidden_back_kernel,
        grid=(hidden // tile,),
        in_specs=[
            pl.BlockSpec((rows, model_width), lambda j: (0, 0)),
            pl.BlockSpec((tile, model_width), lambda j: (j, 0)),
            pl.BlockSpec((rows, tile), lambda j: (0, j)),
        ]
        + [pl.BlockSpec(memory_space=pl.ANY)] * len(held),
        out_specs=pl.BlockSpec((rows, tile), lambda j: (place, j)),
        out_shape=jax.ShapeDtypeStruct((ways * rows, hidden), jnp.bfloat16),
        input_output_aliases={3: 0} if held else {},
        compiler_params=pltpu.CompilerParams(vmem_limit_bytes=40 * 2**20),
        cost_estimate=pl.CostEstimate(
            flops=2 * rows * model_width * hidden,
            bytes_accessed=2 * hidden * model_width,
            transcendentals=0,
        ),
        name="hidden_back",
    )(block, weight, slope, *held)


def gelu_and_slope(u):
    tanh_value = jnp.tanh(GELU_C * (u + 0.044715 * u * u * u))
    value = 0.5 * u * (1.0 + tanh_value)
    slope = 0.5 * (1.0 + tanh_value) + 0.5 * u * (1.0 - tanh_value * tanh_value) * GELU_C * (
        1.0 + 3.0 * 0.044715 * u * u
    )
    return (value, slope)


def contract_rows(left, right):
    return lax.dot_general(
        left, right, (((0,), (0,)), ((), ())), preferred_element_type=jnp.float32
    )


def contract_cols(left, right):
    return lax.dot_general(
        left, right, (((1,), (1,)), ((), ())), preferred_element_type=jnp.float32
    )


def shift(x, pairs):
    return lax.ppermute(x, "tensor", pairs)


class LineGather:
    def __init__(self, x):
        self.up, self.down = [x], [x]

    def step(self):
        n, k = lax.axis_size("tensor"), len(self.up)
        self.up.append(shift(self.up[-1], [(i, i + 1) for i in range(k - 1, n - 1)]))
        self.down.append(shift(self.down[-1], [(i, i - 1) for i in range(1, n - k + 1)]))

    def block(self, k):
        n, me = lax.axis_size("tensor"), lax.axis_index("tensor")
        return jnp.where(me >= k, self.up[k], self.down[n - k]) if k else self.up[0]


class RingScatter:
    def __init__(self, parts, rows):
        self.parts, self.rows, self.k, self.up, self.down = list(parts), rows, 0, None, None

    def next(self):
        place = self.k * self.rows
        for part in self.parts:
            if place < part.shape[0]:
                return part[place : place + self.rows]
            place -= part.shape[0]

    def step(self):
        n, mine = lax.axis_size("tensor"), self.next()
        if self.k:
            mine = (mine.astype(jnp.float32) + self.up.astype(jnp.float32)).astype(jnp.bfloat16)
        self.up = shift(mine, [(i, (i + 1) % n) for i in range(n)])
        self.k += 1

    def total(self):
        return self.next().astype(jnp.float32) + self.up.astype(jnp.float32)


class LineScatter:
    def __init__(self, parts):
        self.parts, self.k, self.up, self.down = parts, 1, None, None

    def step(self):
        n, k = lax.axis_size("tensor"), self.k
        mine_up, mine_down = self.parts[k], self.parts[n - k]
        if k > 1:
            mine_up = mine_up.astype(jnp.float32) + self.up.astype(jnp.float32)
            mine_down = mine_down.astype(jnp.float32) + self.down.astype(jnp.float32)
        self.up = shift(mine_up.astype(jnp.bfloat16), [(i, i + 1) for i in range(k)])
        self.down = shift(mine_down.astype(jnp.bfloat16), [(i, i - 1) for i in range(n - k, n)])
        self.k = k + 1

    def total(self):
        return sum(x.astype(jnp.float32) for x in (self.parts[0], self.up, self.down))


def together(*moves, after=()):
    state = [
        (m.up[-1], m.down[-1]) if isinstance(m, LineGather) else (m.parts, m.up, m.down)
        for m in moves
    ]
    state, after = lax.optimization_barrier((state, after))
    for m, kept in zip(moves, state):
        if isinstance(m, LineGather):
            m.up[-1], m.down[-1] = kept
        else:
            m.parts, m.up, m.down = kept
    return after


def blocks_of(whole, n):
    rows = whole.shape[0] // n
    return [whole[k * rows : (k + 1) * rows] for k in range(n)]


def scatter_low(part, axis, dim):
    return lax.psum_scatter(
        part.astype(jnp.bfloat16), axis, scatter_dimension=dim, tiled=True
    )


def body(
    tokens,
    segments,
    norm_gain,
    norm_shift,
    qkv_weight,
    qkv_bias,
    dense_weight,
    up_weight,
    up_bias,
    down_weight,
    out_bias,
    cotangent,
):
    row_count, model_width = tokens.shape
    length = segments.shape[1]
    ways, copies = lax.axis_size("tensor"), lax.axis_size("dp")
    me = lax.axis_index("tensor")
    low = jnp.bfloat16
    resid = tokens.astype(jnp.float32)
    row_mean = jnp.mean(resid, axis=-1, keepdims=True)
    centered = resid - row_mean
    inverse = lax.rsqrt(jnp.mean(centered * centered, axis=-1, keepdims=True) + EPS)
    normed = centered * inverse
    normed_mine = (normed * norm_gain + norm_shift).astype(low)
    full_qkv = lax.all_gather(qkv_weight, "dp", axis=1, tiled=True)
    normed_mine, up_weight, down_weight, dense_weight = lax.optimization_barrier(
        (normed_mine, up_weight, down_weight, dense_weight)
    )
    full_up = lax.all_gather(up_weight, "dp", axis=0, tiled=True)
    full_down = lax.all_gather(down_weight, "dp", axis=1, tiled=True)
    full_dense = lax.all_gather(dense_weight, "dp", axis=1, tiled=True)
    around = [(i, (i + 1) % ways) for i in range(ways)]
    ring = [normed_mine, shift(normed_mine, around)]

    biases = jnp.concatenate([qkv_bias.reshape(-1), up_bias])
    biases = lax.all_gather(biases, "dp", axis=0).astype(jnp.float32)
    third = qkv_bias.shape[1]
    full_qbias = biases[:, : 3 * third].reshape(copies, 3, third)
    full_qbias = full_qbias.transpose(1, 0, 2).reshape(3, -1, PAIR).transpose(1, 0, 2).reshape(-1)
    full_ubias = biases[:, 3 * third :].reshape(-1)

    starts = segment_starts(segments)[0]
    cos_wide, sin_wide = rotary_wide(starts)
    valid_rows = (segments != 0).astype(jnp.float32).reshape(length, 1)
    valid_wide = jnp.broadcast_to(valid_rows, (length, PAIR))
    lows = starts[::BLOCK] // BLOCK
    chunk = jnp.arange(length // BLOCK, dtype=jnp.int32)
    per = row_count // BLOCK
    places = (me - 1 - chunk // per) % ways * per + chunk % per

    tables = (cos_wide, sin_wide, starts, valid_wide, lows, places)
    valid_mine = lax.dynamic_slice_in_dim(valid_rows, me * row_count, row_count, 0)
    cot_columns = jnp.sum(cotangent, axis=0, dtype=jnp.float32)
    resid_square = jnp.sum(valid_mine * resid * resid)
    fixed = lax.optimization_barrier
    ring[1], cot_mine, tables, full_qbias, full_ubias, cot_columns, resid_square = fixed(
        (ring[1], cotangent, tables, full_qbias, full_ubias, cot_columns, resid_square)
    )
    pairs = qkv_weight.shape[2] // PAIR
    sorted_qkv = full_qkv.reshape(3, model_width, pairs, PAIR).transpose(1, 2, 0, 3)
    sorted_qkv = sorted_qkv.reshape(model_width, 3 * pairs * PAIR)
    half = max(1, pairs // 2)
    projected, slopes, hidden_act, mlp_parts = ([None] * ways for _ in range(4))
    grad_context, grad_pre = [None] * ways, [None]

    def turned(blocks):
        return [*blocks[1:], blocks[0]]

    def project(k):
        projected[k] = jnp.dot(ring[k], sorted_qkv, preferred_element_type=jnp.float32)

    def widen(k):
        pre = jnp.dot(ring[k], full_up, preferred_element_type=jnp.float32) + full_ubias
        value, slopes[k] = gelu_and_slope(pre)
        hidden_act[k] = value.astype(low)

    def narrow(k):
        mlp_parts[k] = jnp.dot(
            hidden_act[k], full_down, preferred_element_type=jnp.float32
        ).astype(low)

    def context_back(k, block):
        grad_context[k] = contract_cols(block, full_dense).astype(low)

    def inner_back(k, block):
        grad_pre[0] = hidden_back(
            block, full_down, slopes[k], (k - 1) % ways, ways, held=grad_pre[0]
        )

    for k in range(2, ways):
        coming = shift(ring[k - 1], around)
        if k == 2:
            project(0)
            project(1)
        if k == ways - 1:
            for j in range(ways - 1):
                if projected[j] is None:
                    project(j)
                widen(j)
        coming, ring, projected, slopes, hidden_act, cot_mine = fixed(
            (coming, ring, projected, slopes, hidden_act, cot_mine)
        )
        ring.append(coming)

    cot = LineGather(cot_mine)
    cot.step()
    project(ways - 1)
    widen(ways - 1)
    for k in range(ways):
        narrow(k)
    ring, projected, slopes, hidden_act, mlp_parts = together(
        cot, after=(ring, projected, slopes, hidden_act, mlp_parts)
    )

    mlp = LineScatter(mlp_parts)
    while len(cot.up) < ways - 1:
        cot.step()
        mlp.step()
    attended = attention_forward(turned(projected), full_qbias, tables, 0, pairs)
    ring, attended, slopes, hidden_act, sorted_qkv = together(
        cot, mlp, after=(ring, attended, slopes, hidden_act, sorted_qkv)
    )
    query, keys, values, context_low, logsum = attended

    cot.step()
    mlp.step()
    for k in [0, *range(2, ways - 1)]:
        context_back(k, cot.block(k))
        inner_back(k, cot.block(k))
    acts = jnp.concatenate(turned(hidden_act), axis=0)
    attn_part = jnp.dot(context_low, full_dense, preferred_element_type=jnp.float32).astype(low)
    normed_low = jnp.concatenate(turned(ring), axis=0)
    grad_context, grad_pre, acts, slopes, attn_part, normed_low = together(
        cot, mlp, after=(grad_context, grad_pre, acts, slopes, attn_part, normed_low)
    )

    while mlp.k < ways:
        mlp.step()
    blocks = [cot.block(k) for k in range(ways)]
    late = sorted({1, ways - 1})
    for k in late:
        context_back(k, blocks[k])
    grad_full = jnp.concatenate(turned(blocks), axis=0)
    grad_down = contract_rows(acts, grad_full).astype(low)
    grad_context, attn_part, grad_full, grad_down, blocks, grad_pre, slopes = together(
        mlp, after=(grad_context, attn_part, grad_full, grad_down, blocks, grad_pre, slopes)
    )
    part_down = scatter_low(grad_down, "dp", 1)

    attn = RingScatter([attn_part], row_count)
    attn.step()
    grads = attention_backward(query, keys, values, turned(grad_context), logsum, tables, 0, half)
    inner_back(late[0], blocks[late[0]])
    grads, grad_context, grad_full, context_low, grad_pre, normed_low = together(
        attn, mlp, after=(grads, grad_context, grad_full, context_low, grad_pre, normed_low)
    )

    while attn.k < ways - 2:
        attn.step()
    if pairs > half:
        grads = attention_backward(
            query, keys, values, turned(grad_context), logsum, tables, half, pairs - half, held=grads
        )
    for k in late[1:]:
        inner_back(k, blocks[k])
    grad_dense = contract_rows(context_low, grad_full).astype(low)
    grads, grad_dense, grad_pre, normed_low, part_down = together(
        attn, mlp, after=(grads, grad_dense, grad_pre, normed_low, part_down)
    )
    part_dense = scatter_low(grad_dense, "dp", 1)
    grad_proj, grad_qbias = grads[0], grads[1][:, 0, :]
    [pre_full] = grad_pre

    def return_normed(low_block, high_block):
        rows = slice(low_block * row_count, high_block * row_count)
        part = contract_cols(pre_full[rows], full_up) + contract_cols(grad_proj[rows], sorted_qkv)
        return part.astype(low)

    attn.step()
    grad_qkv = contract_rows(normed_low, grad_proj).astype(low)
    grad_parts = [return_normed(0, ways // 2)]
    grad_parts, grad_qkv, pre_full, grad_proj, normed_low = together(
        attn, mlp, after=(grad_parts, grad_qkv, pre_full, grad_proj, normed_low)
    )
    part_qkv = scatter_low(grad_qkv, "dp", 0)

    last = RingScatter(grad_parts, row_count)
    last.step()
    last.parts.append(return_normed(ways // 2, ways))
    grad_up = contract_rows(normed_low, pre_full).astype(low)
    grad_up, pre_full, part_dense = together(
        last, attn, mlp, after=(grad_up, pre_full, part_dense)
    )
    part_up = scatter_low(grad_up, "dp", 0)
    while last.k < ways - 2:
        last.step()
    grad_ubias = jnp.sum(pre_full, axis=0, dtype=jnp.float32)
    part_down, part_dense = part_down.astype(jnp.float32), part_dense.astype(jnp.float32)
    attn_mine, mlp_mine = attn.total(), mlp.total()
    attn_mine, mlp_mine, grad_ubias, part_down, part_dense, part_qkv = together(
        last, after=(attn_mine, mlp_mine, grad_ubias, part_down, part_dense, part_qkv)
    )
    part_qkv = part_qkv.astype(jnp.float32).reshape(-1, pairs, 3, PAIR)
    part_qkv = part_qkv.transpose(2, 0, 1, 3).reshape(3, -1, pairs * PAIR)
    last.step()
    output = (resid + attn_mine + mlp_mine + out_bias).astype(low)
    attn_square = jnp.sum(valid_mine * attn_mine * attn_mine)
    mlp_square = jnp.sum(valid_mine * mlp_mine * mlp_mine)
    part_up = part_up.astype(jnp.float32)
    output, attn_square, mlp_square, part_up, part_qkv = together(
        last, after=(output, attn_square, mlp_square, part_up, part_qkv)
    )
    grad_mine = last.total()
    scaled = grad_mine * norm_gain
    grad_tokens = (
        cotangent.astype(jnp.float32)
        + inverse
        * (
            scaled
            - jnp.mean(scaled, axis=-1, keepdims=True)
            - normed * jnp.mean(scaled * normed, axis=-1, keepdims=True)
        )
    ).astype(low)

    totals = jnp.stack(
        [resid_square, attn_square, mlp_square, jnp.sum(valid_mine) * model_width]
    )
    columns = jnp.stack(
        [
            jnp.sum(grad_mine * normed, axis=0),
            jnp.sum(grad_mine, axis=0),
            cot_columns,
        ]
    )
    peers = copies * ways
    share = model_width // peers
    columns = columns.reshape(3, peers, share).transpose(1, 0, 2).reshape(peers, 3 * share)
    own_bias = jnp.concatenate(
        [
            grad_qbias.reshape(3, copies, third).transpose(1, 0, 2).reshape(copies, 3 * third),
            grad_ubias.reshape(copies, -1),
        ],
        axis=1,
    )
    same = (jnp.arange(ways) == me).astype(jnp.float32)[None, :, None]
    own_bias = (own_bias[:, None, :] * same).reshape(peers, -1)
    small = jnp.concatenate(
        [columns, own_bias, jnp.broadcast_to(totals, (peers, 4))], axis=1
    )
    small = jnp.sum(lax.all_to_all(small, ("dp", "tensor"), 0, 0, tiled=True), axis=0)
    part_gain, part_shift, part_obias = small[: 3 * share].reshape(3, share)
    part_qbias = small[3 * share : 3 * share + 3 * third].reshape(3, third)
    part_ubias = small[3 * share + 3 * third : -4]
    root_squares = jnp.sqrt(small[-4:-1] / small[-1])
    return (
        output,
        grad_tokens,
        part_gain,
        part_shift,
        part_qkv,
        part_qbias,
        part_dense,
        part_up,
        part_ubias,
        part_down,
        part_obias,
        root_squares,
    )


def solution(mesh):
    placed = (
        P(("dp", "tensor"), None),
        P("dp", None),
        P(),
        P(),
        P(None, "dp", "tensor"),
        P(None, ("tensor", "dp")),
        P("tensor", "dp"),
        P("dp", "tensor"),
        P(("tensor", "dp")),
        P("tensor", "dp"),
        P(),
        P(("dp", "tensor"), None),
    )
    return jax.shard_map(
        body,
        mesh=mesh,
        in_specs=placed,
        out_specs=(
            P(("dp", "tensor"), None),
            P(("dp", "tensor"), None),
            P(("dp", "tensor")),
            P(("dp", "tensor")),
            P(None, "dp", "tensor"),
            P(None, ("tensor", "dp")),
            P("tensor", "dp"),
            P("dp", "tensor"),
            P(("tensor", "dp")),
            P("tensor", "dp"),
            P(("dp", "tensor")),
            P(),
        ),
        check_vma=False,
    )
```

```python
import functools
import math

import jax
import jax.numpy as jnp
from jax import lax
from jax.experimental import pallas as pl
from jax.experimental.pallas import tpu as pltpu
from jax.sharding import PartitionSpec as P

HEAD_DIM = 64
ROT = 32
PAIR = 2 * HEAD_DIM
BLOCK = 256
MOST = 5

EPS = 1e-05
GELU_C = math.sqrt(2.0 / math.pi)


def segment_starts(segs):
    return jnp.sum((segs[:, None, :] < segs[:, :, None]).astype(jnp.int32), axis=-1)


def rotary_wide(starts):
    length = starts.shape[0]
    half_rot = ROT // 2
    frequency = jnp.exp(-math.log(10000.0) * (2.0 * jnp.arange(half_rot, dtype=jnp.float32) / ROT))
    position = jnp.arange(length, dtype=jnp.int32) - starts
    angles = position.astype(jnp.float32)[:, None] * frequency
    cosines, sines = jnp.cos(angles), jnp.sin(angles)
    ones = jnp.ones((length, HEAD_DIM - ROT), jnp.float32)
    cos_head = jnp.concatenate([cosines, cosines, ones], axis=-1)
    sin_head = jnp.concatenate([-sines, sines, 0.0 * ones], axis=-1)
    return (jnp.concatenate([cos_head, cos_head], -1), jnp.concatenate([sin_head, sin_head], -1))


def turn(x, cos_wide, sin_wide):
    lane = lax.broadcasted_iota(jnp.int32, x.shape, 1) % HEAD_DIM
    half_rot = ROT // 2
    partner = jnp.where(
        lane < half_rot, pltpu.roll(x, PAIR - half_rot, 1), pltpu.roll(x, half_rot, 1)
    )
    return x * cos_wide + partner * sin_wide


def first_half(shape):
    return lax.broadcasted_iota(jnp.int32, shape, len(shape) - 1) < HEAD_DIM


def halves(x):
    front = first_half(x.shape)
    zero = jnp.zeros_like(x)
    return (jnp.where(front, x, zero), jnp.where(front, zero, x))


def nt(left, right):
    return lax.dot_general(
        left, right, (((1,), (1,)), ((), ())), preferred_element_type=jnp.float32
    )


def nn(left, right):
    return lax.dot_general(
        left, right, (((1,), (0,)), ((), ())), preferred_element_type=jnp.float32
    )


def tn(left, right):
    return lax.dot_general(
        left, right, (((0,), (0,)), ((), ())), preferred_element_type=jnp.float32
    )


def attend_kernel(
    low_ref, place_ref, parts, bias_ref, cos_ref, sin_ref, start_ref, valid_ref,
    q_ref, k_ref, v_ref, ctx_ref, lse_ref, km, vm,
):
    length = q_ref.shape[0]
    blocks = length // BLOCK
    scale = 1.0 / math.sqrt(HEAD_DIM)

    per = length // len(parts) // BLOCK

    def project(i, slot):
        rows = pl.ds(pl.multiple_of(place_ref[slot * per + i] * BLOCK, BLOCK), BLOCK)
        here = pl.ds(i * BLOCK, BLOCK)
        part = parts[slot]
        cw, sw = cos_ref[rows, :], sin_ref[rows, :]
        x = part[here, :] + bias_ref[...]
        q = turn(x[:, :PAIR], cw, sw).astype(jnp.bfloat16)
        q_ref[rows, :] = q * jnp.bfloat16(scale)
        k = turn(x[:, PAIR : 2 * PAIR], cw, sw).astype(jnp.bfloat16)
        k_ref[rows, :] = k
        v = x[:, 2 * PAIR :].astype(jnp.bfloat16)
        v_ref[rows, :] = v
        km[0, rows, :], km[1, rows, :] = halves(k)
        vm[0, rows, :], vm[1, rows, :] = halves(v)

    for slot in range(len(parts)):
        for i in range(per):
            project(i, slot)

    def query_block(i, count):
        rows = pl.ds(pl.multiple_of(i * BLOCK, BLOCK), BLOCK)
        base = pl.multiple_of((i + 1 - count) * BLOCK, BLOCK)
        cols = pl.ds(base, count * BLOCK)
        shape = (BLOCK, count * BLOCK)
        q = q_ref[rows, :]
        start = start_ref[rows, :][:, :1] - base
        kpos = lax.broadcasted_iota(jnp.int32, shape, 1)
        qpos = lax.broadcasted_iota(jnp.int32, shape, 0) + (count - 1) * BLOCK
        allowed = (kpos >= start) & (kpos <= qpos)
        there = pl.ds(pl.multiple_of(place_ref[i] * BLOCK, BLOCK), BLOCK)
        acc = jnp.zeros((BLOCK, PAIR), jnp.float32)
        tops, sums = [], []
        for h in range(2):
            s = jnp.where(allowed, nt(q, km[h, cols, :]), -jnp.inf)
            top = jnp.max(s, axis=-1, keepdims=True)
            e = jnp.exp(s - top)
            tops.append(top)
            sums.append(jnp.sum(e, axis=-1, keepdims=True))
            acc = acc + nn(e.astype(jnp.bfloat16), vm[h, cols, :])
        front = first_half((BLOCK, PAIR))
        out = acc / jnp.where(front, sums[0], sums[1])
        ctx_ref[there, :] = (out * valid_ref[rows, :]).astype(jnp.bfloat16)
        lse = jnp.where(front, tops[0] + jnp.log(sums[0]), tops[1] + jnp.log(sums[1]))
        lse_t = lse.T
        lse_ref[0, 0:1, rows] = lse_t[0:1, :]
        lse_ref[0, 1:2, rows] = lse_t[HEAD_DIM : HEAD_DIM + 1, :]

    def step(i, _):
        for count in range(1, MOST + 1):
            pl.when(i + 1 - low_ref[i] == count)(functools.partial(query_block, i, count))
        return 0

    lax.fori_loop(0, blocks, step, 0)


def attention_forward(projected, bias, tables, first, count, held=None):
    cos_wide, sin_wide, starts, valid_wide, lows, places = tables
    width = projected[0].shape[1] // 3
    length = starts.shape[0]
    blocks = length // BLOCK
    ways = len(projected)
    start_wide = jnp.broadcast_to(starts[:, None], (length, PAIR))
    part = pl.BlockSpec((length // ways, 3 * PAIR), lambda p, low, place: (0, p + first))
    table = pl.BlockSpec((length, PAIR), lambda p, low, place: (0, 0))
    flat = pl.BlockSpec((length, PAIR), lambda p, low, place: (0, p + first))
    flat_shape = jax.ShapeDtypeStruct((length, width), jnp.bfloat16)
    held = tuple(held or ())

    def kernel(*refs):
        rest = refs[2 + ways :]
        attend_kernel(*refs[:2], refs[2 : 2 + ways], *rest[:5], *rest[5 + len(held) :])

    return pl.pallas_call(
        kernel,
        grid_spec=pltpu.PrefetchScalarGridSpec(
            num_scalar_prefetch=2,
            grid=(count,),
            in_specs=[
                *[part] * ways,
                pl.BlockSpec((1, 3 * PAIR), lambda p, low, place: (0, p + first)),
                table, table, table, table,
            ] + [pl.BlockSpec(memory_space=pl.ANY)] * len(held),
            out_specs=[flat, flat, flat, flat,
                       pl.BlockSpec((1, 2, length), lambda p, low, place: (p + first, 0, 0))],
            scratch_shapes=[
                pltpu.VMEM((2, length, PAIR), jnp.bfloat16),
                pltpu.VMEM((2, length, PAIR), jnp.bfloat16),
            ],
        ),
        out_shape=[flat_shape] * 4
        + [jax.ShapeDtypeStruct((width // PAIR, 2, length), jnp.float32)],
        input_output_aliases={7 + ways + i: i for i in range(len(held))},
        compiler_params=pltpu.CompilerParams(vmem_limit_bytes=48 * 2**20),
        name="attend",
    )(lows, places, *projected, bias[None, :], cos_wide, sin_wide,
      start_wide, valid_wide, *held)


def attend_back_kernel(
    low_ref, place_ref, dos, q_ref, k_ref, v_ref, lse_ref, cos_ref, sin_ref, start_ref, valid_ref,
    grad_ref, sums_ref, qm, km, vm, dom, do_scr, dk_acc, dv_acc,
):
    length = q_ref.shape[0]
    blocks = length // BLOCK
    scale = 1.0 / math.sqrt(HEAD_DIM)

    def split(i, _):
        rows = pl.ds(pl.multiple_of(i * BLOCK, BLOCK), BLOCK)
        qm[0, rows, :], qm[1, rows, :] = halves(q_ref[rows, :])
        km[0, rows, :], km[1, rows, :] = halves(k_ref[rows, :])
        vm[0, rows, :], vm[1, rows, :] = halves(v_ref[rows, :])
        dk_acc[rows, :] = jnp.zeros((BLOCK, PAIR), jnp.float32)
        dv_acc[rows, :] = jnp.zeros((BLOCK, PAIR), jnp.float32)
        return 0

    lax.fori_loop(0, blocks, split, 0)

    per = length // len(dos) // BLOCK
    for slot in range(len(dos)):
        for i in range(per):
            rows = pl.ds(pl.multiple_of(place_ref[slot * per + i] * BLOCK, BLOCK), BLOCK)
            do = dos[slot][i * BLOCK : (i + 1) * BLOCK, :].astype(jnp.float32)
            do = (do * valid_ref[rows, :]).astype(jnp.bfloat16)
            do_scr[rows, :] = do
            dom[0, rows, :], dom[1, rows, :] = halves(do)

    def query_block(i, count):
        rows = pl.ds(pl.multiple_of(i * BLOCK, BLOCK), BLOCK)
        base = pl.multiple_of((i + 1 - count) * BLOCK, BLOCK)
        cols = pl.ds(base, count * BLOCK)
        shape = (count * BLOCK, BLOCK)
        q = q_ref[rows, :]
        do = do_scr[rows, :]
        start = start_ref[:, rows] - base
        kpos = lax.broadcasted_iota(jnp.int32, shape, 0)
        qpos = lax.broadcasted_iota(jnp.int32, shape, 1) + (count - 1) * BLOCK
        allowed = (kpos >= start) & (kpos <= qpos)
        dk = dk_acc[cols, :]
        dv = dv_acc[cols, :]
        dq = jnp.zeros((BLOCK, PAIR), jnp.float32)
        for h in range(2):
            s = nt(km[h, cols, :], q)
            p = jnp.where(allowed, jnp.exp(s - lse_ref[0, h : h + 1, rows]), 0.0)
            dp = nt(vm[h, cols, :], do)
            delta = jnp.sum(p * dp, axis=0, keepdims=True)
            dv = dv + nn(p.astype(jnp.bfloat16), dom[h, rows, :])
            ds = (p * (dp - delta)).astype(jnp.bfloat16)
            dk = dk + nn(ds, qm[h, rows, :])
            dq = dq + tn(ds, km[h, cols, :])
        dk_acc[cols, :] = dk
        dv_acc[cols, :] = dv
        dq = turn(dq * scale, cos_ref[rows, :], -sin_ref[rows, :]).astype(jnp.bfloat16)
        there = pl.ds(pl.multiple_of(place_ref[i] * BLOCK, BLOCK), BLOCK)
        grad_ref[there, :PAIR] = dq
        sums_ref[0] += jnp.sum(dq.astype(jnp.float32), axis=0, keepdims=True)

    none = jnp.zeros((1, PAIR), jnp.float32)
    sums_ref[0] = none

    def step(i, _):
        for count in range(1, MOST + 1):
            pl.when(i + 1 - low_ref[i] == count)(functools.partial(query_block, i, count))
        return 0

    lax.fori_loop(0, blocks, step, 0)

    def finish(i, totals):
        rows = pl.ds(pl.multiple_of(i * BLOCK, BLOCK), BLOCK)
        dk = turn(dk_acc[rows, :], cos_ref[rows, :], -sin_ref[rows, :]).astype(jnp.bfloat16)
        dv = dv_acc[rows, :].astype(jnp.bfloat16)
        there = pl.ds(pl.multiple_of(place_ref[i] * BLOCK, BLOCK), BLOCK)
        grad_ref[there, PAIR : 2 * PAIR] = dk
        grad_ref[there, 2 * PAIR :] = dv
        return (
            totals[0] + jnp.sum(dk.astype(jnp.float32), axis=0, keepdims=True),
            totals[1] + jnp.sum(dv.astype(jnp.float32), axis=0, keepdims=True),
        )

    sums_ref[1], sums_ref[2] = lax.fori_loop(0, blocks, finish, (none, none))


def attention_backward(q, k, v, do, lse, tables, first, count, held=None):
    cos_wide, sin_wide, starts, valid_wide, lows, places = tables
    length, width = q.shape
    blocks = length // BLOCK
    flat = pl.BlockSpec((length, PAIR), lambda p, low, place: (0, p + first))
    table = pl.BlockSpec((length, PAIR), lambda p, low, place: (0, 0))
    held = tuple(held or ())
    ways = len(do)

    def kernel(*refs):
        rest = refs[2 + ways :]
        attend_back_kernel(*refs[:2], refs[2 : 2 + ways], *rest[:8], *rest[8 + len(held) :])

    return pl.pallas_call(
        kernel,
        grid_spec=pltpu.PrefetchScalarGridSpec(
            num_scalar_prefetch=2,
            grid=(count,),
            in_specs=[
                *[pl.BlockSpec((length // ways, PAIR), lambda p, low, place: (0, p + first))] * ways,
                flat, flat, flat,
                pl.BlockSpec((1, 2, length), lambda p, low, place: (p + first, 0, 0)),
                table, table,
                pl.BlockSpec((1, length), lambda p, low, place: (0, 0)),
                table,
            ] + [pl.BlockSpec(memory_space=pl.ANY)] * len(held),
            out_specs=[
                pl.BlockSpec((length, 3 * PAIR), lambda p, low, place: (0, p + first)),
                pl.BlockSpec((3, 1, PAIR), lambda p, low, place: (0, 0, p + first)),
            ],
            scratch_shapes=[pltpu.VMEM((2, length, PAIR), jnp.bfloat16)] * 4
            + [pltpu.VMEM((length, PAIR), jnp.bfloat16)]
            + [pltpu.VMEM((length, PAIR), jnp.float32)] * 2,
        ),
        out_shape=[
            jax.ShapeDtypeStruct((length, 3 * width), jnp.bfloat16),
            jax.ShapeDtypeStruct((3, 1, width), jnp.float32),
        ],
        input_output_aliases={10 + ways + i: i for i in range(len(held))},
        compiler_params=pltpu.CompilerParams(vmem_limit_bytes=48 * 2**20),
        name="attend_back",
    )(lows, places, *do, q, k, v, lse, cos_wide, sin_wide, starts[None, :], valid_wide, *held)


def hidden_back_kernel(block_ref, weight_ref, slope_ref, *refs):
    grad = nt(block_ref[...], weight_ref[...])
    refs[-1][...] = (grad * slope_ref[...]).astype(jnp.bfloat16)


def hidden_back(block, weight, slope, place, ways, held=None):
    rows, model_width = block.shape
    hidden = weight.shape[0]
    tile = min(512, hidden)
    held = () if held is None else (held,)
    return pl.pallas_call(
        hidden_back_kernel,
        grid=(hidden // tile,),
        in_specs=[
            pl.BlockSpec((rows, model_width), lambda j: (0, 0)),
            pl.BlockSpec((tile, model_width), lambda j: (j, 0)),
            pl.BlockSpec((rows, tile), lambda j: (0, j)),
        ]
        + [pl.BlockSpec(memory_space=pl.ANY)] * len(held),
        out_specs=pl.BlockSpec((rows, tile), lambda j: (place, j)),
        out_shape=jax.ShapeDtypeStruct((ways * rows, hidden), jnp.bfloat16),
        input_output_aliases={3: 0} if held else {},
        compiler_params=pltpu.CompilerParams(vmem_limit_bytes=40 * 2**20),
        cost_estimate=pl.CostEstimate(
            flops=2 * rows * model_width * hidden,
            bytes_accessed=2 * hidden * model_width,
            transcendentals=0,
        ),
        name="hidden_back",
    )(block, weight, slope, *held)


def columns_back_kernel(part_ref, out_ref):
    for c in range(3):
        out_ref[c] = part_ref[:, c * PAIR : (c + 1) * PAIR].astype(jnp.float32)


def columns_back(part):
    rows, width = part.shape
    return pl.pallas_call(
        columns_back_kernel,
        grid=(width // (3 * PAIR),),
        in_specs=[pl.BlockSpec((rows, 3 * PAIR), lambda p: (0, p))],
        out_specs=pl.BlockSpec((3, rows, PAIR), lambda p: (0, 0, p)),
        out_shape=jax.ShapeDtypeStruct((3, rows, width // 3), jnp.float32),
        name="columns_back",
    )(part)


def gelu_and_slope(u):
    tanh_value = jnp.tanh(GELU_C * (u + 0.044715 * u * u * u))
    value = 0.5 * u * (1.0 + tanh_value)
    slope = 0.5 * (1.0 + tanh_value) + 0.5 * u * (1.0 - tanh_value * tanh_value) * GELU_C * (
        1.0 + 3.0 * 0.044715 * u * u
    )
    return (value, slope)


def contract_rows(left, right):
    return lax.dot_general(
        left, right, (((0,), (0,)), ((), ())), preferred_element_type=jnp.float32
    )


def contract_cols(left, right):
    return lax.dot_general(
        left, right, (((1,), (1,)), ((), ())), preferred_element_type=jnp.float32
    )


def shift(x, pairs):
    return lax.ppermute(x, "tensor", pairs)


class LineGather:
    def __init__(self, x):
        self.up, self.down = [x], [x]

    def step(self):
        n, k = lax.axis_size("tensor"), len(self.up)
        self.up.append(shift(self.up[-1], [(i, i + 1) for i in range(k - 1, n - 1)]))
        self.down.append(shift(self.down[-1], [(i, i - 1) for i in range(1, n - k + 1)]))

    def block(self, k):
        n, me = lax.axis_size("tensor"), lax.axis_index("tensor")
        return jnp.where(me >= k, self.up[k], self.down[n - k]) if k else self.up[0]


class RingScatter:
    def __init__(self, parts, rows):
        self.parts, self.rows, self.k, self.up, self.down = list(parts), rows, 0, None, None

    def next(self):
        place = self.k * self.rows
        for part in self.parts:
            if place < part.shape[0]:
                return part[place : place + self.rows]
            place -= part.shape[0]

    def step(self):
        n, mine = lax.axis_size("tensor"), self.next()
        if self.k:
            mine = (mine.astype(jnp.float32) + self.up.astype(jnp.float32)).astype(jnp.bfloat16)
        self.up = shift(mine, [(i, (i + 1) % n) for i in range(n)])
        self.k += 1

    def total(self):
        return self.next().astype(jnp.float32) + self.up.astype(jnp.float32)


class LineScatter:
    def __init__(self, parts):
        self.parts, self.k, self.up, self.down = parts, 1, None, None

    def step(self):
        n, k = lax.axis_size("tensor"), self.k
        mine_up, mine_down = self.parts[k], self.parts[n - k]
        if k > 1:
            mine_up = mine_up.astype(jnp.float32) + self.up.astype(jnp.float32)
            mine_down = mine_down.astype(jnp.float32) + self.down.astype(jnp.float32)
        self.up = shift(mine_up.astype(jnp.bfloat16), [(i, i + 1) for i in range(k)])
        self.down = shift(mine_down.astype(jnp.bfloat16), [(i, i - 1) for i in range(n - k, n)])
        self.k = k + 1

    def total(self):
        return sum(x.astype(jnp.float32) for x in (self.parts[0], self.up, self.down))


def together(*moves, after=()):
    state = [
        (m.up[-1], m.down[-1]) if isinstance(m, LineGather) else (m.parts, m.up, m.down)
        for m in moves
    ]
    state, after = lax.optimization_barrier((state, after))
    for m, kept in zip(moves, state):
        if isinstance(m, LineGather):
            m.up[-1], m.down[-1] = kept
        else:
            m.parts, m.up, m.down = kept
    return after


def blocks_of(whole, n):
    rows = whole.shape[0] // n
    return [whole[k * rows : (k + 1) * rows] for k in range(n)]


def scatter_low(part, axis, dim):
    return lax.psum_scatter(
        part.astype(jnp.bfloat16), axis, scatter_dimension=dim, tiled=True
    )


def body(
    tokens,
    segments,
    norm_gain,
    norm_shift,
    qkv_weight,
    qkv_bias,
    dense_weight,
    up_weight,
    up_bias,
    down_weight,
    out_bias,
    cotangent,
):
    row_count, model_width = tokens.shape
    length = segments.shape[1]
    ways, copies = lax.axis_size("tensor"), lax.axis_size("dp")
    me = lax.axis_index("tensor")
    low = jnp.bfloat16
    resid = tokens.astype(jnp.float32)
    row_mean = jnp.mean(resid, axis=-1, keepdims=True)
    centered = resid - row_mean
    inverse = lax.rsqrt(jnp.mean(centered * centered, axis=-1, keepdims=True) + EPS)
    normed = centered * inverse
    normed_mine = (normed * norm_gain + norm_shift).astype(low)
    full_qkv = lax.all_gather(qkv_weight, "dp", axis=1, tiled=True)
    normed_mine, up_weight, down_weight, dense_weight = lax.optimization_barrier(
        (normed_mine, up_weight, down_weight, dense_weight)
    )
    full_up = lax.all_gather(up_weight, "dp", axis=0, tiled=True)
    full_down = lax.all_gather(down_weight, "dp", axis=1, tiled=True)
    full_dense = lax.all_gather(dense_weight, "dp", axis=1, tiled=True)
    around = [(i, (i + 1) % ways) for i in range(ways)]
    ring = [normed_mine, shift(normed_mine, around)]

    biases = jnp.concatenate([qkv_bias.reshape(-1), up_bias])
    biases = lax.all_gather(biases, "dp", axis=0).astype(jnp.float32)
    third = qkv_bias.shape[1]
    full_qbias = biases[:, : 3 * third].reshape(copies, 3, third)
    full_qbias = full_qbias.transpose(1, 0, 2).reshape(3, -1, PAIR).transpose(1, 0, 2).reshape(-1)
    full_ubias = biases[:, 3 * third :].reshape(-1)

    starts = segment_starts(segments)[0]
    cos_wide, sin_wide = rotary_wide(starts)
    valid_rows = (segments != 0).astype(jnp.float32).reshape(length, 1)
    valid_wide = jnp.broadcast_to(valid_rows, (length, PAIR))
    lows = starts[::BLOCK] // BLOCK
    chunk = jnp.arange(length // BLOCK, dtype=jnp.int32)
    per = row_count // BLOCK
    places = (me - 1 - chunk // per) % ways * per + chunk % per

    tables = (cos_wide, sin_wide, starts, valid_wide, lows, places)
    valid_mine = lax.dynamic_slice_in_dim(valid_rows, me * row_count, row_count, 0)
    cot_columns = jnp.sum(cotangent, axis=0, dtype=jnp.float32)
    resid_square = jnp.sum(valid_mine * resid * resid)
    fixed = lax.optimization_barrier
    ring[1], cot_mine, tables, full_qbias, full_ubias, cot_columns, resid_square = fixed(
        (ring[1], cotangent, tables, full_qbias, full_ubias, cot_columns, resid_square)
    )
    pairs = qkv_weight.shape[2] // PAIR
    sorted_qkv = full_qkv.reshape(3, model_width, pairs, PAIR).transpose(1, 2, 0, 3)
    sorted_qkv = sorted_qkv.reshape(model_width, 3 * pairs * PAIR)
    half = max(1, pairs // 2)
    projected, slopes, hidden_act, mlp_parts = ([None] * ways for _ in range(4))
    grad_context, grad_pre = [None] * ways, [None]

    def turned(blocks):
        return [*blocks[1:], blocks[0]]

    def project(k):
        projected[k] = jnp.dot(ring[k], sorted_qkv, preferred_element_type=jnp.float32)

    def widen(k):
        pre = jnp.dot(ring[k], full_up, preferred_element_type=jnp.float32) + full_ubias
        value, slopes[k] = gelu_and_slope(pre)
        hidden_act[k] = value.astype(low)

    def narrow(k):
        mlp_parts[k] = jnp.dot(
            hidden_act[k], full_down, preferred_element_type=jnp.float32
        ).astype(low)

    def context_back(k, block):
        grad_context[k] = contract_cols(block, full_dense).astype(low)

    def inner_back(k, block):
        grad_pre[0] = hidden_back(
            block, full_down, slopes[k], (k - 1) % ways, ways, held=grad_pre[0]
        )

    for k in range(2, ways):
        coming = shift(ring[k - 1], around)
        if k == 2:
            project(0)
            project(1)
        if k == ways - 1:
            for j in range(ways - 1):
                if projected[j] is None:
                    project(j)
                widen(j)
        coming, ring, projected, slopes, hidden_act, cot_mine = fixed(
            (coming, ring, projected, slopes, hidden_act, cot_mine)
        )
        ring.append(coming)

    cot = LineGather(cot_mine)
    cot.step()
    project(ways - 1)
    widen(ways - 1)
    for k in range(ways):
        narrow(k)
    ring, projected, slopes, hidden_act, mlp_parts = together(
        cot, after=(ring, projected, slopes, hidden_act, mlp_parts)
    )

    mlp = LineScatter(mlp_parts)
    while len(cot.up) < ways - 1:
        cot.step()
        mlp.step()
    attended = attention_forward(turned(projected), full_qbias, tables, 0, pairs)
    ring, attended, slopes, hidden_act, sorted_qkv, cot.up[0] = together(
        cot, mlp, after=(ring, attended, slopes, hidden_act, sorted_qkv, cot.up[0])
    )
    query, keys, values, context_low, logsum = attended

    cot.step()
    mlp.step()
    for k in [0, *range(2, ways - 1)]:
        context_back(k, cot.block(k))
        inner_back(k, cot.block(k))
    acts = jnp.concatenate(turned(hidden_act), axis=0)
    attn_part = [
        jnp.dot(rows, full_dense, preferred_element_type=jnp.float32).astype(low)
        for rows in (context_low[:row_count], context_low[row_count:])
    ]
    normed_low = jnp.concatenate(turned(ring), axis=0)
    grad_context, grad_pre, acts, slopes, attn_part, normed_low = together(
        cot, mlp, after=(grad_context, grad_pre, acts, slopes, attn_part, normed_low)
    )

    while mlp.k < ways:
        mlp.step()
    blocks = [cot.block(k) for k in range(ways)]
    late = sorted({1, ways - 1})
    for k in late:
        context_back(k, blocks[k])
    grad_full = jnp.concatenate(turned(blocks), axis=0)
    grad_down = contract_rows(acts, grad_full).astype(low)
    grad_context, attn_part, grad_full, grad_down, blocks, grad_pre, slopes = together(
        mlp, after=(grad_context, attn_part, grad_full, grad_down, blocks, grad_pre, slopes)
    )
    part_down = scatter_low(grad_down, "dp", 1)

    attn = RingScatter(attn_part, row_count)
    attn.step()
    grads = attention_backward(query, keys, values, turned(grad_context), logsum, tables, 0, half)
    inner_back(late[0], blocks[late[0]])
    grads, grad_context, grad_full, context_low, grad_pre, normed_low = together(
        attn, mlp, after=(grads, grad_context, grad_full, context_low, grad_pre, normed_low)
    )

    while attn.k < ways - 2:
        attn.step()
    if pairs > half:
        grads = attention_backward(
            query, keys, values, turned(grad_context), logsum, tables, half, pairs - half, held=grads
        )
    for k in late[1:]:
        inner_back(k, blocks[k])
    grad_dense = contract_rows(context_low, grad_full).astype(low)
    grads, grad_dense, grad_pre, normed_low, part_down = together(
        attn, mlp, after=(grads, grad_dense, grad_pre, normed_low, part_down)
    )
    part_dense = scatter_low(grad_dense, "dp", 1)
    grad_proj, grad_qbias = grads[0], grads[1][:, 0, :]
    [pre_full] = grad_pre

    def return_normed(low_block, high_block):
        rows = slice(low_block * row_count, high_block * row_count)
        part = contract_cols(pre_full[rows], full_up) + contract_cols(grad_proj[rows], sorted_qkv)
        return part.astype(low)

    attn.step()
    grad_qkv = contract_rows(normed_low, grad_proj).astype(low)
    grad_parts = [return_normed(0, 1)]
    grad_parts, grad_qkv, pre_full, grad_proj, normed_low = together(
        attn, mlp, after=(grad_parts, grad_qkv, pre_full, grad_proj, normed_low)
    )
    part_qkv = scatter_low(grad_qkv, "dp", 0)

    last = RingScatter(grad_parts, row_count)
    last.step()
    grad_up = contract_rows(normed_low, pre_full).astype(low)
    last.parts.append(return_normed(1, 2))
    grad_up, pre_full, grad_proj, part_dense = together(
        last, attn, mlp, after=(grad_up, pre_full, grad_proj, part_dense)
    )
    part_up = scatter_low(grad_up, "dp", 0)
    last.parts.append(return_normed(2, ways))
    while last.k < ways - 2:
        last.step()
    grad_ubias = jnp.sum(pre_full, axis=0, dtype=jnp.float32)
    attn_mine, mlp_mine = attn.total(), mlp.total()
    attn_mine, mlp_mine, grad_ubias, part_down, part_dense, part_qkv = together(
        last, after=(attn_mine, mlp_mine, grad_ubias, part_down, part_dense, part_qkv)
    )
    part_qkv = columns_back(part_qkv)
    part_down, part_dense = part_down.astype(jnp.float32), part_dense.astype(jnp.float32)
    last.step()
    output = (resid + attn_mine + mlp_mine + out_bias).astype(low)
    attn_square = jnp.sum(valid_mine * attn_mine * attn_mine)
    mlp_square = jnp.sum(valid_mine * mlp_mine * mlp_mine)
    part_up = part_up.astype(jnp.float32)
    output, attn_square, mlp_square, part_up, part_qkv, part_down, part_dense = together(
        last,
        after=(output, attn_square, mlp_square, part_up, part_qkv, part_down, part_dense),
    )
    grad_mine = last.total()
    scaled = grad_mine * norm_gain
    grad_tokens = (
        cotangent.astype(jnp.float32)
        + inverse
        * (
            scaled
            - jnp.mean(scaled, axis=-1, keepdims=True)
            - normed * jnp.mean(scaled * normed, axis=-1, keepdims=True)
        )
    ).astype(low)

    totals = jnp.stack(
        [resid_square, attn_square, mlp_square, jnp.sum(valid_mine) * model_width]
    )
    columns = jnp.stack(
        [
            jnp.sum(grad_mine * normed, axis=0),
            jnp.sum(grad_mine, axis=0),
            cot_columns,
        ]
    )
    peers = copies * ways
    share = model_width // peers
    columns = columns.reshape(3, peers, share).transpose(1, 0, 2).reshape(peers, 3 * share)
    own_bias = jnp.concatenate(
        [
            grad_qbias.reshape(3, copies, third).transpose(1, 0, 2).reshape(copies, 3 * third),
            grad_ubias.reshape(copies, -1),
        ],
        axis=1,
    )
    same = (jnp.arange(ways) == me).astype(jnp.float32)[None, :, None]
    own_bias = (own_bias[:, None, :] * same).reshape(peers, -1)
    small = jnp.concatenate(
        [columns, own_bias, jnp.broadcast_to(totals, (peers, 4))], axis=1
    )
    small = jnp.sum(lax.all_to_all(small, ("dp", "tensor"), 0, 0, tiled=True), axis=0)
    part_gain, part_shift, part_obias = small[: 3 * share].reshape(3, share)
    part_qbias = small[3 * share : 3 * share + 3 * third].reshape(3, third)
    part_ubias = small[3 * share + 3 * third : -4]
    root_squares = jnp.sqrt(small[-4:-1] / small[-1])
    return (
        output,
        grad_tokens,
        part_gain,
        part_shift,
        part_qkv,
        part_qbias,
        part_dense,
        part_up,
        part_ubias,
        part_down,
        part_obias,
        root_squares,
    )


def solution(mesh):
    placed = (
        P(("dp", "tensor"), None),
        P("dp", None),
        P(),
        P(),
        P(None, "dp", "tensor"),
        P(None, ("tensor", "dp")),
        P("tensor", "dp"),
        P("dp", "tensor"),
        P(("tensor", "dp")),
        P("tensor", "dp"),
        P(),
        P(("dp", "tensor"), None),
    )
    return jax.shard_map(
        body,
        mesh=mesh,
        in_specs=placed,
        out_specs=(
            P(("dp", "tensor"), None),
            P(("dp", "tensor"), None),
            P(("dp", "tensor")),
            P(("dp", "tensor")),
            P(None, "dp", "tensor"),
            P(None, ("tensor", "dp")),
            P("tensor", "dp"),
            P("dp", "tensor"),
            P(("tensor", "dp")),
            P("tensor", "dp"),
            P(("dp", "tensor")),
            P(),
        ),
        check_vma=False,
    )
```

```python
import functools
import math

import jax
import jax.numpy as jnp
from jax import lax
from jax.experimental import pallas as pl
from jax.experimental.pallas import tpu as pltpu
from jax.sharding import PartitionSpec as P

HEAD_DIM = 64
ROT = 32
PAIR = 2 * HEAD_DIM
BLOCK = 256
MOST = 5

EPS = 1e-05
GELU_C = math.sqrt(2.0 / math.pi)


def segment_starts(segs):
    return jnp.sum((segs[:, None, :] < segs[:, :, None]).astype(jnp.int32), axis=-1)


def rotary_wide(starts):
    length = starts.shape[0]
    half_rot = ROT // 2
    frequency = jnp.exp(-math.log(10000.0) * (2.0 * jnp.arange(half_rot, dtype=jnp.float32) / ROT))
    position = jnp.arange(length, dtype=jnp.int32) - starts
    angles = position.astype(jnp.float32)[:, None] * frequency
    cosines, sines = jnp.cos(angles), jnp.sin(angles)
    ones = jnp.ones((length, HEAD_DIM - ROT), jnp.float32)
    cos_head = jnp.concatenate([cosines, cosines, ones], axis=-1)
    sin_head = jnp.concatenate([-sines, sines, 0.0 * ones], axis=-1)
    return (jnp.concatenate([cos_head, cos_head], -1), jnp.concatenate([sin_head, sin_head], -1))


def turn(x, cos_wide, sin_wide):
    lane = lax.broadcasted_iota(jnp.int32, x.shape, 1) % HEAD_DIM
    half_rot = ROT // 2
    partner = jnp.where(
        lane < half_rot, pltpu.roll(x, PAIR - half_rot, 1), pltpu.roll(x, half_rot, 1)
    )
    return x * cos_wide + partner * sin_wide


def first_half(shape):
    return lax.broadcasted_iota(jnp.int32, shape, len(shape) - 1) < HEAD_DIM


def halves(x):
    front = first_half(x.shape)
    zero = jnp.zeros_like(x)
    return (jnp.where(front, x, zero), jnp.where(front, zero, x))


def nt(left, right):
    return lax.dot_general(
        left, right, (((1,), (1,)), ((), ())), preferred_element_type=jnp.float32
    )


def nn(left, right):
    return lax.dot_general(
        left, right, (((1,), (0,)), ((), ())), preferred_element_type=jnp.float32
    )


def tn(left, right):
    return lax.dot_general(
        left, right, (((0,), (0,)), ((), ())), preferred_element_type=jnp.float32
    )


def attend_kernel(
    low_ref, place_ref, parts, bias_ref, cos_ref, sin_ref, start_ref, valid_ref,
    q_ref, k_ref, v_ref, ctx_ref, lse_ref, km, vm,
):
    length = q_ref.shape[0]
    blocks = length // BLOCK
    scale = 1.0 / math.sqrt(HEAD_DIM)

    per = length // len(parts) // BLOCK

    def project(i, slot):
        rows = pl.ds(pl.multiple_of(place_ref[slot * per + i] * BLOCK, BLOCK), BLOCK)
        here = pl.ds(i * BLOCK, BLOCK)
        part = parts[slot]
        cw, sw = cos_ref[rows, :], sin_ref[rows, :]
        x = part[here, :] + bias_ref[...]
        q = turn(x[:, :PAIR], cw, sw).astype(jnp.bfloat16)
        q_ref[rows, :] = q * jnp.bfloat16(scale)
        k = turn(x[:, PAIR : 2 * PAIR], cw, sw).astype(jnp.bfloat16)
        k_ref[rows, :] = k
        v = x[:, 2 * PAIR :].astype(jnp.bfloat16)
        v_ref[rows, :] = v
        km[0, rows, :], km[1, rows, :] = halves(k)
        vm[0, rows, :], vm[1, rows, :] = halves(v)

    for slot in range(len(parts)):
        for i in range(per):
            project(i, slot)

    def query_block(i, count):
        rows = pl.ds(pl.multiple_of(i * BLOCK, BLOCK), BLOCK)
        base = pl.multiple_of((i + 1 - count) * BLOCK, BLOCK)
        cols = pl.ds(base, count * BLOCK)
        shape = (BLOCK, count * BLOCK)
        q = q_ref[rows, :]
        start = start_ref[rows, :][:, :1] - base
        kpos = lax.broadcasted_iota(jnp.int32, shape, 1)
        qpos = lax.broadcasted_iota(jnp.int32, shape, 0) + (count - 1) * BLOCK
        allowed = (kpos >= start) & (kpos <= qpos)
        there = pl.ds(pl.multiple_of(place_ref[i] * BLOCK, BLOCK), BLOCK)
        acc = jnp.zeros((BLOCK, PAIR), jnp.float32)
        tops, sums = [], []
        for h in range(2):
            s = jnp.where(allowed, nt(q, km[h, cols, :]), -jnp.inf)
            top = jnp.max(s, axis=-1, keepdims=True)
            e = jnp.exp(s - top)
            tops.append(top)
            sums.append(jnp.sum(e, axis=-1, keepdims=True))
            acc = acc + nn(e.astype(jnp.bfloat16), vm[h, cols, :])
        front = first_half((BLOCK, PAIR))
        out = acc / jnp.where(front, sums[0], sums[1])
        ctx_ref[there, :] = (out * valid_ref[rows, :]).astype(jnp.bfloat16)
        lse = jnp.where(front, tops[0] + jnp.log(sums[0]), tops[1] + jnp.log(sums[1]))
        lse_t = lse.T
        lse_ref[0, 0:1, rows] = lse_t[0:1, :]
        lse_ref[0, 1:2, rows] = lse_t[HEAD_DIM : HEAD_DIM + 1, :]

    def step(i, _):
        for count in range(1, MOST + 1):
            pl.when(i + 1 - low_ref[i] == count)(functools.partial(query_block, i, count))
        return 0

    lax.fori_loop(0, blocks, step, 0)


def attention_forward(projected, bias, tables, first, count, held=None):
    cos_wide, sin_wide, starts, valid_wide, lows, places = tables
    width = projected[0].shape[1] // 3
    length = starts.shape[0]
    blocks = length // BLOCK
    ways = len(projected)
    start_wide = jnp.broadcast_to(starts[:, None], (length, PAIR))
    part = pl.BlockSpec((length // ways, 3 * PAIR), lambda p, low, place: (0, p + first))
    table = pl.BlockSpec((length, PAIR), lambda p, low, place: (0, 0))
    flat = pl.BlockSpec((length, PAIR), lambda p, low, place: (0, p + first))
    flat_shape = jax.ShapeDtypeStruct((length, width), jnp.bfloat16)
    held = tuple(held or ())

    def kernel(*refs):
        rest = refs[2 + ways :]
        attend_kernel(*refs[:2], refs[2 : 2 + ways], *rest[:5], *rest[5 + len(held) :])

    return pl.pallas_call(
        kernel,
        grid_spec=pltpu.PrefetchScalarGridSpec(
            num_scalar_prefetch=2,
            grid=(count,),
            in_specs=[
                *[part] * ways,
                pl.BlockSpec((1, 3 * PAIR), lambda p, low, place: (0, p + first)),
                table, table, table, table,
            ] + [pl.BlockSpec(memory_space=pl.ANY)] * len(held),
            out_specs=[flat, flat, flat, flat,
                       pl.BlockSpec((1, 2, length), lambda p, low, place: (p + first, 0, 0))],
            scratch_shapes=[
                pltpu.VMEM((2, length, PAIR), jnp.bfloat16),
                pltpu.VMEM((2, length, PAIR), jnp.bfloat16),
            ],
        ),
        out_shape=[flat_shape] * 4
        + [jax.ShapeDtypeStruct((width // PAIR, 2, length), jnp.float32)],
        input_output_aliases={7 + ways + i: i for i in range(len(held))},
        compiler_params=pltpu.CompilerParams(vmem_limit_bytes=48 * 2**20),
        name="attend",
    )(lows, places, *projected, bias[None, :], cos_wide, sin_wide,
      start_wide, valid_wide, *held)


def attend_back_kernel(
    low_ref, place_ref, dos, q_ref, k_ref, v_ref, lse_ref, cos_ref, sin_ref, start_ref, valid_ref,
    grad_ref, sums_ref, qm, km, vm, dom, do_scr, dk_acc, dv_acc,
):
    length = q_ref.shape[0]
    blocks = length // BLOCK
    scale = 1.0 / math.sqrt(HEAD_DIM)

    def split(i, _):
        rows = pl.ds(pl.multiple_of(i * BLOCK, BLOCK), BLOCK)
        qm[0, rows, :], qm[1, rows, :] = halves(q_ref[rows, :])
        km[0, rows, :], km[1, rows, :] = halves(k_ref[rows, :])
        vm[0, rows, :], vm[1, rows, :] = halves(v_ref[rows, :])
        dk_acc[rows, :] = jnp.zeros((BLOCK, PAIR), jnp.float32)
        dv_acc[rows, :] = jnp.zeros((BLOCK, PAIR), jnp.float32)
        return 0

    lax.fori_loop(0, blocks, split, 0)

    per = length // len(dos) // BLOCK
    for slot in range(len(dos)):
        for i in range(per):
            rows = pl.ds(pl.multiple_of(place_ref[slot * per + i] * BLOCK, BLOCK), BLOCK)
            do = dos[slot][i * BLOCK : (i + 1) * BLOCK, :].astype(jnp.float32)
            do = (do * valid_ref[rows, :]).astype(jnp.bfloat16)
            do_scr[rows, :] = do
            dom[0, rows, :], dom[1, rows, :] = halves(do)

    def query_block(i, count):
        rows = pl.ds(pl.multiple_of(i * BLOCK, BLOCK), BLOCK)
        base = pl.multiple_of((i + 1 - count) * BLOCK, BLOCK)
        cols = pl.ds(base, count * BLOCK)
        shape = (count * BLOCK, BLOCK)
        q = q_ref[rows, :]
        do = do_scr[rows, :]
        start = start_ref[:, rows] - base
        kpos = lax.broadcasted_iota(jnp.int32, shape, 0)
        qpos = lax.broadcasted_iota(jnp.int32, shape, 1) + (count - 1) * BLOCK
        allowed = (kpos >= start) & (kpos <= qpos)
        dk = dk_acc[cols, :]
        dv = dv_acc[cols, :]
        dq = jnp.zeros((BLOCK, PAIR), jnp.float32)
        for h in range(2):
            s = nt(km[h, cols, :], q)
            p = jnp.where(allowed, jnp.exp(s - lse_ref[0, h : h + 1, rows]), 0.0)
            dp = nt(vm[h, cols, :], do)
            delta = jnp.sum(p * dp, axis=0, keepdims=True)
            dv = dv + nn(p.astype(jnp.bfloat16), dom[h, rows, :])
            ds = (p * (dp - delta)).astype(jnp.bfloat16)
            dk = dk + nn(ds, qm[h, rows, :])
            dq = dq + tn(ds, km[h, cols, :])
        dk_acc[cols, :] = dk
        dv_acc[cols, :] = dv
        dq = turn(dq * scale, cos_ref[rows, :], -sin_ref[rows, :]).astype(jnp.bfloat16)
        there = pl.ds(pl.multiple_of(place_ref[i] * BLOCK, BLOCK), BLOCK)
        grad_ref[there, :PAIR] = dq
        sums_ref[0] += jnp.sum(dq.astype(jnp.float32), axis=0, keepdims=True)

    none = jnp.zeros((1, PAIR), jnp.float32)
    sums_ref[0] = none

    def step(i, _):
        for count in range(1, MOST + 1):
            pl.when(i + 1 - low_ref[i] == count)(functools.partial(query_block, i, count))
        return 0

    lax.fori_loop(0, blocks, step, 0)

    def finish(i, totals):
        rows = pl.ds(pl.multiple_of(i * BLOCK, BLOCK), BLOCK)
        dk = turn(dk_acc[rows, :], cos_ref[rows, :], -sin_ref[rows, :]).astype(jnp.bfloat16)
        dv = dv_acc[rows, :].astype(jnp.bfloat16)
        there = pl.ds(pl.multiple_of(place_ref[i] * BLOCK, BLOCK), BLOCK)
        grad_ref[there, PAIR : 2 * PAIR] = dk
        grad_ref[there, 2 * PAIR :] = dv
        return (
            totals[0] + jnp.sum(dk.astype(jnp.float32), axis=0, keepdims=True),
            totals[1] + jnp.sum(dv.astype(jnp.float32), axis=0, keepdims=True),
        )

    sums_ref[1], sums_ref[2] = lax.fori_loop(0, blocks, finish, (none, none))


def attention_backward(q, k, v, do, lse, tables, first, count, held=None):
    cos_wide, sin_wide, starts, valid_wide, lows, places = tables
    length, width = q.shape
    blocks = length // BLOCK
    flat = pl.BlockSpec((length, PAIR), lambda p, low, place: (0, p + first))
    table = pl.BlockSpec((length, PAIR), lambda p, low, place: (0, 0))
    held = tuple(held or ())
    ways = len(do)

    def kernel(*refs):
        rest = refs[2 + ways :]
        attend_back_kernel(*refs[:2], refs[2 : 2 + ways], *rest[:8], *rest[8 + len(held) :])

    return pl.pallas_call(
        kernel,
        grid_spec=pltpu.PrefetchScalarGridSpec(
            num_scalar_prefetch=2,
            grid=(count,),
            in_specs=[
                *[pl.BlockSpec((length // ways, PAIR), lambda p, low, place: (0, p + first))] * ways,
                flat, flat, flat,
                pl.BlockSpec((1, 2, length), lambda p, low, place: (p + first, 0, 0)),
                table, table,
                pl.BlockSpec((1, length), lambda p, low, place: (0, 0)),
                table,
            ] + [pl.BlockSpec(memory_space=pl.ANY)] * len(held),
            out_specs=[
                pl.BlockSpec((length, 3 * PAIR), lambda p, low, place: (0, p + first)),
                pl.BlockSpec((3, 1, PAIR), lambda p, low, place: (0, 0, p + first)),
            ],
            scratch_shapes=[pltpu.VMEM((2, length, PAIR), jnp.bfloat16)] * 4
            + [pltpu.VMEM((length, PAIR), jnp.bfloat16)]
            + [pltpu.VMEM((length, PAIR), jnp.float32)] * 2,
        ),
        out_shape=[
            jax.ShapeDtypeStruct((length, 3 * width), jnp.bfloat16),
            jax.ShapeDtypeStruct((3, 1, width), jnp.float32),
        ],
        input_output_aliases={10 + ways + i: i for i in range(len(held))},
        compiler_params=pltpu.CompilerParams(vmem_limit_bytes=48 * 2**20),
        name="attend_back",
    )(lows, places, *do, q, k, v, lse, cos_wide, sin_wide, starts[None, :], valid_wide, *held)


def hidden_back_kernel(block_ref, weight_ref, slope_ref, *refs):
    grad = nt(block_ref[...], weight_ref[...])
    refs[-1][...] = (grad * slope_ref[...]).astype(jnp.bfloat16)


def hidden_back(block, weight, slope, place, ways, held=None):
    rows, model_width = block.shape
    hidden = weight.shape[0]
    tile = min(512, hidden)
    held = () if held is None else (held,)
    return pl.pallas_call(
        hidden_back_kernel,
        grid=(hidden // tile,),
        in_specs=[
            pl.BlockSpec((rows, model_width), lambda j: (0, 0)),
            pl.BlockSpec((tile, model_width), lambda j: (j, 0)),
            pl.BlockSpec((rows, tile), lambda j: (0, j)),
        ]
        + [pl.BlockSpec(memory_space=pl.ANY)] * len(held),
        out_specs=pl.BlockSpec((rows, tile), lambda j: (place, j)),
        out_shape=jax.ShapeDtypeStruct((ways * rows, hidden), jnp.bfloat16),
        input_output_aliases={3: 0} if held else {},
        compiler_params=pltpu.CompilerParams(vmem_limit_bytes=40 * 2**20),
        cost_estimate=pl.CostEstimate(
            flops=2 * rows * model_width * hidden,
            bytes_accessed=2 * hidden * model_width,
            transcendentals=0,
        ),
        name="hidden_back",
    )(block, weight, slope, *held)


def normalize_kernel(x_ref, gain_ref, shift_ref, out_ref):
    x = x_ref[...].astype(jnp.float32)
    centered = x - jnp.mean(x, axis=-1, keepdims=True)
    inverse = lax.rsqrt(jnp.mean(centered * centered, axis=-1, keepdims=True) + EPS)
    out_ref[...] = (centered * inverse * gain_ref[...] + shift_ref[...]).astype(jnp.bfloat16)


def normalize(x, gain, shift_in):
    rows, width = x.shape
    block = pl.BlockSpec((128, width), lambda i: (i, 0))
    wide = pl.BlockSpec((1, width), lambda i: (0, 0))
    return pl.pallas_call(
        normalize_kernel,
        grid=(rows // 128,),
        in_specs=[block, wide, wide],
        out_specs=block,
        out_shape=jax.ShapeDtypeStruct((rows, width), jnp.bfloat16),
        name="normalize",
    )(x, gain[None, :], shift_in[None, :])


def add_pair_kernel(a_ref, b_ref, c_ref, d_ref, ab_ref, cd_ref):
    ab_ref[...] = (a_ref[...].astype(jnp.float32) + b_ref[...].astype(jnp.float32)).astype(
        jnp.bfloat16
    )
    cd_ref[...] = (c_ref[...].astype(jnp.float32) + d_ref[...].astype(jnp.float32)).astype(
        jnp.bfloat16
    )


def add_pair(a, b, c, d):
    rows, width = a.shape
    block = pl.BlockSpec((128, width), lambda i: (i, 0))
    return pl.pallas_call(
        add_pair_kernel,
        grid=(rows // 128,),
        in_specs=[block] * 4,
        out_specs=[block] * 2,
        out_shape=[jax.ShapeDtypeStruct((rows, width), jnp.bfloat16)] * 2,
        name="add_pair",
    )(a, b, c, d)


def columns_sorted_kernel(weight_ref, out_ref):
    for c in range(3):
        out_ref[:, c * PAIR : (c + 1) * PAIR] = weight_ref[c]


def columns_sorted(weight):
    _, rows, width = weight.shape
    tile = min(512, rows)
    return pl.pallas_call(
        columns_sorted_kernel,
        grid=(rows // tile, width // PAIR),
        in_specs=[pl.BlockSpec((3, tile, PAIR), lambda r, p: (0, r, p))],
        out_specs=pl.BlockSpec((tile, 3 * PAIR), lambda r, p: (r, p)),
        out_shape=jax.ShapeDtypeStruct((rows, 3 * width), weight.dtype),
        name="columns_sorted",
    )(weight)


def columns_back_kernel(part_ref, out_ref):
    for c in range(3):
        out_ref[c] = part_ref[:, c * PAIR : (c + 1) * PAIR].astype(jnp.float32)


def columns_back(part):
    rows, width = part.shape
    return pl.pallas_call(
        columns_back_kernel,
        grid=(width // (3 * PAIR),),
        in_specs=[pl.BlockSpec((rows, 3 * PAIR), lambda p: (0, p))],
        out_specs=pl.BlockSpec((3, rows, PAIR), lambda p: (0, 0, p)),
        out_shape=jax.ShapeDtypeStruct((3, rows, width // 3), jnp.float32),
        name="columns_back",
    )(part)


def gelu_and_slope(u):
    tanh_value = jnp.tanh(GELU_C * (u + 0.044715 * u * u * u))
    value = 0.5 * u * (1.0 + tanh_value)
    slope = 0.5 * (1.0 + tanh_value) + 0.5 * u * (1.0 - tanh_value * tanh_value) * GELU_C * (
        1.0 + 3.0 * 0.044715 * u * u
    )
    return (value, slope)


def contract_rows(left, right):
    return lax.dot_general(
        left, right, (((0,), (0,)), ((), ())), preferred_element_type=jnp.float32
    )


def contract_cols(left, right):
    return lax.dot_general(
        left, right, (((1,), (1,)), ((), ())), preferred_element_type=jnp.float32
    )


def shift(x, pairs):
    return lax.ppermute(x, "tensor", pairs)


class LineGather:
    def __init__(self, x):
        self.up, self.down = [x], [x]

    def step(self):
        n, k = lax.axis_size("tensor"), len(self.up)
        self.up.append(shift(self.up[-1], [(i, i + 1) for i in range(k - 1, n - 1)]))
        self.down.append(shift(self.down[-1], [(i, i - 1) for i in range(1, n - k + 1)]))

    def block(self, k):
        n, me = lax.axis_size("tensor"), lax.axis_index("tensor")
        return jnp.where(me >= k, self.up[k], self.down[n - k]) if k else self.up[0]


class RingScatter:
    def __init__(self, parts, rows):
        self.parts, self.rows, self.k, self.up, self.down = list(parts), rows, 0, None, None

    def next(self):
        place = self.k * self.rows
        for part in self.parts:
            if place < part.shape[0]:
                return part[place : place + self.rows]
            place -= part.shape[0]

    def step(self):
        n, mine = lax.axis_size("tensor"), self.next()
        if self.k:
            mine = (mine.astype(jnp.float32) + self.up.astype(jnp.float32)).astype(jnp.bfloat16)
        self.up = shift(mine, [(i, (i + 1) % n) for i in range(n)])
        self.k += 1

    def total(self):
        return self.next().astype(jnp.float32) + self.up.astype(jnp.float32)


class LineScatter:
    def __init__(self, parts):
        self.parts, self.k, self.up, self.down = parts, 1, None, None

    def step(self):
        n, k = lax.axis_size("tensor"), self.k
        mine_up, mine_down = self.parts[k], self.parts[n - k]
        if k > 1:
            mine_up, mine_down = add_pair(mine_up, self.up, mine_down, self.down)
        self.up = shift(mine_up, [(i, i + 1) for i in range(k)])
        self.down = shift(mine_down, [(i, i - 1) for i in range(n - k, n)])
        self.k = k + 1

    def total(self):
        return sum(x.astype(jnp.float32) for x in (self.parts[0], self.up, self.down))


def together(*moves, after=()):
    state = [
        (m.up[-1], m.down[-1]) if isinstance(m, LineGather) else (m.parts, m.up, m.down)
        for m in moves
    ]
    state, after = lax.optimization_barrier((state, after))
    for m, kept in zip(moves, state):
        if isinstance(m, LineGather):
            m.up[-1], m.down[-1] = kept
        else:
            m.parts, m.up, m.down = kept
    return after


def blocks_of(whole, n):
    rows = whole.shape[0] // n
    return [whole[k * rows : (k + 1) * rows] for k in range(n)]


def scatter_low(part, axis, dim):
    return lax.psum_scatter(
        part.astype(jnp.bfloat16), axis, scatter_dimension=dim, tiled=True
    )


def body(
    tokens,
    segments,
    norm_gain,
    norm_shift,
    qkv_weight,
    qkv_bias,
    dense_weight,
    up_weight,
    up_bias,
    down_weight,
    out_bias,
    cotangent,
):
    row_count, model_width = tokens.shape
    length = segments.shape[1]
    ways, copies = lax.axis_size("tensor"), lax.axis_size("dp")
    me = lax.axis_index("tensor")
    low = jnp.bfloat16
    resid = tokens.astype(jnp.float32)
    row_mean = jnp.mean(resid, axis=-1, keepdims=True)
    centered = resid - row_mean
    inverse = lax.rsqrt(jnp.mean(centered * centered, axis=-1, keepdims=True) + EPS)
    normed = centered * inverse
    normed_mine = normalize(tokens, norm_gain, norm_shift)
    full_qkv = lax.all_gather(qkv_weight, "dp", axis=1, tiled=True)
    normed_mine, up_weight, down_weight, dense_weight = lax.optimization_barrier(
        (normed_mine, up_weight, down_weight, dense_weight)
    )
    full_up = lax.all_gather(up_weight, "dp", axis=0, tiled=True)
    full_down = lax.all_gather(down_weight, "dp", axis=1, tiled=True)
    full_dense = lax.all_gather(dense_weight, "dp", axis=1, tiled=True)
    around = [(i, (i + 1) % ways) for i in range(ways)]
    ring = [normed_mine, shift(normed_mine, around)]

    biases = jnp.concatenate([qkv_bias.reshape(-1), up_bias])
    biases = lax.all_gather(biases, "dp", axis=0).astype(jnp.float32)
    third = qkv_bias.shape[1]
    full_qbias = biases[:, : 3 * third].reshape(copies, 3, third)
    full_qbias = full_qbias.transpose(1, 0, 2).reshape(3, -1, PAIR).transpose(1, 0, 2).reshape(-1)
    full_ubias = biases[:, 3 * third :].reshape(-1)

    starts = segment_starts(segments)[0]
    cos_wide, sin_wide = rotary_wide(starts)
    valid_rows = (segments != 0).astype(jnp.float32).reshape(length, 1)
    valid_wide = jnp.broadcast_to(valid_rows, (length, PAIR))
    lows = starts[::BLOCK] // BLOCK
    chunk = jnp.arange(length // BLOCK, dtype=jnp.int32)
    per = row_count // BLOCK
    places = (me - 1 - chunk // per) % ways * per + chunk % per

    tables = (cos_wide, sin_wide, starts, valid_wide, lows, places)
    valid_mine = lax.dynamic_slice_in_dim(valid_rows, me * row_count, row_count, 0)
    cot_columns = jnp.sum(cotangent, axis=0, dtype=jnp.float32)
    resid_square = jnp.sum(valid_mine * resid * resid)
    fixed = lax.optimization_barrier
    ring[1], cot_mine, tables, full_qbias, full_ubias, cot_columns, resid_square = fixed(
        (ring[1], cotangent, tables, full_qbias, full_ubias, cot_columns, resid_square)
    )
    pairs = qkv_weight.shape[2] // PAIR
    sorted_qkv = columns_sorted(full_qkv)
    half = max(1, pairs // 2)
    projected, slopes, hidden_act, mlp_parts = ([None] * ways for _ in range(4))
    grad_context, grad_pre = [None] * ways, [None]

    def turned(blocks):
        return [*blocks[1:], blocks[0]]

    def project(k):
        projected[k] = jnp.dot(ring[k], sorted_qkv, preferred_element_type=jnp.float32)

    def widen(k):
        pre = jnp.dot(ring[k], full_up, preferred_element_type=jnp.float32) + full_ubias
        value, slopes[k] = gelu_and_slope(pre)
        hidden_act[k] = value.astype(low)

    def narrow(k):
        mlp_parts[k] = jnp.dot(
            hidden_act[k], full_down, preferred_element_type=jnp.float32
        ).astype(low)

    def context_back(k, block):
        grad_context[k] = contract_cols(block, full_dense).astype(low)

    def inner_back(k, block):
        grad_pre[0] = hidden_back(
            block, full_down, slopes[k], (k - 1) % ways, ways, held=grad_pre[0]
        )

    for k in range(2, ways):
        coming = shift(ring[k - 1], around)
        if k == 2:
            project(0)
            project(1)
        if k == ways - 1:
            for j in range(ways - 1):
                if projected[j] is None:
                    project(j)
                widen(j)
        coming, ring, projected, slopes, hidden_act, cot_mine = fixed(
            (coming, ring, projected, slopes, hidden_act, cot_mine)
        )
        ring.append(coming)

    cot = LineGather(cot_mine)
    cot.step()
    project(ways - 1)
    widen(ways - 1)
    for k in range(ways):
        narrow(k)
    ring, projected, slopes, hidden_act, mlp_parts = together(
        cot, after=(ring, projected, slopes, hidden_act, mlp_parts)
    )

    mlp = LineScatter(mlp_parts)
    while len(cot.up) < ways - 1:
        cot.step()
        mlp.step()
    attended = attention_forward(turned(projected), full_qbias, tables, 0, pairs)
    ring, attended, slopes, hidden_act, sorted_qkv, cot.up[0] = together(
        cot, mlp, after=(ring, attended, slopes, hidden_act, sorted_qkv, cot.up[0])
    )
    query, keys, values, context_low, logsum = attended

    cot.step()
    mlp.step()
    for k in [0, *range(2, ways - 1)]:
        context_back(k, cot.block(k))
        inner_back(k, cot.block(k))
    acts = jnp.concatenate(turned(hidden_act), axis=0)
    attn_part = [
        jnp.dot(rows, full_dense, preferred_element_type=jnp.float32).astype(low)
        for rows in (context_low[:row_count], context_low[row_count:])
    ]
    normed_low = jnp.concatenate(turned(ring), axis=0)
    grad_context, grad_pre, acts, slopes, attn_part, normed_low = together(
        cot, mlp, after=(grad_context, grad_pre, acts, slopes, attn_part, normed_low)
    )

    while mlp.k < ways:
        mlp.step()
    blocks = [cot.block(k) for k in range(ways)]
    late = sorted({1, ways - 1})
    for k in late:
        context_back(k, blocks[k])
    grad_full = jnp.concatenate(turned(blocks), axis=0)
    grad_down = contract_rows(acts, grad_full).astype(low)
    grad_context, attn_part, grad_full, grad_down, blocks, grad_pre, slopes = together(
        mlp, after=(grad_context, attn_part, grad_full, grad_down, blocks, grad_pre, slopes)
    )
    part_down = scatter_low(grad_down, "dp", 1)

    attn = RingScatter(attn_part, row_count)
    attn.step()
    grads = attention_backward(query, keys, values, turned(grad_context), logsum, tables, 0, half)
    grad_dense = contract_rows(context_low, grad_full).astype(low)
    grads, grad_context, grad_dense, grad_pre, normed_low, blocks, slopes = together(
        attn, mlp, after=(grads, grad_context, grad_dense, grad_pre, normed_low, blocks, slopes)
    )
    part_dense = scatter_low(grad_dense, "dp", 1)

    while attn.k < ways - 2:
        attn.step()
    if pairs > half:
        grads = attention_backward(
            query, keys, values, turned(grad_context), logsum, tables, half, pairs - half, held=grads
        )
    for k in late:
        inner_back(k, blocks[k])
    grads, grad_pre, normed_low, part_down = together(
        attn, mlp, after=(grads, grad_pre, normed_low, part_down)
    )
    grad_proj, grad_qbias = grads[0], grads[1][:, 0, :]
    [pre_full] = grad_pre

    def return_normed(low_block, high_block):
        rows = slice(low_block * row_count, high_block * row_count)
        part = contract_cols(pre_full[rows], full_up) + contract_cols(grad_proj[rows], sorted_qkv)
        return part.astype(low)

    attn.step()
    grad_up = contract_rows(normed_low, pre_full).astype(low)
    grad_parts = [return_normed(0, 1)]
    grad_parts, grad_up, pre_full, grad_proj, normed_low, part_dense = together(
        attn, mlp, after=(grad_parts, grad_up, pre_full, grad_proj, normed_low, part_dense)
    )
    part_up = scatter_low(grad_up, "dp", 0)

    last = RingScatter(grad_parts, row_count)
    last.step()
    grad_qkv = contract_rows(normed_low, grad_proj).astype(low)
    last.parts.append(return_normed(1, 2))
    grad_qkv, pre_full, grad_proj = together(last, attn, mlp, after=(grad_qkv, pre_full, grad_proj))
    part_qkv = scatter_low(grad_qkv, "dp", 0)
    last.parts.append(return_normed(2, ways))
    while last.k < ways - 2:
        last.step()
    grad_ubias = jnp.sum(pre_full, axis=0, dtype=jnp.float32)
    attn_mine, mlp_mine = attn.total(), mlp.total()
    attn_mine, mlp_mine, grad_ubias, part_down, part_dense, part_up = together(
        last, after=(attn_mine, mlp_mine, grad_ubias, part_down, part_dense, part_up)
    )
    part_qkv = columns_back(part_qkv)
    part_down, part_dense = part_down.astype(jnp.float32), part_dense.astype(jnp.float32)
    last.step()
    output = (resid + attn_mine + mlp_mine + out_bias).astype(low)
    attn_square = jnp.sum(valid_mine * attn_mine * attn_mine)
    mlp_square = jnp.sum(valid_mine * mlp_mine * mlp_mine)
    part_up = part_up.astype(jnp.float32)
    output, attn_square, mlp_square, part_up, part_qkv, part_down, part_dense = together(
        last,
        after=(output, attn_square, mlp_square, part_up, part_qkv, part_down, part_dense),
    )
    grad_mine = last.total()
    scaled = grad_mine * norm_gain
    grad_tokens = (
        cotangent.astype(jnp.float32)
        + inverse
        * (
            scaled
            - jnp.mean(scaled, axis=-1, keepdims=True)
            - normed * jnp.mean(scaled * normed, axis=-1, keepdims=True)
        )
    ).astype(low)

    totals = jnp.stack(
        [resid_square, attn_square, mlp_square, jnp.sum(valid_mine) * model_width]
    )
    columns = jnp.stack(
        [
            jnp.sum(grad_mine * normed, axis=0),
            jnp.sum(grad_mine, axis=0),
            cot_columns,
        ]
    )
    peers = copies * ways
    share = model_width // peers
    columns = columns.reshape(3, peers, share).transpose(1, 0, 2).reshape(peers, 3 * share)
    own_bias = jnp.concatenate(
        [
            grad_qbias.reshape(3, copies, third).transpose(1, 0, 2).reshape(copies, 3 * third),
            grad_ubias.reshape(copies, -1),
        ],
        axis=1,
    )
    same = (jnp.arange(ways) == me).astype(jnp.float32)[None, :, None]
    own_bias = (own_bias[:, None, :] * same).reshape(peers, -1)
    small = jnp.concatenate(
        [columns, own_bias, jnp.broadcast_to(totals, (peers, 4))], axis=1
    )
    small = jnp.sum(lax.all_to_all(small, ("dp", "tensor"), 0, 0, tiled=True), axis=0)
    part_gain, part_shift, part_obias = small[: 3 * share].reshape(3, share)
    part_qbias = small[3 * share : 3 * share + 3 * third].reshape(3, third)
    part_ubias = small[3 * share + 3 * third : -4]
    root_squares = jnp.sqrt(small[-4:-1] / small[-1])
    return (
        output,
        grad_tokens,
        part_gain,
        part_shift,
        part_qkv,
        part_qbias,
        part_dense,
        part_up,
        part_ubias,
        part_down,
        part_obias,
        root_squares,
    )


def solution(mesh):
    placed = (
        P(("dp", "tensor"), None),
        P("dp", None),
        P(),
        P(),
        P(None, "dp", "tensor"),
        P(None, ("tensor", "dp")),
        P("tensor", "dp"),
        P("dp", "tensor"),
        P(("tensor", "dp")),
        P("tensor", "dp"),
        P(),
        P(("dp", "tensor"), None),
    )
    return jax.shard_map(
        body,
        mesh=mesh,
        in_specs=placed,
        out_specs=(
            P(("dp", "tensor"), None),
            P(("dp", "tensor"), None),
            P(("dp", "tensor")),
            P(("dp", "tensor")),
            P(None, "dp", "tensor"),
            P(None, ("tensor", "dp")),
            P("tensor", "dp"),
            P("dp", "tensor"),
            P(("tensor", "dp")),
            P("tensor", "dp"),
            P(("dp", "tensor")),
            P(),
        ),
        check_vma=False,
    )
```

```python
import functools
import math

import jax
import jax.numpy as jnp
from jax import lax
from jax.experimental import pallas as pl
from jax.experimental.pallas import tpu as pltpu
from jax.sharding import PartitionSpec as P

HEAD_DIM = 64
ROT = 32
PAIR = 2 * HEAD_DIM
BLOCK = 256
MOST = 5

EPS = 1e-05
GELU_C = math.sqrt(2.0 / math.pi)


def segment_starts(segs):
    return jnp.sum((segs[:, None, :] < segs[:, :, None]).astype(jnp.int32), axis=-1)


def rotary_wide(starts):
    length = starts.shape[0]
    half_rot = ROT // 2
    frequency = jnp.exp(-math.log(10000.0) * (2.0 * jnp.arange(half_rot, dtype=jnp.float32) / ROT))
    position = jnp.arange(length, dtype=jnp.int32) - starts
    angles = position.astype(jnp.float32)[:, None] * frequency
    cosines, sines = jnp.cos(angles), jnp.sin(angles)
    ones = jnp.ones((length, HEAD_DIM - ROT), jnp.float32)
    cos_head = jnp.concatenate([cosines, cosines, ones], axis=-1)
    sin_head = jnp.concatenate([-sines, sines, 0.0 * ones], axis=-1)
    return (jnp.concatenate([cos_head, cos_head], -1), jnp.concatenate([sin_head, sin_head], -1))


def turn(x, cos_wide, sin_wide):
    lane = lax.broadcasted_iota(jnp.int32, x.shape, 1) % HEAD_DIM
    half_rot = ROT // 2
    partner = jnp.where(
        lane < half_rot, pltpu.roll(x, PAIR - half_rot, 1), pltpu.roll(x, half_rot, 1)
    )
    return x * cos_wide + partner * sin_wide


def first_half(shape):
    return lax.broadcasted_iota(jnp.int32, shape, len(shape) - 1) < HEAD_DIM


def halves(x):
    front = first_half(x.shape)
    zero = jnp.zeros_like(x)
    return (jnp.where(front, x, zero), jnp.where(front, zero, x))


def nt(left, right):
    return lax.dot_general(
        left, right, (((1,), (1,)), ((), ())), preferred_element_type=jnp.float32
    )


def nn(left, right):
    return lax.dot_general(
        left, right, (((1,), (0,)), ((), ())), preferred_element_type=jnp.float32
    )


def tn(left, right):
    return lax.dot_general(
        left, right, (((0,), (0,)), ((), ())), preferred_element_type=jnp.float32
    )


def attend_kernel(
    low_ref, place_ref, parts, bias_ref, cos_ref, sin_ref, start_ref, valid_ref,
    q_ref, k_ref, v_ref, ctx_ref, lse_ref, km, vm,
):
    length = q_ref.shape[0]
    blocks = length // BLOCK
    scale = 1.0 / math.sqrt(HEAD_DIM)

    per = length // len(parts) // BLOCK

    def project(i, slot):
        rows = pl.ds(pl.multiple_of(place_ref[slot * per + i] * BLOCK, BLOCK), BLOCK)
        here = pl.ds(i * BLOCK, BLOCK)
        part = parts[slot]
        cw, sw = cos_ref[rows, :], sin_ref[rows, :]
        x = part[here, :] + bias_ref[...]
        q = turn(x[:, :PAIR], cw, sw).astype(jnp.bfloat16)
        q_ref[rows, :] = q * jnp.bfloat16(scale)
        k = turn(x[:, PAIR : 2 * PAIR], cw, sw).astype(jnp.bfloat16)
        k_ref[rows, :] = k
        v = x[:, 2 * PAIR :].astype(jnp.bfloat16)
        v_ref[rows, :] = v
        km[0, rows, :], km[1, rows, :] = halves(k)
        vm[0, rows, :], vm[1, rows, :] = halves(v)

    for slot in range(len(parts)):
        for i in range(per):
            project(i, slot)

    def query_block(i, count):
        rows = pl.ds(pl.multiple_of(i * BLOCK, BLOCK), BLOCK)
        base = pl.multiple_of((i + 1 - count) * BLOCK, BLOCK)
        cols = pl.ds(base, count * BLOCK)
        shape = (BLOCK, count * BLOCK)
        q = q_ref[rows, :]
        start = start_ref[rows, :][:, :1] - base
        kpos = lax.broadcasted_iota(jnp.int32, shape, 1)
        qpos = lax.broadcasted_iota(jnp.int32, shape, 0) + (count - 1) * BLOCK
        allowed = (kpos >= start) & (kpos <= qpos)
        there = pl.ds(pl.multiple_of(place_ref[i] * BLOCK, BLOCK), BLOCK)
        acc = jnp.zeros((BLOCK, PAIR), jnp.float32)
        tops, sums = [], []
        for h in range(2):
            s = jnp.where(allowed, nt(q, km[h, cols, :]), -jnp.inf)
            top = jnp.max(s, axis=-1, keepdims=True)
            e = jnp.exp(s - top)
            tops.append(top)
            sums.append(jnp.sum(e, axis=-1, keepdims=True))
            acc = acc + nn(e.astype(jnp.bfloat16), vm[h, cols, :])
        front = first_half((BLOCK, PAIR))
        out = acc / jnp.where(front, sums[0], sums[1])
        ctx_ref[there, :] = (out * valid_ref[rows, :]).astype(jnp.bfloat16)
        lse = jnp.where(front, tops[0] + jnp.log(sums[0]), tops[1] + jnp.log(sums[1]))
        lse_t = lse.T
        lse_ref[0, 0:1, rows] = lse_t[0:1, :]
        lse_ref[0, 1:2, rows] = lse_t[HEAD_DIM : HEAD_DIM + 1, :]

    def step(i, _):
        for count in range(1, MOST + 1):
            pl.when(i + 1 - low_ref[i] == count)(functools.partial(query_block, i, count))
        return 0

    lax.fori_loop(0, blocks, step, 0)


def attention_forward(projected, bias, tables, first, count, held=None):
    cos_wide, sin_wide, starts, valid_wide, lows, places = tables
    width = projected[0].shape[1] // 3
    length = starts.shape[0]
    blocks = length // BLOCK
    ways = len(projected)
    start_wide = jnp.broadcast_to(starts[:, None], (length, PAIR))
    part = pl.BlockSpec((length // ways, 3 * PAIR), lambda p, low, place: (0, p + first))
    table = pl.BlockSpec((length, PAIR), lambda p, low, place: (0, 0))
    flat = pl.BlockSpec((length, PAIR), lambda p, low, place: (0, p + first))
    flat_shape = jax.ShapeDtypeStruct((length, width), jnp.bfloat16)
    held = tuple(held or ())

    def kernel(*refs):
        rest = refs[2 + ways :]
        attend_kernel(*refs[:2], refs[2 : 2 + ways], *rest[:5], *rest[5 + len(held) :])

    return pl.pallas_call(
        kernel,
        grid_spec=pltpu.PrefetchScalarGridSpec(
            num_scalar_prefetch=2,
            grid=(count,),
            in_specs=[
                *[part] * ways,
                pl.BlockSpec((1, 3 * PAIR), lambda p, low, place: (0, p + first)),
                table, table, table, table,
            ] + [pl.BlockSpec(memory_space=pl.ANY)] * len(held),
            out_specs=[flat, flat, flat, flat,
                       pl.BlockSpec((1, 2, length), lambda p, low, place: (p + first, 0, 0))],
            scratch_shapes=[
                pltpu.VMEM((2, length, PAIR), jnp.bfloat16),
                pltpu.VMEM((2, length, PAIR), jnp.bfloat16),
            ],
        ),
        out_shape=[flat_shape] * 4
        + [jax.ShapeDtypeStruct((width // PAIR, 2, length), jnp.float32)],
        input_output_aliases={7 + ways + i: i for i in range(len(held))},
        compiler_params=pltpu.CompilerParams(vmem_limit_bytes=48 * 2**20),
        name="attend",
    )(lows, places, *projected, bias[None, :], cos_wide, sin_wide,
      start_wide, valid_wide, *held)


def attend_back_kernel(
    low_ref, place_ref, dos, q_ref, k_ref, v_ref, lse_ref, cos_ref, sin_ref, start_ref, valid_ref,
    grad_ref, sums_ref, qm, km, vm, dom, do_scr, dk_acc, dv_acc,
):
    length = q_ref.shape[0]
    blocks = length // BLOCK
    scale = 1.0 / math.sqrt(HEAD_DIM)

    def split(i, _):
        rows = pl.ds(pl.multiple_of(i * BLOCK, BLOCK), BLOCK)
        qm[0, rows, :], qm[1, rows, :] = halves(q_ref[rows, :])
        km[0, rows, :], km[1, rows, :] = halves(k_ref[rows, :])
        vm[0, rows, :], vm[1, rows, :] = halves(v_ref[rows, :])
        dk_acc[rows, :] = jnp.zeros((BLOCK, PAIR), jnp.float32)
        dv_acc[rows, :] = jnp.zeros((BLOCK, PAIR), jnp.float32)
        return 0

    lax.fori_loop(0, blocks, split, 0)

    per = length // len(dos) // BLOCK
    for slot in range(len(dos)):
        for i in range(per):
            rows = pl.ds(pl.multiple_of(place_ref[slot * per + i] * BLOCK, BLOCK), BLOCK)
            do = dos[slot][i * BLOCK : (i + 1) * BLOCK, :].astype(jnp.float32)
            do = (do * valid_ref[rows, :]).astype(jnp.bfloat16)
            do_scr[rows, :] = do
            dom[0, rows, :], dom[1, rows, :] = halves(do)

    def query_block(i, count):
        rows = pl.ds(pl.multiple_of(i * BLOCK, BLOCK), BLOCK)
        base = pl.multiple_of((i + 1 - count) * BLOCK, BLOCK)
        cols = pl.ds(base, count * BLOCK)
        shape = (count * BLOCK, BLOCK)
        q = q_ref[rows, :]
        do = do_scr[rows, :]
        start = start_ref[:, rows] - base
        kpos = lax.broadcasted_iota(jnp.int32, shape, 0)
        qpos = lax.broadcasted_iota(jnp.int32, shape, 1) + (count - 1) * BLOCK
        allowed = (kpos >= start) & (kpos <= qpos)
        dk = dk_acc[cols, :]
        dv = dv_acc[cols, :]
        dq = jnp.zeros((BLOCK, PAIR), jnp.float32)
        for h in range(2):
            s = nt(km[h, cols, :], q)
            p = jnp.where(allowed, jnp.exp(s - lse_ref[0, h : h + 1, rows]), 0.0)
            dp = nt(vm[h, cols, :], do)
            delta = jnp.sum(p * dp, axis=0, keepdims=True)
            dv = dv + nn(p.astype(jnp.bfloat16), dom[h, rows, :])
            ds = (p * (dp - delta)).astype(jnp.bfloat16)
            dk = dk + nn(ds, qm[h, rows, :])
            dq = dq + tn(ds, km[h, cols, :])
        dk_acc[cols, :] = dk
        dv_acc[cols, :] = dv
        dq = turn(dq * scale, cos_ref[rows, :], -sin_ref[rows, :]).astype(jnp.bfloat16)
        there = pl.ds(pl.multiple_of(place_ref[i] * BLOCK, BLOCK), BLOCK)
        grad_ref[there, :PAIR] = dq
        sums_ref[0] += jnp.sum(dq.astype(jnp.float32), axis=0, keepdims=True)

    none = jnp.zeros((1, PAIR), jnp.float32)
    sums_ref[0] = none

    def step(i, _):
        for count in range(1, MOST + 1):
            pl.when(i + 1 - low_ref[i] == count)(functools.partial(query_block, i, count))
        return 0

    lax.fori_loop(0, blocks, step, 0)

    def finish(i, totals):
        rows = pl.ds(pl.multiple_of(i * BLOCK, BLOCK), BLOCK)
        dk = turn(dk_acc[rows, :], cos_ref[rows, :], -sin_ref[rows, :]).astype(jnp.bfloat16)
        dv = dv_acc[rows, :].astype(jnp.bfloat16)
        there = pl.ds(pl.multiple_of(place_ref[i] * BLOCK, BLOCK), BLOCK)
        grad_ref[there, PAIR : 2 * PAIR] = dk
        grad_ref[there, 2 * PAIR :] = dv
        return (
            totals[0] + jnp.sum(dk.astype(jnp.float32), axis=0, keepdims=True),
            totals[1] + jnp.sum(dv.astype(jnp.float32), axis=0, keepdims=True),
        )

    sums_ref[1], sums_ref[2] = lax.fori_loop(0, blocks, finish, (none, none))


def attention_backward(q, k, v, do, lse, tables, first, count, held=None):
    cos_wide, sin_wide, starts, valid_wide, lows, places = tables
    length, width = q.shape
    blocks = length // BLOCK
    flat = pl.BlockSpec((length, PAIR), lambda p, low, place: (0, p + first))
    table = pl.BlockSpec((length, PAIR), lambda p, low, place: (0, 0))
    held = tuple(held or ())
    ways = len(do)

    def kernel(*refs):
        rest = refs[2 + ways :]
        attend_back_kernel(*refs[:2], refs[2 : 2 + ways], *rest[:8], *rest[8 + len(held) :])

    return pl.pallas_call(
        kernel,
        grid_spec=pltpu.PrefetchScalarGridSpec(
            num_scalar_prefetch=2,
            grid=(count,),
            in_specs=[
                *[pl.BlockSpec((length // ways, PAIR), lambda p, low, place: (0, p + first))] * ways,
                flat, flat, flat,
                pl.BlockSpec((1, 2, length), lambda p, low, place: (p + first, 0, 0)),
                table, table,
                pl.BlockSpec((1, length), lambda p, low, place: (0, 0)),
                table,
            ] + [pl.BlockSpec(memory_space=pl.ANY)] * len(held),
            out_specs=[
                pl.BlockSpec((length, 3 * PAIR), lambda p, low, place: (0, p + first)),
                pl.BlockSpec((3, 1, PAIR), lambda p, low, place: (0, 0, p + first)),
            ],
            scratch_shapes=[pltpu.VMEM((2, length, PAIR), jnp.bfloat16)] * 4
            + [pltpu.VMEM((length, PAIR), jnp.bfloat16)]
            + [pltpu.VMEM((length, PAIR), jnp.float32)] * 2,
        ),
        out_shape=[
            jax.ShapeDtypeStruct((length, 3 * width), jnp.bfloat16),
            jax.ShapeDtypeStruct((3, 1, width), jnp.float32),
        ],
        input_output_aliases={10 + ways + i: i for i in range(len(held))},
        compiler_params=pltpu.CompilerParams(vmem_limit_bytes=48 * 2**20),
        name="attend_back",
    )(lows, places, *do, q, k, v, lse, cos_wide, sin_wide, starts[None, :], valid_wide, *held)


def hidden_back_kernel(block_ref, weight_ref, slope_ref, *refs):
    grad = nt(block_ref[...], weight_ref[...])
    refs[-1][...] = (grad * slope_ref[...]).astype(jnp.bfloat16)


def hidden_back(block, weight, slope, place, ways, held=None):
    rows, model_width = block.shape
    hidden = weight.shape[0]
    tile = min(512, hidden)
    held = () if held is None else (held,)
    return pl.pallas_call(
        hidden_back_kernel,
        grid=(hidden // tile,),
        in_specs=[
            pl.BlockSpec((rows, model_width), lambda j: (0, 0)),
            pl.BlockSpec((tile, model_width), lambda j: (j, 0)),
            pl.BlockSpec((rows, tile), lambda j: (0, j)),
        ]
        + [pl.BlockSpec(memory_space=pl.ANY)] * len(held),
        out_specs=pl.BlockSpec((rows, tile), lambda j: (place, j)),
        out_shape=jax.ShapeDtypeStruct((ways * rows, hidden), jnp.bfloat16),
        input_output_aliases={3: 0} if held else {},
        compiler_params=pltpu.CompilerParams(vmem_limit_bytes=40 * 2**20),
        cost_estimate=pl.CostEstimate(
            flops=2 * rows * model_width * hidden,
            bytes_accessed=2 * hidden * model_width,
            transcendentals=0,
        ),
        name="hidden_back",
    )(block, weight, slope, *held)


def normalize_kernel(x_ref, gain_ref, shift_ref, out_ref):
    x = x_ref[...].astype(jnp.float32)
    centered = x - jnp.mean(x, axis=-1, keepdims=True)
    inverse = lax.rsqrt(jnp.mean(centered * centered, axis=-1, keepdims=True) + EPS)
    out_ref[...] = (centered * inverse * gain_ref[...] + shift_ref[...]).astype(jnp.bfloat16)


def normalize(x, gain, shift_in):
    rows, width = x.shape
    block = pl.BlockSpec((128, width), lambda i: (i, 0))
    wide = pl.BlockSpec((1, width), lambda i: (0, 0))
    return pl.pallas_call(
        normalize_kernel,
        grid=(rows // 128,),
        in_specs=[block, wide, wide],
        out_specs=block,
        out_shape=jax.ShapeDtypeStruct((rows, width), jnp.bfloat16),
        name="normalize",
    )(x, gain[None, :], shift_in[None, :])


def columns_sorted_kernel(weight_ref, out_ref):
    for c in range(3):
        out_ref[:, c * PAIR : (c + 1) * PAIR] = weight_ref[c]


def columns_sorted(weight):
    _, rows, width = weight.shape
    tile = min(512, rows)
    return pl.pallas_call(
        columns_sorted_kernel,
        grid=(rows // tile, width // PAIR),
        in_specs=[pl.BlockSpec((3, tile, PAIR), lambda r, p: (0, r, p))],
        out_specs=pl.BlockSpec((tile, 3 * PAIR), lambda r, p: (r, p)),
        out_shape=jax.ShapeDtypeStruct((rows, 3 * width), weight.dtype),
        name="columns_sorted",
    )(weight)


def columns_back_kernel(part_ref, out_ref):
    for c in range(3):
        out_ref[c] = part_ref[:, c * PAIR : (c + 1) * PAIR].astype(jnp.float32)


def columns_back(part):
    rows, width = part.shape
    return pl.pallas_call(
        columns_back_kernel,
        grid=(width // (3 * PAIR),),
        in_specs=[pl.BlockSpec((rows, 3 * PAIR), lambda p: (0, p))],
        out_specs=pl.BlockSpec((3, rows, PAIR), lambda p: (0, 0, p)),
        out_shape=jax.ShapeDtypeStruct((3, rows, width // 3), jnp.float32),
        name="columns_back",
    )(part)


def gelu_and_slope(u):
    tanh_value = jnp.tanh(GELU_C * (u + 0.044715 * u * u * u))
    value = 0.5 * u * (1.0 + tanh_value)
    slope = 0.5 * (1.0 + tanh_value) + 0.5 * u * (1.0 - tanh_value * tanh_value) * GELU_C * (
        1.0 + 3.0 * 0.044715 * u * u
    )
    return (value, slope)


def contract_rows(left, right):
    return lax.dot_general(
        left, right, (((0,), (0,)), ((), ())), preferred_element_type=jnp.float32
    )


def contract_cols(left, right):
    return lax.dot_general(
        left, right, (((1,), (1,)), ((), ())), preferred_element_type=jnp.float32
    )


def shift(x, pairs):
    return lax.ppermute(x, "tensor", pairs)


class LineGather:
    def __init__(self, x):
        self.up, self.down = [x], [x]

    def step(self):
        n, k = lax.axis_size("tensor"), len(self.up)
        self.up.append(shift(self.up[-1], [(i, i + 1) for i in range(k - 1, n - 1)]))
        self.down.append(shift(self.down[-1], [(i, i - 1) for i in range(1, n - k + 1)]))

    def block(self, k):
        n, me = lax.axis_size("tensor"), lax.axis_index("tensor")
        return jnp.where(me >= k, self.up[k], self.down[n - k]) if k else self.up[0]


class RingScatter:
    def __init__(self, parts, rows):
        self.parts, self.rows, self.k, self.up, self.down = list(parts), rows, 0, None, None

    def next(self):
        place = self.k * self.rows
        for part in self.parts:
            if place < part.shape[0]:
                return part[place : place + self.rows]
            place -= part.shape[0]

    def step(self):
        n, mine = lax.axis_size("tensor"), self.next()
        if self.k:
            mine = (mine.astype(jnp.float32) + self.up.astype(jnp.float32)).astype(jnp.bfloat16)
        self.up = shift(mine, [(i, (i + 1) % n) for i in range(n)])
        self.k += 1

    def total(self):
        return self.next().astype(jnp.float32) + self.up.astype(jnp.float32)


class LineScatter:
    def __init__(self, parts):
        self.parts, self.k, self.up, self.down = parts, 1, None, None

    def step(self):
        n, k = lax.axis_size("tensor"), self.k
        mine_up, mine_down = self.parts[k], self.parts[n - k]
        if k > 1:
            mine_up = mine_up.astype(jnp.float32) + self.up.astype(jnp.float32)
            mine_down = mine_down.astype(jnp.float32) + self.down.astype(jnp.float32)
        self.up = shift(mine_up.astype(jnp.bfloat16), [(i, i + 1) for i in range(k)])
        self.down = shift(mine_down.astype(jnp.bfloat16), [(i, i - 1) for i in range(n - k, n)])
        self.k = k + 1

    def total(self):
        return sum(x.astype(jnp.float32) for x in (self.parts[0], self.up, self.down))


def together(*moves, after=()):
    state = [
        (m.up[-1], m.down[-1]) if isinstance(m, LineGather) else (m.parts, m.up, m.down)
        for m in moves
    ]
    state, after = lax.optimization_barrier((state, after))
    for m, kept in zip(moves, state):
        if isinstance(m, LineGather):
            m.up[-1], m.down[-1] = kept
        else:
            m.parts, m.up, m.down = kept
    return after


def blocks_of(whole, n):
    rows = whole.shape[0] // n
    return [whole[k * rows : (k + 1) * rows] for k in range(n)]


def scatter_low(part, axis, dim):
    return lax.psum_scatter(
        part.astype(jnp.bfloat16), axis, scatter_dimension=dim, tiled=True
    )


def body(
    tokens,
    segments,
    norm_gain,
    norm_shift,
    qkv_weight,
    qkv_bias,
    dense_weight,
    up_weight,
    up_bias,
    down_weight,
    out_bias,
    cotangent,
):
    row_count, model_width = tokens.shape
    length = segments.shape[1]
    ways, copies = lax.axis_size("tensor"), lax.axis_size("dp")
    me = lax.axis_index("tensor")
    low = jnp.bfloat16
    resid = tokens.astype(jnp.float32)
    row_mean = jnp.mean(resid, axis=-1, keepdims=True)
    centered = resid - row_mean
    inverse = lax.rsqrt(jnp.mean(centered * centered, axis=-1, keepdims=True) + EPS)
    normed = centered * inverse
    normed_mine = normalize(tokens, norm_gain, norm_shift)
    full_qkv = lax.all_gather(qkv_weight, "dp", axis=1, tiled=True)
    normed_mine, up_weight, down_weight, dense_weight = lax.optimization_barrier(
        (normed_mine, up_weight, down_weight, dense_weight)
    )
    full_up = lax.all_gather(up_weight, "dp", axis=0, tiled=True)
    full_down = lax.all_gather(down_weight, "dp", axis=1, tiled=True)
    full_dense = lax.all_gather(dense_weight, "dp", axis=1, tiled=True)
    around = [(i, (i + 1) % ways) for i in range(ways)]
    ring = [normed_mine, shift(normed_mine, around)]

    biases = jnp.concatenate([qkv_bias.reshape(-1), up_bias])
    biases = lax.all_gather(biases, "dp", axis=0).astype(jnp.float32)
    third = qkv_bias.shape[1]
    full_qbias = biases[:, : 3 * third].reshape(copies, 3, third)
    full_qbias = full_qbias.transpose(1, 0, 2).reshape(3, -1, PAIR).transpose(1, 0, 2).reshape(-1)
    full_ubias = biases[:, 3 * third :].reshape(-1)

    starts = segment_starts(segments)[0]
    cos_wide, sin_wide = rotary_wide(starts)
    valid_rows = (segments != 0).astype(jnp.float32).reshape(length, 1)
    valid_wide = jnp.broadcast_to(valid_rows, (length, PAIR))
    lows = starts[::BLOCK] // BLOCK
    chunk = jnp.arange(length // BLOCK, dtype=jnp.int32)
    per = row_count // BLOCK
    places = (me - 1 - chunk // per) % ways * per + chunk % per

    tables = (cos_wide, sin_wide, starts, valid_wide, lows, places)
    valid_mine = lax.dynamic_slice_in_dim(valid_rows, me * row_count, row_count, 0)
    cot_columns = jnp.sum(cotangent, axis=0, dtype=jnp.float32)
    resid_square = jnp.sum(valid_mine * resid * resid)
    fixed = lax.optimization_barrier
    ring[1], cot_mine, tables, full_qbias, full_ubias, cot_columns, resid_square = fixed(
        (ring[1], cotangent, tables, full_qbias, full_ubias, cot_columns, resid_square)
    )
    pairs = qkv_weight.shape[2] // PAIR
    sorted_qkv = columns_sorted(full_qkv)
    half = max(1, pairs // 2)
    projected, slopes, hidden_act, mlp_parts = ([None] * ways for _ in range(4))
    grad_context, grad_pre = [None] * ways, [None]

    def turned(blocks):
        return [*blocks[1:], blocks[0]]

    def project(k):
        projected[k] = jnp.dot(ring[k], sorted_qkv, preferred_element_type=jnp.float32)

    def widen(k):
        pre = jnp.dot(ring[k], full_up, preferred_element_type=jnp.float32) + full_ubias
        value, slopes[k] = gelu_and_slope(pre)
        hidden_act[k] = value.astype(low)

    def narrow(k):
        mlp_parts[k] = jnp.dot(
            hidden_act[k], full_down, preferred_element_type=jnp.float32
        ).astype(low)

    def context_back(k, block):
        grad_context[k] = contract_cols(block, full_dense).astype(low)

    def inner_back(k, block):
        grad_pre[0] = hidden_back(
            block, full_down, slopes[k], (k - 1) % ways, ways, held=grad_pre[0]
        )

    for k in range(2, ways):
        coming = shift(ring[k - 1], around)
        if k == 2:
            project(0)
            project(1)
        if k == ways - 1:
            for j in range(ways - 1):
                if projected[j] is None:
                    project(j)
                widen(j)
        coming, ring, projected, slopes, hidden_act, cot_mine = fixed(
            (coming, ring, projected, slopes, hidden_act, cot_mine)
        )
        ring.append(coming)

    cot = LineGather(cot_mine)
    cot.step()
    project(ways - 1)
    widen(ways - 1)
    for k in range(ways):
        narrow(k)
    ring, projected, slopes, hidden_act, mlp_parts = together(
        cot, after=(ring, projected, slopes, hidden_act, mlp_parts)
    )

    mlp = LineScatter(mlp_parts)
    while len(cot.up) < ways - 1:
        cot.step()
        mlp.step()
    attended = attention_forward(turned(projected), full_qbias, tables, 0, pairs)
    ring, attended, slopes, hidden_act, sorted_qkv, cot.up[0] = together(
        cot, mlp, after=(ring, attended, slopes, hidden_act, sorted_qkv, cot.up[0])
    )
    query, keys, values, context_low, logsum = attended

    cot.step()
    mlp.step()
    for k in [0, *range(2, ways - 1)]:
        context_back(k, cot.block(k))
        inner_back(k, cot.block(k))
    acts = jnp.concatenate(turned(hidden_act), axis=0)
    attn_part = [
        jnp.dot(rows, full_dense, preferred_element_type=jnp.float32).astype(low)
        for rows in (context_low[:row_count], context_low[row_count:])
    ]
    normed_low = jnp.concatenate(turned(ring), axis=0)
    grad_context, grad_pre, acts, slopes, attn_part, normed_low = together(
        cot, mlp, after=(grad_context, grad_pre, acts, slopes, attn_part, normed_low)
    )

    while mlp.k < ways:
        mlp.step()
    blocks = [cot.block(k) for k in range(ways)]
    late = sorted({1, ways - 1})
    for k in late:
        context_back(k, blocks[k])
    grad_full = jnp.concatenate(turned(blocks), axis=0)
    grad_down = contract_rows(acts, grad_full).astype(low)
    grad_context, attn_part, grad_full, grad_down, blocks, grad_pre, slopes = together(
        mlp, after=(grad_context, attn_part, grad_full, grad_down, blocks, grad_pre, slopes)
    )
    part_down = scatter_low(grad_down, "dp", 1)

    attn = RingScatter(attn_part, row_count)
    attn.step()
    grads = attention_backward(query, keys, values, turned(grad_context), logsum, tables, 0, half)
    inner_back(late[0], blocks[late[0]])
    grads, grad_context, grad_full, context_low, grad_pre, normed_low = together(
        attn, mlp, after=(grads, grad_context, grad_full, context_low, grad_pre, normed_low)
    )

    while attn.k < ways - 2:
        attn.step()
    if pairs > half:
        grads = attention_backward(
            query, keys, values, turned(grad_context), logsum, tables, half, pairs - half, held=grads
        )
    for k in late[1:]:
        inner_back(k, blocks[k])
    grad_dense = contract_rows(context_low, grad_full).astype(low)
    grads, grad_dense, grad_pre, normed_low, part_down = together(
        attn, mlp, after=(grads, grad_dense, grad_pre, normed_low, part_down)
    )
    part_dense = scatter_low(grad_dense, "dp", 1)
    grad_proj, grad_qbias = grads[0], grads[1][:, 0, :]
    [pre_full] = grad_pre

    def return_normed(low_block, high_block):
        rows = slice(low_block * row_count, high_block * row_count)
        part = contract_cols(pre_full[rows], full_up) + contract_cols(grad_proj[rows], sorted_qkv)
        return part.astype(low)

    attn.step()
    grad_qkv = contract_rows(normed_low, grad_proj).astype(low)
    grad_parts = [return_normed(0, 1)]
    grad_parts, grad_qkv, pre_full, grad_proj, normed_low = together(
        attn, mlp, after=(grad_parts, grad_qkv, pre_full, grad_proj, normed_low)
    )
    part_qkv = scatter_low(grad_qkv, "dp", 0)

    last = RingScatter(grad_parts, row_count)
    last.step()
    grad_up = contract_rows(normed_low, pre_full).astype(low)
    last.parts.append(return_normed(1, 2))
    grad_up, pre_full, grad_proj, part_dense = together(
        last, attn, mlp, after=(grad_up, pre_full, grad_proj, part_dense)
    )
    part_up = scatter_low(grad_up, "dp", 0)
    last.parts.append(return_normed(2, ways))
    while last.k < ways - 2:
        last.step()
    grad_ubias = jnp.sum(pre_full, axis=0, dtype=jnp.float32)
    attn_mine, mlp_mine = attn.total(), mlp.total()
    attn_mine, mlp_mine, grad_ubias, part_down, part_dense, part_qkv = together(
        last, after=(attn_mine, mlp_mine, grad_ubias, part_down, part_dense, part_qkv)
    )
    part_qkv = columns_back(part_qkv)
    part_down, part_dense = part_down.astype(jnp.float32), part_dense.astype(jnp.float32)
    last.step()
    output = (resid + attn_mine + mlp_mine + out_bias).astype(low)
    attn_square = jnp.sum(valid_mine * attn_mine * attn_mine)
    mlp_square = jnp.sum(valid_mine * mlp_mine * mlp_mine)
    part_up = part_up.astype(jnp.float32)
    output, attn_square, mlp_square, part_up, part_qkv, part_down, part_dense = together(
        last,
        after=(output, attn_square, mlp_square, part_up, part_qkv, part_down, part_dense),
    )
    grad_mine = last.total()
    scaled = grad_mine * norm_gain
    grad_tokens = (
        cotangent.astype(jnp.float32)
        + inverse
        * (
            scaled
            - jnp.mean(scaled, axis=-1, keepdims=True)
            - normed * jnp.mean(scaled * normed, axis=-1, keepdims=True)
        )
    ).astype(low)

    totals = jnp.stack(
        [resid_square, attn_square, mlp_square, jnp.sum(valid_mine) * model_width]
    )
    columns = jnp.stack(
        [
            jnp.sum(grad_mine * normed, axis=0),
            jnp.sum(grad_mine, axis=0),
            cot_columns,
        ]
    )
    peers = copies * ways
    share = model_width // peers
    columns = columns.reshape(3, peers, share).transpose(1, 0, 2).reshape(peers, 3 * share)
    own_bias = jnp.concatenate(
        [
            grad_qbias.reshape(3, copies, third).transpose(1, 0, 2).reshape(copies, 3 * third),
            grad_ubias.reshape(copies, -1),
        ],
        axis=1,
    )
    same = (jnp.arange(ways) == me).astype(jnp.float32)[None, :, None]
    own_bias = (own_bias[:, None, :] * same).reshape(peers, -1)
    small = jnp.concatenate(
        [columns, own_bias, jnp.broadcast_to(totals, (peers, 4))], axis=1
    )
    small = jnp.sum(lax.all_to_all(small, ("dp", "tensor"), 0, 0, tiled=True), axis=0)
    part_gain, part_shift, part_obias = small[: 3 * share].reshape(3, share)
    part_qbias = small[3 * share : 3 * share + 3 * third].reshape(3, third)
    part_ubias = small[3 * share + 3 * third : -4]
    root_squares = jnp.sqrt(small[-4:-1] / small[-1])
    return (
        output,
        grad_tokens,
        part_gain,
        part_shift,
        part_qkv,
        part_qbias,
        part_dense,
        part_up,
        part_ubias,
        part_down,
        part_obias,
        root_squares,
    )


def solution(mesh):
    placed = (
        P(("dp", "tensor"), None),
        P("dp", None),
        P(),
        P(),
        P(None, "dp", "tensor"),
        P(None, ("tensor", "dp")),
        P("tensor", "dp"),
        P("dp", "tensor"),
        P(("tensor", "dp")),
        P("tensor", "dp"),
        P(),
        P(("dp", "tensor"), None),
    )
    return jax.shard_map(
        body,
        mesh=mesh,
        in_specs=placed,
        out_specs=(
            P(("dp", "tensor"), None),
            P(("dp", "tensor"), None),
            P(("dp", "tensor")),
            P(("dp", "tensor")),
            P(None, "dp", "tensor"),
            P(None, ("tensor", "dp")),
            P("tensor", "dp"),
            P("dp", "tensor"),
            P(("tensor", "dp")),
            P("tensor", "dp"),
            P(("dp", "tensor")),
            P(),
        ),
        check_vma=False,
    )
```

```python
import functools
import math

import jax
import jax.numpy as jnp
from jax import lax
from jax.experimental import pallas as pl
from jax.experimental.pallas import tpu as pltpu
from jax.sharding import PartitionSpec as P

HEAD_DIM = 64
ROT = 32
PAIR = 2 * HEAD_DIM
BLOCK = 256
MOST = 5

EPS = 1e-05
GELU_C = math.sqrt(2.0 / math.pi)


def segment_starts(segs):
    return jnp.sum((segs[:, None, :] < segs[:, :, None]).astype(jnp.int32), axis=-1)


def rotary_wide(starts):
    length = starts.shape[0]
    half_rot = ROT // 2
    frequency = jnp.exp(-math.log(10000.0) * (2.0 * jnp.arange(half_rot, dtype=jnp.float32) / ROT))
    position = jnp.arange(length, dtype=jnp.int32) - starts
    angles = position.astype(jnp.float32)[:, None] * frequency
    cosines, sines = jnp.cos(angles), jnp.sin(angles)
    ones = jnp.ones((length, HEAD_DIM - ROT), jnp.float32)
    cos_head = jnp.concatenate([cosines, cosines, ones], axis=-1)
    sin_head = jnp.concatenate([-sines, sines, 0.0 * ones], axis=-1)
    return (jnp.concatenate([cos_head, cos_head], -1), jnp.concatenate([sin_head, sin_head], -1))


def turn(x, cos_wide, sin_wide):
    lane = lax.broadcasted_iota(jnp.int32, x.shape, 1) % HEAD_DIM
    half_rot = ROT // 2
    partner = jnp.where(
        lane < half_rot, pltpu.roll(x, PAIR - half_rot, 1), pltpu.roll(x, half_rot, 1)
    )
    return x * cos_wide + partner * sin_wide


def first_half(shape):
    return lax.broadcasted_iota(jnp.int32, shape, len(shape) - 1) < HEAD_DIM


def halves(x):
    front = first_half(x.shape)
    zero = jnp.zeros_like(x)
    return (jnp.where(front, x, zero), jnp.where(front, zero, x))


def nt(left, right):
    return lax.dot_general(
        left, right, (((1,), (1,)), ((), ())), preferred_element_type=jnp.float32
    )


def nn(left, right):
    return lax.dot_general(
        left, right, (((1,), (0,)), ((), ())), preferred_element_type=jnp.float32
    )


def tn(left, right):
    return lax.dot_general(
        left, right, (((0,), (0,)), ((), ())), preferred_element_type=jnp.float32
    )


def attend_kernel(
    low_ref, place_ref, parts, bias_ref, cos_ref, sin_ref, start_ref, valid_ref,
    q_ref, k_ref, v_ref, ctx_ref, lse_ref, km, vm,
):
    length = q_ref.shape[0]
    blocks = length // BLOCK
    scale = 1.0 / math.sqrt(HEAD_DIM)

    per = length // len(parts) // BLOCK

    def project(i, slot):
        rows = pl.ds(pl.multiple_of(place_ref[slot * per + i] * BLOCK, BLOCK), BLOCK)
        here = pl.ds(i * BLOCK, BLOCK)
        part = parts[slot]
        cw, sw = cos_ref[rows, :], sin_ref[rows, :]
        x = part[here, :] + bias_ref[...]
        q = turn(x[:, :PAIR], cw, sw).astype(jnp.bfloat16)
        q_ref[rows, :] = q * jnp.bfloat16(scale)
        k = turn(x[:, PAIR : 2 * PAIR], cw, sw).astype(jnp.bfloat16)
        k_ref[rows, :] = k
        v = x[:, 2 * PAIR :].astype(jnp.bfloat16)
        v_ref[rows, :] = v
        km[0, rows, :], km[1, rows, :] = halves(k)
        vm[0, rows, :], vm[1, rows, :] = halves(v)

    for slot in range(len(parts)):
        for i in range(per):
            project(i, slot)

    def query_block(i, count):
        rows = pl.ds(pl.multiple_of(i * BLOCK, BLOCK), BLOCK)
        base = pl.multiple_of((i + 1 - count) * BLOCK, BLOCK)
        cols = pl.ds(base, count * BLOCK)
        shape = (BLOCK, count * BLOCK)
        q = q_ref[rows, :]
        start = start_ref[rows, :][:, :1] - base
        kpos = lax.broadcasted_iota(jnp.int32, shape, 1)
        qpos = lax.broadcasted_iota(jnp.int32, shape, 0) + (count - 1) * BLOCK
        allowed = (kpos >= start) & (kpos <= qpos)
        there = pl.ds(pl.multiple_of(place_ref[i] * BLOCK, BLOCK), BLOCK)
        acc = jnp.zeros((BLOCK, PAIR), jnp.float32)
        tops, sums = [], []
        for h in range(2):
            s = jnp.where(allowed, nt(q, km[h, cols, :]), -jnp.inf)
            top = jnp.max(s, axis=-1, keepdims=True)
            e = jnp.exp(s - top)
            tops.append(top)
            sums.append(jnp.sum(e, axis=-1, keepdims=True))
            acc = acc + nn(e.astype(jnp.bfloat16), vm[h, cols, :])
        front = first_half((BLOCK, PAIR))
        out = acc / jnp.where(front, sums[0], sums[1])
        ctx_ref[there, :] = (out * valid_ref[rows, :]).astype(jnp.bfloat16)
        lse = jnp.where(front, tops[0] + jnp.log(sums[0]), tops[1] + jnp.log(sums[1]))
        lse_t = lse.T
        lse_ref[0, 0:1, rows] = lse_t[0:1, :]
        lse_ref[0, 1:2, rows] = lse_t[HEAD_DIM : HEAD_DIM + 1, :]

    def step(i, _):
        for count in range(1, MOST + 1):
            pl.when(i + 1 - low_ref[i] == count)(functools.partial(query_block, i, count))
        return 0

    lax.fori_loop(0, blocks, step, 0)


def attention_forward(projected, bias, tables, first, count, held=None):
    cos_wide, sin_wide, starts, valid_wide, lows, places = tables
    width = projected[0].shape[1] // 3
    length = starts.shape[0]
    blocks = length // BLOCK
    ways = len(projected)
    start_wide = jnp.broadcast_to(starts[:, None], (length, PAIR))
    part = pl.BlockSpec((length // ways, 3 * PAIR), lambda p, low, place: (0, p + first))
    table = pl.BlockSpec((length, PAIR), lambda p, low, place: (0, 0))
    flat = pl.BlockSpec((length, PAIR), lambda p, low, place: (0, p + first))
    flat_shape = jax.ShapeDtypeStruct((length, width), jnp.bfloat16)
    held = tuple(held or ())

    def kernel(*refs):
        rest = refs[2 + ways :]
        attend_kernel(*refs[:2], refs[2 : 2 + ways], *rest[:5], *rest[5 + len(held) :])

    return pl.pallas_call(
        kernel,
        grid_spec=pltpu.PrefetchScalarGridSpec(
            num_scalar_prefetch=2,
            grid=(count,),
            in_specs=[
                *[part] * ways,
                pl.BlockSpec((1, 3 * PAIR), lambda p, low, place: (0, p + first)),
                table, table, table, table,
            ] + [pl.BlockSpec(memory_space=pl.ANY)] * len(held),
            out_specs=[flat, flat, flat, flat,
                       pl.BlockSpec((1, 2, length), lambda p, low, place: (p + first, 0, 0))],
            scratch_shapes=[
                pltpu.VMEM((2, length, PAIR), jnp.bfloat16),
                pltpu.VMEM((2, length, PAIR), jnp.bfloat16),
            ],
        ),
        out_shape=[flat_shape] * 4
        + [jax.ShapeDtypeStruct((width // PAIR, 2, length), jnp.float32)],
        input_output_aliases={7 + ways + i: i for i in range(len(held))},
        compiler_params=pltpu.CompilerParams(vmem_limit_bytes=48 * 2**20),
        name="attend",
    )(lows, places, *projected, bias[None, :], cos_wide, sin_wide,
      start_wide, valid_wide, *held)


def attend_back_kernel(
    low_ref, place_ref, dos, q_ref, k_ref, v_ref, lse_ref, cos_ref, sin_ref, start_ref, valid_ref,
    grad_ref, sums_ref, qm, km, vm, dom, do_scr, dk_acc, dv_acc,
):
    length = q_ref.shape[0]
    blocks = length // BLOCK
    scale = 1.0 / math.sqrt(HEAD_DIM)

    def split(i, _):
        rows = pl.ds(pl.multiple_of(i * BLOCK, BLOCK), BLOCK)
        qm[0, rows, :], qm[1, rows, :] = halves(q_ref[rows, :])
        km[0, rows, :], km[1, rows, :] = halves(k_ref[rows, :])
        vm[0, rows, :], vm[1, rows, :] = halves(v_ref[rows, :])
        dk_acc[rows, :] = jnp.zeros((BLOCK, PAIR), jnp.float32)
        dv_acc[rows, :] = jnp.zeros((BLOCK, PAIR), jnp.float32)
        return 0

    lax.fori_loop(0, blocks, split, 0)

    per = length // len(dos) // BLOCK
    for slot in range(len(dos)):
        for i in range(per):
            rows = pl.ds(pl.multiple_of(place_ref[slot * per + i] * BLOCK, BLOCK), BLOCK)
            do = dos[slot][i * BLOCK : (i + 1) * BLOCK, :].astype(jnp.float32)
            do = (do * valid_ref[rows, :]).astype(jnp.bfloat16)
            do_scr[rows, :] = do
            dom[0, rows, :], dom[1, rows, :] = halves(do)

    def query_block(i, count):
        rows = pl.ds(pl.multiple_of(i * BLOCK, BLOCK), BLOCK)
        base = pl.multiple_of((i + 1 - count) * BLOCK, BLOCK)
        cols = pl.ds(base, count * BLOCK)
        shape = (count * BLOCK, BLOCK)
        q = q_ref[rows, :]
        do = do_scr[rows, :]
        start = start_ref[:, rows] - base
        kpos = lax.broadcasted_iota(jnp.int32, shape, 0)
        qpos = lax.broadcasted_iota(jnp.int32, shape, 1) + (count - 1) * BLOCK
        allowed = (kpos >= start) & (kpos <= qpos)
        dk = dk_acc[cols, :]
        dv = dv_acc[cols, :]
        dq = jnp.zeros((BLOCK, PAIR), jnp.float32)
        for h in range(2):
            s = nt(km[h, cols, :], q)
            p = jnp.where(allowed, jnp.exp(s - lse_ref[0, h : h + 1, rows]), 0.0)
            dp = nt(vm[h, cols, :], do)
            delta = jnp.sum(p * dp, axis=0, keepdims=True)
            dv = dv + nn(p.astype(jnp.bfloat16), dom[h, rows, :])
            ds = (p * (dp - delta)).astype(jnp.bfloat16)
            dk = dk + nn(ds, qm[h, rows, :])
            dq = dq + tn(ds, km[h, cols, :])
        dk_acc[cols, :] = dk
        dv_acc[cols, :] = dv
        dq = turn(dq * scale, cos_ref[rows, :], -sin_ref[rows, :]).astype(jnp.bfloat16)
        there = pl.ds(pl.multiple_of(place_ref[i] * BLOCK, BLOCK), BLOCK)
        grad_ref[there, :PAIR] = dq
        sums_ref[0] += jnp.sum(dq.astype(jnp.float32), axis=0, keepdims=True)

    none = jnp.zeros((1, PAIR), jnp.float32)
    sums_ref[0] = none

    def step(i, _):
        for count in range(1, MOST + 1):
            pl.when(i + 1 - low_ref[i] == count)(functools.partial(query_block, i, count))
        return 0

    lax.fori_loop(0, blocks, step, 0)

    def finish(i, totals):
        rows = pl.ds(pl.multiple_of(i * BLOCK, BLOCK), BLOCK)
        dk = turn(dk_acc[rows, :], cos_ref[rows, :], -sin_ref[rows, :]).astype(jnp.bfloat16)
        dv = dv_acc[rows, :].astype(jnp.bfloat16)
        there = pl.ds(pl.multiple_of(place_ref[i] * BLOCK, BLOCK), BLOCK)
        grad_ref[there, PAIR : 2 * PAIR] = dk
        grad_ref[there, 2 * PAIR :] = dv
        return (
            totals[0] + jnp.sum(dk.astype(jnp.float32), axis=0, keepdims=True),
            totals[1] + jnp.sum(dv.astype(jnp.float32), axis=0, keepdims=True),
        )

    sums_ref[1], sums_ref[2] = lax.fori_loop(0, blocks, finish, (none, none))


def attention_backward(q, k, v, do, lse, tables, first, count, held=None):
    cos_wide, sin_wide, starts, valid_wide, lows, places = tables
    length, width = q.shape
    blocks = length // BLOCK
    flat = pl.BlockSpec((length, PAIR), lambda p, low, place: (0, p + first))
    table = pl.BlockSpec((length, PAIR), lambda p, low, place: (0, 0))
    held = tuple(held or ())
    ways = len(do)

    def kernel(*refs):
        rest = refs[2 + ways :]
        attend_back_kernel(*refs[:2], refs[2 : 2 + ways], *rest[:8], *rest[8 + len(held) :])

    return pl.pallas_call(
        kernel,
        grid_spec=pltpu.PrefetchScalarGridSpec(
            num_scalar_prefetch=2,
            grid=(count,),
            in_specs=[
                *[pl.BlockSpec((length // ways, PAIR), lambda p, low, place: (0, p + first))] * ways,
                flat, flat, flat,
                pl.BlockSpec((1, 2, length), lambda p, low, place: (p + first, 0, 0)),
                table, table,
                pl.BlockSpec((1, length), lambda p, low, place: (0, 0)),
                table,
            ] + [pl.BlockSpec(memory_space=pl.ANY)] * len(held),
            out_specs=[
                pl.BlockSpec((length, 3 * PAIR), lambda p, low, place: (0, p + first)),
                pl.BlockSpec((3, 1, PAIR), lambda p, low, place: (0, 0, p + first)),
            ],
            scratch_shapes=[pltpu.VMEM((2, length, PAIR), jnp.bfloat16)] * 4
            + [pltpu.VMEM((length, PAIR), jnp.bfloat16)]
            + [pltpu.VMEM((length, PAIR), jnp.float32)] * 2,
        ),
        out_shape=[
            jax.ShapeDtypeStruct((length, 3 * width), jnp.bfloat16),
            jax.ShapeDtypeStruct((3, 1, width), jnp.float32),
        ],
        input_output_aliases={10 + ways + i: i for i in range(len(held))},
        compiler_params=pltpu.CompilerParams(vmem_limit_bytes=48 * 2**20),
        name="attend_back",
    )(lows, places, *do, q, k, v, lse, cos_wide, sin_wide, starts[None, :], valid_wide, *held)


def hidden_back_kernel(block_ref, weight_ref, slope_ref, *refs):
    grad = nt(block_ref[...], weight_ref[...])
    refs[-1][...] = (grad * slope_ref[...]).astype(jnp.bfloat16)


def hidden_back(block, weight, slope, place, ways, held=None):
    rows, model_width = block.shape
    hidden = weight.shape[0]
    tile = min(512, hidden)
    held = () if held is None else (held,)
    return pl.pallas_call(
        hidden_back_kernel,
        grid=(hidden // tile,),
        in_specs=[
            pl.BlockSpec((rows, model_width), lambda j: (0, 0)),
            pl.BlockSpec((tile, model_width), lambda j: (j, 0)),
            pl.BlockSpec((rows, tile), lambda j: (0, j)),
        ]
        + [pl.BlockSpec(memory_space=pl.ANY)] * len(held),
        out_specs=pl.BlockSpec((rows, tile), lambda j: (place, j)),
        out_shape=jax.ShapeDtypeStruct((ways * rows, hidden), jnp.bfloat16),
        input_output_aliases={3: 0} if held else {},
        compiler_params=pltpu.CompilerParams(vmem_limit_bytes=40 * 2**20),
        cost_estimate=pl.CostEstimate(
            flops=2 * rows * model_width * hidden,
            bytes_accessed=2 * hidden * model_width,
            transcendentals=0,
        ),
        name="hidden_back",
    )(block, weight, slope, *held)


def normalize_kernel(x_ref, gain_ref, shift_ref, out_ref):
    x = x_ref[...].astype(jnp.float32)
    centered = x - jnp.mean(x, axis=-1, keepdims=True)
    inverse = lax.rsqrt(jnp.mean(centered * centered, axis=-1, keepdims=True) + EPS)
    out_ref[...] = (centered * inverse * gain_ref[...] + shift_ref[...]).astype(jnp.bfloat16)


def normalize(x, gain, shift_in):
    rows, width = x.shape
    block = pl.BlockSpec((128, width), lambda i: (i, 0))
    wide = pl.BlockSpec((1, width), lambda i: (0, 0))
    return pl.pallas_call(
        normalize_kernel,
        grid=(rows // 128,),
        in_specs=[block, wide, wide],
        out_specs=block,
        out_shape=jax.ShapeDtypeStruct((rows, width), jnp.bfloat16),
        name="normalize",
    )(x, gain[None, :], shift_in[None, :])


def columns_sorted_kernel(weight_ref, out_ref):
    for c in range(3):
        out_ref[:, c * PAIR : (c + 1) * PAIR] = weight_ref[c]


def columns_sorted(weight):
    _, rows, width = weight.shape
    tile = min(512, rows)
    return pl.pallas_call(
        columns_sorted_kernel,
        grid=(rows // tile, width // PAIR),
        in_specs=[pl.BlockSpec((3, tile, PAIR), lambda r, p: (0, r, p))],
        out_specs=pl.BlockSpec((tile, 3 * PAIR), lambda r, p: (r, p)),
        out_shape=jax.ShapeDtypeStruct((rows, 3 * width), weight.dtype),
        name="columns_sorted",
    )(weight)


def columns_back_kernel(part_ref, out_ref):
    for c in range(3):
        out_ref[c] = part_ref[:, c * PAIR : (c + 1) * PAIR].astype(jnp.float32)


def columns_back(part):
    rows, width = part.shape
    return pl.pallas_call(
        columns_back_kernel,
        grid=(width // (3 * PAIR),),
        in_specs=[pl.BlockSpec((rows, 3 * PAIR), lambda p: (0, p))],
        out_specs=pl.BlockSpec((3, rows, PAIR), lambda p: (0, 0, p)),
        out_shape=jax.ShapeDtypeStruct((3, rows, width // 3), jnp.float32),
        name="columns_back",
    )(part)


def gelu_and_slope(u):
    tanh_value = jnp.tanh(GELU_C * (u + 0.044715 * u * u * u))
    value = 0.5 * u * (1.0 + tanh_value)
    slope = 0.5 * (1.0 + tanh_value) + 0.5 * u * (1.0 - tanh_value * tanh_value) * GELU_C * (
        1.0 + 3.0 * 0.044715 * u * u
    )
    return (value, slope)


def contract_rows(left, right):
    return lax.dot_general(
        left, right, (((0,), (0,)), ((), ())), preferred_element_type=jnp.float32
    )


def contract_cols(left, right):
    return lax.dot_general(
        left, right, (((1,), (1,)), ((), ())), preferred_element_type=jnp.float32
    )


def shift(x, pairs):
    return lax.ppermute(x, "tensor", pairs)


class LineGather:
    def __init__(self, x):
        self.up, self.down = [x], [x]

    def step(self):
        n, k = lax.axis_size("tensor"), len(self.up)
        self.up.append(shift(self.up[-1], [(i, i + 1) for i in range(k - 1, n - 1)]))
        self.down.append(shift(self.down[-1], [(i, i - 1) for i in range(1, n - k + 1)]))

    def block(self, k):
        n, me = lax.axis_size("tensor"), lax.axis_index("tensor")
        return jnp.where(me >= k, self.up[k], self.down[n - k]) if k else self.up[0]


class RingScatter:
    def __init__(self, parts, rows):
        self.parts, self.rows, self.k, self.up, self.down = list(parts), rows, 0, None, None

    def next(self):
        place = self.k * self.rows
        for part in self.parts:
            if place < part.shape[0]:
                return part[place : place + self.rows]
            place -= part.shape[0]

    def step(self):
        n, mine = lax.axis_size("tensor"), self.next()
        if self.k:
            mine = (mine.astype(jnp.float32) + self.up.astype(jnp.float32)).astype(jnp.bfloat16)
        self.up = shift(mine, [(i, (i + 1) % n) for i in range(n)])
        self.k += 1

    def total(self):
        return self.next().astype(jnp.float32) + self.up.astype(jnp.float32)


class LineScatter:
    def __init__(self, parts):
        self.parts, self.k, self.up, self.down = parts, 1, None, None

    def step(self):
        n, k = lax.axis_size("tensor"), self.k
        mine_up, mine_down = self.parts[k], self.parts[n - k]
        if k > 1:
            mine_up = mine_up.astype(jnp.float32) + self.up.astype(jnp.float32)
            mine_down = mine_down.astype(jnp.float32) + self.down.astype(jnp.float32)
        self.up = shift(mine_up.astype(jnp.bfloat16), [(i, i + 1) for i in range(k)])
        self.down = shift(mine_down.astype(jnp.bfloat16), [(i, i - 1) for i in range(n - k, n)])
        self.k = k + 1

    def total(self):
        return sum(x.astype(jnp.float32) for x in (self.parts[0], self.up, self.down))


def together(*moves, after=()):
    state = [
        (m.up[-1], m.down[-1]) if isinstance(m, LineGather) else (m.parts, m.up, m.down)
        for m in moves
    ]
    state, after = lax.optimization_barrier((state, after))
    for m, kept in zip(moves, state):
        if isinstance(m, LineGather):
            m.up[-1], m.down[-1] = kept
        else:
            m.parts, m.up, m.down = kept
    return after


def blocks_of(whole, n):
    rows = whole.shape[0] // n
    return [whole[k * rows : (k + 1) * rows] for k in range(n)]


def scatter_low(part, axis, dim):
    return lax.psum_scatter(
        part.astype(jnp.bfloat16), axis, scatter_dimension=dim, tiled=True
    )


def body(
    tokens,
    segments,
    norm_gain,
    norm_shift,
    qkv_weight,
    qkv_bias,
    dense_weight,
    up_weight,
    up_bias,
    down_weight,
    out_bias,
    cotangent,
):
    row_count, model_width = tokens.shape
    length = segments.shape[1]
    ways, copies = lax.axis_size("tensor"), lax.axis_size("dp")
    me = lax.axis_index("tensor")
    low = jnp.bfloat16
    resid = tokens.astype(jnp.float32)
    row_mean = jnp.mean(resid, axis=-1, keepdims=True)
    centered = resid - row_mean
    inverse = lax.rsqrt(jnp.mean(centered * centered, axis=-1, keepdims=True) + EPS)
    normed = centered * inverse
    normed_mine = normalize(tokens, norm_gain, norm_shift)
    full_qkv = lax.all_gather(qkv_weight, "dp", axis=1, tiled=True)
    normed_mine, up_weight, down_weight, dense_weight = lax.optimization_barrier(
        (normed_mine, up_weight, down_weight, dense_weight)
    )
    full_up = lax.all_gather(up_weight, "dp", axis=0, tiled=True)
    full_down = lax.all_gather(down_weight, "dp", axis=1, tiled=True)
    full_dense = lax.all_gather(dense_weight, "dp", axis=1, tiled=True)
    around = [(i, (i + 1) % ways) for i in range(ways)]
    ring = [normed_mine, shift(normed_mine, around)]

    biases = jnp.concatenate([qkv_bias.reshape(-1), up_bias])
    biases = lax.all_gather(biases, "dp", axis=0).astype(jnp.float32)
    third = qkv_bias.shape[1]
    full_qbias = biases[:, : 3 * third].reshape(copies, 3, third)
    full_qbias = full_qbias.transpose(1, 0, 2).reshape(3, -1, PAIR).transpose(1, 0, 2).reshape(-1)
    full_ubias = biases[:, 3 * third :].reshape(-1)

    starts = segment_starts(segments)[0]
    cos_wide, sin_wide = rotary_wide(starts)
    valid_rows = (segments != 0).astype(jnp.float32).reshape(length, 1)
    valid_wide = jnp.broadcast_to(valid_rows, (length, PAIR))
    lows = starts[::BLOCK] // BLOCK
    chunk = jnp.arange(length // BLOCK, dtype=jnp.int32)
    per = row_count // BLOCK
    places = (me - 1 - chunk // per) % ways * per + chunk % per

    tables = (cos_wide, sin_wide, starts, valid_wide, lows, places)
    valid_mine = lax.dynamic_slice_in_dim(valid_rows, me * row_count, row_count, 0)
    cot_columns = jnp.sum(cotangent, axis=0, dtype=jnp.float32)
    resid_square = jnp.sum(valid_mine * resid * resid)
    fixed = lax.optimization_barrier
    ring[1], cot_mine, tables, full_qbias, full_ubias, cot_columns, resid_square = fixed(
        (ring[1], cotangent, tables, full_qbias, full_ubias, cot_columns, resid_square)
    )
    pairs = qkv_weight.shape[2] // PAIR
    sorted_qkv = columns_sorted(full_qkv)
    half = max(1, pairs // 2)
    projected, slopes, hidden_act, mlp_parts = ([None] * ways for _ in range(4))
    grad_context, grad_pre = [None] * ways, [None]

    def turned(blocks):
        return [*blocks[1:], blocks[0]]

    def project(k):
        projected[k] = jnp.dot(ring[k], sorted_qkv, preferred_element_type=jnp.float32)

    def widen(k):
        pre = jnp.dot(ring[k], full_up, preferred_element_type=jnp.float32) + full_ubias
        value, slopes[k] = gelu_and_slope(pre)
        hidden_act[k] = value.astype(low)

    def narrow(k):
        mlp_parts[k] = jnp.dot(
            hidden_act[k], full_down, preferred_element_type=jnp.float32
        ).astype(low)

    def context_back(k, block):
        grad_context[k] = contract_cols(block, full_dense).astype(low)

    def inner_back(k, block):
        grad_pre[0] = hidden_back(
            block, full_down, slopes[k], (k - 1) % ways, ways, held=grad_pre[0]
        )

    for k in range(2, ways):
        coming = shift(ring[k - 1], around)
        if k == 2:
            project(0)
            project(1)
        if k == ways - 1:
            for j in range(ways - 1):
                if projected[j] is None:
                    project(j)
                widen(j)
        coming, ring, projected, slopes, hidden_act, cot_mine = fixed(
            (coming, ring, projected, slopes, hidden_act, cot_mine)
        )
        ring.append(coming)

    cot = LineGather(cot_mine)
    cot.step()
    project(ways - 1)
    widen(ways - 1)
    for k in range(ways):
        narrow(k)
    ring, projected, slopes, hidden_act, mlp_parts = together(
        cot, after=(ring, projected, slopes, hidden_act, mlp_parts)
    )

    mlp = LineScatter(mlp_parts)
    while len(cot.up) < ways - 1:
        cot.step()
        mlp.step()
    attended = attention_forward(turned(projected), full_qbias, tables, 0, pairs)
    ring, attended, slopes, hidden_act, sorted_qkv, cot.up[0] = together(
        cot, mlp, after=(ring, attended, slopes, hidden_act, sorted_qkv, cot.up[0])
    )
    query, keys, values, context_low, logsum = attended

    cot.step()
    mlp.step()
    for k in [0, *range(2, ways - 1)]:
        context_back(k, cot.block(k))
        inner_back(k, cot.block(k))
    acts = jnp.concatenate(turned(hidden_act), axis=0)
    attn_part = [
        jnp.dot(rows, full_dense, preferred_element_type=jnp.float32).astype(low)
        for rows in (context_low[:row_count], context_low[row_count:])
    ]
    normed_low = jnp.concatenate(turned(ring), axis=0)
    grad_context, grad_pre, acts, slopes, attn_part, normed_low = together(
        cot, mlp, after=(grad_context, grad_pre, acts, slopes, attn_part, normed_low)
    )

    while mlp.k < ways:
        mlp.step()
    blocks = [cot.block(k) for k in range(ways)]
    late = sorted({1, ways - 1})
    for k in late:
        context_back(k, blocks[k])
    grad_full = jnp.concatenate(turned(blocks), axis=0)
    grad_down = contract_rows(acts, grad_full).astype(low)
    grad_context, attn_part, grad_full, grad_down, blocks, grad_pre, slopes = together(
        mlp, after=(grad_context, attn_part, grad_full, grad_down, blocks, grad_pre, slopes)
    )
    part_down = scatter_low(grad_down, "dp", 1)

    attn = RingScatter(attn_part, row_count)
    attn.step()
    grads = attention_backward(query, keys, values, turned(grad_context), logsum, tables, 0, half)
    grad_dense = contract_rows(context_low, grad_full).astype(low)
    grads, grad_context, grad_dense, grad_pre, normed_low, blocks, slopes = together(
        attn, mlp, after=(grads, grad_context, grad_dense, grad_pre, normed_low, blocks, slopes)
    )
    part_dense = scatter_low(grad_dense, "dp", 1)

    while attn.k < ways - 2:
        attn.step()
    if pairs > half:
        grads = attention_backward(
            query, keys, values, turned(grad_context), logsum, tables, half, pairs - half, held=grads
        )
    for k in late:
        inner_back(k, blocks[k])
    grads, grad_pre, normed_low, part_down = together(
        attn, mlp, after=(grads, grad_pre, normed_low, part_down)
    )
    grad_proj, grad_qbias = grads[0], grads[1][:, 0, :]
    [pre_full] = grad_pre

    def return_normed(low_block, high_block):
        rows = slice(low_block * row_count, high_block * row_count)
        part = contract_cols(pre_full[rows], full_up) + contract_cols(grad_proj[rows], sorted_qkv)
        return part.astype(low)

    attn.step()
    grad_up = contract_rows(normed_low, pre_full).astype(low)
    grad_parts = [return_normed(0, 1)]
    grad_parts, grad_up, pre_full, grad_proj, normed_low, part_dense = together(
        attn, mlp, after=(grad_parts, grad_up, pre_full, grad_proj, normed_low, part_dense)
    )
    part_up = scatter_low(grad_up, "dp", 0)

    last = RingScatter(grad_parts, row_count)
    last.step()
    grad_qkv = contract_rows(normed_low, grad_proj).astype(low)
    last.parts.append(return_normed(1, 2))
    grad_qkv, pre_full, grad_proj = together(last, attn, mlp, after=(grad_qkv, pre_full, grad_proj))
    part_qkv = scatter_low(grad_qkv, "dp", 0)
    last.parts.append(return_normed(2, ways))
    while last.k < ways - 2:
        last.step()
    grad_ubias = jnp.sum(pre_full, axis=0, dtype=jnp.float32)
    attn_mine, mlp_mine = attn.total(), mlp.total()
    attn_mine, mlp_mine, grad_ubias, part_down, part_dense, part_up = together(
        last, after=(attn_mine, mlp_mine, grad_ubias, part_down, part_dense, part_up)
    )
    part_qkv = columns_back(part_qkv)
    part_down, part_dense = part_down.astype(jnp.float32), part_dense.astype(jnp.float32)
    last.step()
    output = (resid + attn_mine + mlp_mine + out_bias).astype(low)
    attn_square = jnp.sum(valid_mine * attn_mine * attn_mine)
    mlp_square = jnp.sum(valid_mine * mlp_mine * mlp_mine)
    part_up = part_up.astype(jnp.float32)
    output, attn_square, mlp_square, part_up, part_qkv, part_down, part_dense = together(
        last,
        after=(output, attn_square, mlp_square, part_up, part_qkv, part_down, part_dense),
    )
    grad_mine = last.total()
    scaled = grad_mine * norm_gain
    grad_tokens = (
        cotangent.astype(jnp.float32)
        + inverse
        * (
            scaled
            - jnp.mean(scaled, axis=-1, keepdims=True)
            - normed * jnp.mean(scaled * normed, axis=-1, keepdims=True)
        )
    ).astype(low)

    totals = jnp.stack(
        [resid_square, attn_square, mlp_square, jnp.sum(valid_mine) * model_width]
    )
    columns = jnp.stack(
        [
            jnp.sum(grad_mine * normed, axis=0),
            jnp.sum(grad_mine, axis=0),
            cot_columns,
        ]
    )
    peers = copies * ways
    share = model_width // peers
    columns = columns.reshape(3, peers, share).transpose(1, 0, 2).reshape(peers, 3 * share)
    own_bias = jnp.concatenate(
        [
            grad_qbias.reshape(3, copies, third).transpose(1, 0, 2).reshape(copies, 3 * third),
            grad_ubias.reshape(copies, -1),
        ],
        axis=1,
    )
    same = (jnp.arange(ways) == me).astype(jnp.float32)[None, :, None]
    own_bias = (own_bias[:, None, :] * same).reshape(peers, -1)
    small = jnp.concatenate(
        [columns, own_bias, jnp.broadcast_to(totals, (peers, 4))], axis=1
    )
    small = jnp.sum(lax.all_to_all(small, ("dp", "tensor"), 0, 0, tiled=True), axis=0)
    part_gain, part_shift, part_obias = small[: 3 * share].reshape(3, share)
    part_qbias = small[3 * share : 3 * share + 3 * third].reshape(3, third)
    part_ubias = small[3 * share + 3 * third : -4]
    root_squares = jnp.sqrt(small[-4:-1] / small[-1])
    return (
        output,
        grad_tokens,
        part_gain,
        part_shift,
        part_qkv,
        part_qbias,
        part_dense,
        part_up,
        part_ubias,
        part_down,
        part_obias,
        root_squares,
    )


def solution(mesh):
    placed = (
        P(("dp", "tensor"), None),
        P("dp", None),
        P(),
        P(),
        P(None, "dp", "tensor"),
        P(None, ("tensor", "dp")),
        P("tensor", "dp"),
        P("dp", "tensor"),
        P(("tensor", "dp")),
        P("tensor", "dp"),
        P(),
        P(("dp", "tensor"), None),
    )
    return jax.shard_map(
        body,
        mesh=mesh,
        in_specs=placed,
        out_specs=(
            P(("dp", "tensor"), None),
            P(("dp", "tensor"), None),
            P(("dp", "tensor")),
            P(("dp", "tensor")),
            P(None, "dp", "tensor"),
            P(None, ("tensor", "dp")),
            P("tensor", "dp"),
            P("dp", "tensor"),
            P(("tensor", "dp")),
            P("tensor", "dp"),
            P(("dp", "tensor")),
            P(),
        ),
        check_vma=False,
    )
```
